32 devices in a mesh: dp: 4 (over y, core), ctx: 8 (over z, x).
Axes of the slice: x: 2, y: 2, z: 4, core: 2. Of those that a mesh axis runs over, the one named last changes fastest.
Arguments:
- tokens: bfloat16 [4096, 768], P(('dp', 'ctx')), may hold values from -15 to 15
- w_query: bfloat16 [768, 768], P(('dp', 'ctx')), may hold values from -0.21875 to 0.21875
- w_key: bfloat16 [768, 768], P(('dp', 'ctx')), may hold values from -0.21875 to 0.21875
- w_value: bfloat16 [768, 768], P(('dp', 'ctx')), may hold values from -0.21875 to 0.21875
- w_out: bfloat16 [768, 768], P(('dp', 'ctx')), may hold values from -0.4375 to 0.4375
- b_query: bfloat16 [768], P(('dp', 'ctx')), may hold values from -3 to 3
- b_value: bfloat16 [768], P(('dp', 'ctx')), may hold values from -1.1953125 to 1.1953125
- b_out: bfloat16 [768], P(('dp', 'ctx')), may hold values from -3 to 3
- norm1_gain: bfloat16 [768], P(('dp', 'ctx')), may hold values from 0.099609375 to 1.8984375
- norm1_shift: bfloat16 [768], P(('dp', 'ctx')), may hold values from -3 to 3
- w_in: bfloat16 [768, 3072], P(('dp', 'ctx')), may hold values from -0.21875 to 0.21875
- b_in: bfloat16 [3072], P(('dp', 'ctx')), may hold values from -3 to 3
- w_back: bfloat16 [3072, 768], P(('dp', 'ctx')), may hold values from -0.109375 to 0.109375
- b_back: bfloat16 [768], P(('dp', 'ctx')), may hold values from -3 to 3
- norm2_gain: bfloat16 [768], P(('dp', 'ctx')), may hold values from 0.099609375 to 1.8984375
- norm2_shift: bfloat16 [768], P(('dp', 'ctx')), may hold values from -3 to 3
- cotangent: bfloat16 [4096, 768], P(('dp', 'ctx')), may hold values from -6 to 6
Outputs:
- layer_out: bfloat16 [4096, 768], P(('dp', 'ctx'))
- input_grad: float32 [4096, 768], P(('dp', 'ctx'))
- w_query_grad: float32 [768, 768], P(('dp', 'ctx'))
- w_key_grad: float32 [768, 768], P(('dp', 'ctx'))
- w_value_grad: float32 [768, 768], P(('dp', 'ctx'))
- w_out_grad: float32 [768, 768], P(('dp', 'ctx'))
- b_query_grad: float32 [768], P(('dp', 'ctx'))
- b_value_grad: float32 [768], P(('dp', 'ctx'))
- b_out_grad: float32 [768], P(('dp', 'ctx'))
- norm1_gain_grad: float32 [768], P(('dp', 'ctx'))
- norm1_shift_grad: float32 [768], P(('dp', 'ctx'))
- w_in_grad: float32 [768, 3072], P(('dp', 'ctx'))
- b_in_grad: float32 [3072], P(('dp', 'ctx'))
- w_back_grad: float32 [3072, 768], P(('dp', 'ctx'))
- b_back_grad: float32 [768], P(('dp', 'ctx'))
- norm2_gain_grad: float32 [768], P(('dp', 'ctx'))
- norm2_shift_grad: float32 [768], P(('dp', 'ctx'))
- rms_values: float32 [2], replicated
The draws below stay inside these ranges and needn't reach their ends.
All inputs are finite; a program needn't handle non-finite values.
Results may differ from the reference program's by a relative error of at most 0.015.
Values may be sent and summed in bfloat16 or wider, within the bound.
A program may use at most 256 MiB of HBM per device.

```python
import math
import jax
import jax.numpy as jnp
from jax import lax

D = 768
FF = 3072
DH = 64
LENGTH = 1024
SEQS = 4
TOKENS = 4096


def draw_tokens(key, part):
    key_values = jax.random.fold_in(key, 11)
    key_columns = jax.random.fold_in(key, 12)
    base = jnp.clip(jax.random.normal(key_values, (TOKENS, D), jnp.float32), -4.0, 4.0)
    positions = jnp.arange(TOKENS, dtype=jnp.float32)[:, None]
    row_scale = jnp.exp(positions * (0.5 * math.log(3.0) / TOKENS))
    column_scale = jnp.exp(jax.random.uniform(key_columns, (1, D), jnp.float32, -1.1513, 1.1513)) / 1.47
    return (base * row_scale * column_scale).astype(jnp.bfloat16)


def strengthened(values, rng, source, target, shards_of, factor):
    def block_of(position):
        return (jnp.arange(values.shape[position]) // (values.shape[position] // shards_of)).reshape((-1,) + (1,) * (values.ndim - 1 - position))

    one_side = jax.random.permutation(rng, shards_of)[block_of(target)]
    far = (block_of(target) + shards_of // 2) % shards_of
    return jnp.where((block_of(source) == one_side) | (block_of(source) == far), factor * values, values)


def shard_levels(rng, shape, cuts, low, largest):
    level = 1.0
    for position, blocks in cuts:
        draws = jax.random.uniform(jax.random.fold_in(jax.random.fold_in(rng, 6), position), (blocks,), jnp.float32, low / len(cuts), largest / len(cuts))
        level = level * jnp.repeat(jnp.exp(draws), shape[position] // blocks).reshape((-1,) + (1,) * (len(shape) - 1 - position))
    return level


def bell_draw(rng, dims, deviation, reach, shards=(), held_as=jnp.bfloat16):
    level = shard_levels(rng, dims, shards, -0.22, 0.18) if shards else 1.0
    drawn = jax.random.normal(rng, dims, jnp.float32) * deviation * level
    return jnp.minimum(jnp.maximum(drawn, -reach), reach).astype(held_as)


def bell_draw_with(rng, shape, scale, limit, shards, heavy, held_as=jnp.bfloat16):
    values = scale * jax.random.normal(rng, shape, jnp.float32)
    if shards:
        values = values * shard_levels(rng, shape, shards, -0.22, 0.18)
    return jnp.clip(strengthened(values, jax.random.fold_in(rng, 3), *heavy), -limit, limit).astype(held_as)


def setup_inputs(seed: int = 0) -> dict:
    splits = jax.random.split(jax.random.key(seed), 18)
    return {
        "tokens": draw_tokens(jax.random.fold_in(splits[17], 71), 0),
        "w_query": bell_draw(splits[1], (D, D), D ** -0.5, 0.21875, ((0, 32),)),
        "w_key": bell_draw(splits[2], (D, D), D ** -0.5, 0.21875, ((0, 32),)),
        "w_value": bell_draw(splits[3], (D, D), D ** -0.5, 0.21875, ((0, 32),)),
        "w_out": bell_draw(splits[4], (D, D), (max(D * 256 // LENGTH, 1)) ** -0.5, 0.4375, ((0, 32),)),
        "b_query": bell_draw(splits[5], (D,), 0.5, 3.0, ((0, 32),)),
        "b_value": bell_draw(splits[6], (D,), 0.2, 1.1953125, ((0, 32),)),
        "b_out": bell_draw(splits[7], (D,), 0.5, 3.0, ((0, 32),)),
        "norm1_gain": jnp.clip(1.0 + 0.18 * jax.random.normal(splits[8], (D,), jnp.float32), 0.099609375, 1.8984375).astype(jnp.bfloat16),
        "norm1_shift": bell_draw(splits[9], (D,), 0.5, 3.0, ((0, 32),)),
        "w_in": bell_draw(splits[10], (D, FF), D ** -0.5, 0.21875, ((0, 32),)),
        "b_in": bell_draw(splits[11], (FF,), 0.5, 3.0, ((0, 32),)),
        "w_back": bell_draw(splits[12], (FF, D), FF ** -0.5, 0.109375, ((0, 32),)),
        "b_back": bell_draw(splits[13], (D,), 0.5, 3.0, ((0, 32),)),
        "norm2_gain": jnp.clip(1.0 + 0.18 * jax.random.normal(splits[14], (D,), jnp.float32), 0.099609375, 1.8984375).astype(jnp.bfloat16),
        "norm2_shift": bell_draw(splits[15], (D,), 0.5, 3.0, ((0, 32),)),
        "cotangent": bell_draw_with(splits[16], (TOKENS, D), 1.0, 6.0, ((0, 32),), (0, 1, 32, 2.75)),
    }


@jax.custom_vjp
def low(v):
    return lax.optimization_barrier(v.astype(jnp.bfloat16)).astype(jnp.float32)

@jax.custom_vjp
def low_back(v):
    return v

def low_keep(v):
    return (low(v), None)

def low_pass(kept, grad):
    return (grad,)

def back_keep(v):
    return (v, None)

def back_low(kept, grad):
    return (low(grad),)
low.defvjp(low_keep, low_pass)
low_back.defvjp(back_keep, back_low)
epsilon = 1e-12
highest = lax.Precision.HIGHEST

def product(left, right):
    return jnp.dot(left, right, precision=highest, preferred_element_type=jnp.float32)

def rounded(value):
    return low(low_back(value))

def layer_norm(values, gain, shift):
    average = lax.optimization_barrier(jnp.mean(values, axis=-1, keepdims=True))
    centered = values - average
    spread = lax.optimization_barrier(jnp.mean(centered * centered, axis=-1, keepdims=True))
    return centered * lax.rsqrt(spread + epsilon) * gain + shift

def attention(query_rows, key_rows, value_rows):
    length = query_rows.shape[0]
    head_count = query_rows.shape[1] // DH
    block_rows = min(512, length)
    query_blocks = query_rows.reshape(length // block_rows, block_rows, head_count, DH)
    key_heads = key_rows.reshape(length, head_count, DH)
    value_heads = value_rows.reshape(length, head_count, DH)

    def one_block(query_block):
        scores = low_back(jnp.einsum('qhd,khd->hqk', query_block, key_heads, precision=highest) * 0.125)
        weights = jnp.exp(scores)
        totals = lax.optimization_barrier(jnp.sum(weights, axis=-1))
        summed = low_back(jnp.einsum('hqk,khd->qhd', low(weights), value_heads, precision=highest))
        return summed / jnp.transpose(totals)[:, :, None]
    mixed = lax.map(jax.checkpoint(one_block), query_blocks)
    return mixed.reshape(length, head_count * DH)

def forward(residual, w_query, w_key, w_value, w_out, b_query, b_value, b_out, norm1_gain, norm1_shift, w_in, b_in, w_back, b_back, norm2_gain, norm2_shift):
    query_rows = rounded(product(residual, w_query) + b_query)
    key_rows = rounded(product(residual, w_key))
    value_rows = rounded(product(residual, w_value) + b_value)
    mixed = attention(query_rows, key_rows, value_rows)
    branch_attn = low_back(product(low(mixed), w_out) + b_out)
    stream_one = residual + branch_attn
    hidden = layer_norm(stream_one, norm1_gain, norm1_shift)
    pre_act = low_back(product(low(hidden), w_in) + b_in)
    activated = jax.nn.gelu(pre_act, approximate=False)
    branch_ffn = low_back(product(low(activated), w_back) + b_back)
    result = layer_norm(hidden + branch_ffn, norm2_gain, norm2_shift)
    return (result, stream_one)

def reference(tokens, w_query, w_key, w_value, w_out, b_query, b_value, b_out, norm1_gain, norm1_shift, w_in, b_in, w_back, b_back, norm2_gain, norm2_shift, cotangent):
    params = tuple((member.astype(jnp.float32) for member in (w_query, w_key, w_value, w_out, b_query, b_value, b_out, norm1_gain, norm1_shift, w_in, b_in, w_back, b_back, norm2_gain, norm2_shift)))
    inputs = tokens.astype(jnp.float32).reshape(SEQS, LENGTH, D)
    upstream = cotangent.astype(jnp.float32).reshape(SEQS, LENGTH, D)

    def one_sequence(running, sequence_pair):
        grad_sums, squares = running
        residual, incoming = sequence_pair
        result, pullback, stream_one = jax.vjp(forward, residual, *params, has_aux=True)
        fresh = pullback(incoming)
        grad_sums = tuple((older + newer for older, newer in zip(grad_sums, fresh[1:])))
        squares = squares + jnp.stack([jnp.sum(residual * residual), jnp.sum(stream_one * stream_one)])
        return ((grad_sums, squares), (result.astype(jnp.bfloat16), fresh[0]))
    initial = (tuple((jnp.zeros(member.shape, jnp.float32) for member in params)), jnp.zeros((2,), jnp.float32))
    (grad_sums, squares), (outputs, input_grads) = lax.scan(one_sequence, initial, (inputs, upstream))
    rms_values = jnp.sqrt(squares / (TOKENS * D))
    return (outputs.reshape(TOKENS, D), input_grads.reshape(TOKENS, D), grad_sums[0], grad_sums[1], grad_sums[2], grad_sums[3], grad_sums[4], grad_sums[5], grad_sums[6], grad_sums[7], grad_sums[8], grad_sums[9], grad_sums[10], grad_sums[11], grad_sums[12], grad_sums[13], grad_sums[14], rms_values)
```

```python
from functools import partial

import jax
import jax.numpy as jnp
from jax import lax
from jax.experimental import pallas as pl
from jax.experimental.pallas import tpu as pltpu
from jax.sharding import PartitionSpec as P

MESH = pl.DeviceIdType.MESH
f32 = jnp.float32
bf16 = jnp.bfloat16
DH = 64
epsilon = 1e-12


def dot(a, b, ca=1, cb=0):
    return lax.dot_general(a, b, (((ca,), (cb,)), ((), ())), preferred_element_type=f32)


def norm_parts(values):
    average = jnp.mean(values, axis=-1, keepdims=True)
    centered = values - average
    spread = jnp.mean(centered * centered, axis=-1, keepdims=True)
    inverse = lax.rsqrt(spread + epsilon)
    return centered * inverse, inverse


def norm_back(incoming, scaled, inverse, gain):
    along = incoming * gain
    return inverse * (
        along
        - jnp.mean(along, axis=-1, keepdims=True)
        - scaled * jnp.mean(along * scaled, axis=-1, keepdims=True)
    )


def layer_kernel(
    tok, cot, wq, wk, wv, wo, wi, wb, vec,
    lo_out, ig_out, dq_out, dk_out, dv_out, do_out, di_out, db_out, sm_out,
    xr, cr, xg, pa, sa, si, sb, so, wa_f, wi_f, wb_f, wo8, wo_f,
    sm0, smr, sm1, smz, sm2, sms, vf,
    qs, kv, ee, mt, tot, mx, po, ro, hid, xh1, iv1, hg, gp, act, ds2, dg, dp, tg, dmt, dqt,
    dkv, kvr, dall, ds1,
    ga, ga_b, ra, s_a, za, fa, la,
    gi, gi_b, ri, s_i, zi, fi,
    gb, gb_b, rb, s_b, zb, fb,
    go, go_b, r_o, s_o, z_o, fo,
    igs, igr, gs0, gsr, gs1, gsz, gs2, gss,
    ssem, rsem,
):
    d = lax.axis_index("dp")
    k = lax.axis_index("ctx")
    y, c = d // 2, d % 2
    z, x = k // 2, k % 2
    q = 2 * y + x
    r = 8 * d + k

    def dev(xx, yy, cc, zz):
        return (2 * yy + cc, 2 * zz + xx)

    def mate_q(m):
        a, b = m % 2, m // 2
        return 2 * ((y + b) % 2) + (x + a) % 2

    def mate(m):
        a, b = m % 2, m // 2
        return dev((x + a) % 2, (y + b) % 2, c, z)

    def plane(dz):
        return dev(x, y, c, (z + dz) % 4)

    sibling = dev(x, y, 1 - c, z)
    pd, pz = 2 * (z % 2) + z // 2, 2 * c + y
    partner = (pd, 2 * pz + x)
    alone = (pd == d) & (pz == z)
    cross = dev(c, y, x, z)
    stays = x == c

    bar = pltpu.get_barrier_semaphore()
    near = [mate(1), mate(2), mate(3), sibling, plane(1), plane(2), plane(3)]
    for other in near:
        pl.semaphore_signal(bar, inc=1, device_id=other, device_id_type=MESH)

    @pl.when(jnp.logical_not(alone))
    def _():
        pl.semaphore_signal(bar, inc=1, device_id=partner, device_id_type=MESH)

    @pl.when(jnp.logical_not(stays))
    def _():
        pl.semaphore_signal(bar, inc=1, device_id=cross, device_id_type=MESH)

    pl.semaphore_wait(bar, len(near) + 2 - alone.astype(jnp.int32) - stays.astype(jnp.int32))

    sends = []

    def send(src, dst, to, own=None):
        i = len(sends)
        cp = pltpu.make_async_remote_copy(
            src_ref=src, dst_ref=dst, send_sem=ssem.at[i], recv_sem=rsem.at[i],
            device_id=to, device_id_type=MESH,
        )
        if own is None:
            cp.start()
        else:
            @pl.when(jnp.logical_not(own))
            def _():
                cp.start()

            @pl.when(own)
            def _():
                dst[...] = src[...]
        sends.append((cp, own))
        return cp

    def arrived(cp, own=None):
        if own is None:
            cp.wait_recv()
        else:
            @pl.when(jnp.logical_not(own))
            def _():
                cp.wait_recv()

    def gather(ref):
        return [send(ref.at[q], ref.at[q], mate(m)) for m in (1, 2, 3)]

    def scatter(src, first, dst):
        return [send(src.at[first + mate_q(m)], dst.at[m - 1], mate(m)) for m in (1, 2, 3)]

    def all_in(copies):
        for cp in copies:
            cp.wait_recv()

    c_tok = send(tok, xr, partner, alone)
    for j in range(4):
        cols = slice(192 * j, 192 * j + 192)
        pa[j] = jnp.concatenate([wq[:, cols], wk[:, cols], wv[:, cols]], axis=1)
    sa[q] = pa[q]
    c_sa = [send(pa.at[mate_q(m)], sa.at[q], mate(m)) for m in (1, 2, 3)]
    vec32 = vec[...].astype(f32)
    row = lax.broadcasted_iota(jnp.int32, (16, 768), 0)
    lane = lax.broadcasted_iota(jnp.int32, (16, 768), 1)
    placed = jnp.where(row < 8, pltpu.roll(vec32, 24 * r, 1), 0.0)
    b_in_row = pltpu.roll(vec32, 96 * (r % 8), 1)[8:9]
    placed = placed + jnp.where(row == 8 + r // 8, b_in_row, 0.0)
    sm0[...] = placed.astype(bf16)
    c_sm = [send(sm0, smr.at[m - 1], mate(m)) for m in (1, 2, 3)]

    def in_cols(j):
        return wi.at[:, pl.ds(pl.multiple_of(768 * j, 768), 768)]

    si[q] = wi[:, pl.ds(pl.multiple_of(768 * q, 768), 768)]
    c_si = [send(in_cols(mate_q(m)), si.at[q], mate(m)) for m in (1, 2, 3)]
    c_so = send(wo, so, cross, stays)
    c_sb = send(wb, sb, cross, stays)

    def own_rows(b, zz=None):
        zz = z if zz is None else zz
        return pl.ds(pl.multiple_of(384 * b + 192 * c + 48 * zz, 16), 48)

    def core_rows(b, cc):
        return pl.ds(pl.multiple_of(384 * b + 192 * cc, 16), 192)

    def bundle(landed, full):
        for b in range(2):
            full[own_rows(b), :] = jnp.concatenate([landed[2 * b], landed[2 * b + 1]], axis=0)
        return [
            send(full.at[own_rows(b), :], full.at[own_rows(b), :], plane(dz))
            for dz in (1, 2, 3)
            for b in range(2)
        ]

    all_in(c_sa)
    c_za = bundle(sa, wa_f)

    all_in(c_sm)
    total = sm0[...].astype(f32) + smr[0].astype(f32) + smr[1].astype(f32) + smr[2].astype(f32)
    sm1[...] = total.astype(bf16)
    c_smz = [send(sm1, smz.at[dz - 1], plane(dz)) for dz in (1, 2, 3)]

    arrived(c_tok, alone)
    xg[q] = xr[...]
    c_xg = gather(xg)

    all_in(c_smz)
    total = sm1[...].astype(f32) + smz[0].astype(f32) + smz[1].astype(f32) + smz[2].astype(f32)
    sm2[...] = total.astype(bf16)
    c_sms = send(sm2, sms, sibling)

    all_in(c_za)
    c_ca = [
        send(wa_f.at[core_rows(b, c), :], wa_f.at[core_rows(b, c), :], sibling) for b in range(2)
    ]

    arrived(c_so, stays)
    slot_o = 2 * z + c
    wo8[slot_o] = so[...]
    c_zo = [send(wo8.at[slot_o], wo8.at[slot_o], plane(dz)) for dz in (1, 2, 3)]
    all_in(c_si)
    c_zi = bundle(si, wi_f)
    arrived(c_sb, stays)

    def b_rows(zz, cc):
        return pl.ds(pl.multiple_of(96 * (2 * zz + cc), 96), 96)

    wb_f[b_rows(z, c), :] = sb[...]
    c_zb = [send(wb_f.at[b_rows(z, c), :], wb_f.at[b_rows(z, c), :], plane(dz)) for dz in (1, 2, 3)]
    c_cot = send(cot, cr, partner, alone)

    arrived(c_sms)
    vf[...] = sm2[...].astype(f32) + sms[...].astype(f32)
    b_out, gain1, shift1 = vf[2:3], vf[3:4], vf[4:5]
    b_back, gain2, shift2 = vf[5:6], vf[6:7], vf[7:8]
    turned = pltpu.roll(vf[...], lax.rem(768 - 192 * q, 768), 1)
    b_qkv = jnp.concatenate(
        [turned[0:1, :192], jnp.zeros((1, 192), f32), turned[1:2, :192]], axis=1
    )
    row1 = lax.broadcasted_iota(jnp.int32, (16, 768), 0)
    b_in = jnp.sum(jnp.where(row1 == 8 + q, vf[...], 0.0), axis=0, keepdims=True)

    all_in(c_ca)
    c_kv = []
    for m in range(4):
        j = mate_q(m)
        if m:
            c_xg[m - 1].wait_recv()
        out = dot(xg[j], wa_f[...]) + b_qkv
        rows = pl.ds(pl.multiple_of(128 * j, 128), 128)
        qs[rows, :] = (out[:, :192].astype(bf16).astype(f32) * 0.125).astype(bf16)
        kv[c, rows, :] = out[:, 192:].astype(bf16)
        c_kv.append(send(kv.at[c, rows, :], kv.at[c, rows, :], sibling))

    mt[...] = jnp.zeros_like(mt)
    tot[...] = jnp.zeros_like(tot)

    def expo_rows(h, half, part):
        return slice(1024 * h + 512 * half + 256 * part, 1024 * h + 512 * half + 256 * part + 256)

    def forward_chunk(half, slot, part):
        rows = slice(256 * part, 256 * part + 256)
        keys_values = kv[half, rows, :]
        for h in range(3):
            key = keys_values[:, 64 * h:64 * h + 64]
            value = keys_values[:, 192 + 64 * h:256 + 64 * h]
            query = qs[:, 64 * h:64 * h + 64]
            expo = jnp.exp(dot(key, query, 1, 1))
            low = expo.astype(bf16)
            ee[expo_rows(h, slot, part), :] = low
            tot[h:h + 1, :] += jnp.sum(expo, axis=0, keepdims=True)
            mt[64 * h:64 * h + 64, :] += dot(value, low, 0, 0)

    forward_chunk(c, 0, 0)
    forward_chunk(c, 0, 1)
    all_in(c_kv)
    forward_chunk(1 - c, 1, 0)
    forward_chunk(1 - c, 1, 1)
    for h in range(3):
        part = slice(64 * h, 64 * h + 64)
        mt[part, :] = mt[part, :] / tot[h:h + 1, :]
    mx[...] = jnp.transpose(mt[...]).astype(bf16)

    all_in(c_zo)
    c_co = [send(wo8.at[2 * zz + c], wo8.at[2 * zz + c], sibling) for zz in range(4)]
    all_in(c_co)
    for j in range(8):
        wo_f[24 * j:24 * j + 24, :] = wo8[j]

    def project(m, _):
        j = mate_q(m)
        rows = pl.ds(pl.multiple_of(128 * j, 128), 128)
        po[j] = dot(mx[rows, :], wo_f[...]).astype(bf16)
        return 0

    lax.fori_loop(1, 4, project, 0)
    c_ro = scatter(po, 0, ro.at[0])
    own = pl.ds(pl.multiple_of(128 * q, 128), 128)
    attn = dot(mx[own, :], wo_f[...]) + b_out
    all_in(c_ro)
    attn = attn + ro[0, 0].astype(f32) + ro[0, 1].astype(f32) + ro[0, 2].astype(f32)
    x32 = xr[...].astype(f32)
    stream = x32 + attn
    squares_x = jnp.sum(x32 * x32)
    squares_s = jnp.sum(stream * stream)
    scaled, inverse = norm_parts(stream)
    xh1[...] = scaled
    iv1[...] = jnp.broadcast_to(inverse, iv1.shape)
    hidden = scaled * gain1 + shift1
    hid[...] = hidden
    hg[q] = hidden.astype(bf16)
    c_hg = gather(hg)

    all_in(c_zi)
    c_ci = [
        send(wi_f.at[core_rows(b, c), :], wi_f.at[core_rows(b, c), :], sibling) for b in range(2)
    ]
    all_in(c_zb)
    c_cb = [send(wb_f.at[b_rows(zz, c), :], wb_f.at[b_rows(zz, c), :], sibling) for zz in range(4)]
    all_in(c_ci)
    all_in(c_cb)

    def ffn(j):
        pre = dot(hg[j], wi_f[...]) + b_in
        phi = 0.5 + 0.5 * lax.erf(pre * 0.7071067811865476)
        gp[j] = phi + pre * jnp.exp(-0.5 * pre * pre) * 0.3989422804014327
        act[j] = (pre * phi).astype(bf16)
        return dot(act[j], wb_f[...])

    own_part = ffn(q)
    c_ffn = []
    for m in (1, 2, 3):
        c_hg[m - 1].wait_recv()
        j = mate_q(m)
        po[4 + j] = ffn(j).astype(bf16)
        c_ffn.append(send(po.at[4 + j], ro.at[1, m - 1], mate(m)))
    all_in(c_ffn)
    out = own_part + b_back + ro[1, 0].astype(f32) + ro[1, 1].astype(f32) + ro[1, 2].astype(f32)
    scaled2, inverse2 = norm_parts(hid[...] + out)
    igs[0] = (scaled2 * gain2 + shift2).astype(bf16)
    arrived(c_cot, alone)
    dy = cr[...].astype(f32)
    gain2_grad = jnp.sum(dy * scaled2, axis=0, keepdims=True)
    shift2_grad = jnp.sum(dy, axis=0, keepdims=True)
    dsum2 = norm_back(dy, scaled2, inverse2, gain2)
    ds2[...] = dsum2
    low = dsum2.astype(bf16)
    dg[q] = low
    back_grad = jnp.sum(low.astype(f32), axis=0, keepdims=True)
    c_dg = gather(dg)
    c_lo = send(igs.at[0], lo_out, partner, alone)

    def ffn_back(j):
        dact = dot(dg[j], wb_f[...], 1, 1)
        dp[j] = (dact * gp[j]).astype(bf16)
        return dot(dp[j], wi_f[...], 1, 1)

    own_part = ffn_back(q)
    c_dh = []
    for m in (1, 2, 3):
        c_dg[m - 1].wait_recv()
        j = mate_q(m)
        po[8 + j] = ffn_back(j).astype(bf16)
        c_dh.append(send(po.at[8 + j], ro.at[2, m - 1], mate(m)))

    def weight_grad(left, right, out, low, rows):
        for i in range(rows // 256):
            cols = slice(256 * i, 256 * i + 256)
            part = dot(left[:, cols], right, 0, 0)
            out[cols, :] = part
            low[cols, :] = part.astype(bf16)

    def flat(ref):
        return ref[...].reshape(512, ref.shape[-1])

    weight_grad(flat(act), flat(dg), gb, gb_b, 768)
    c_rb = [send(gb_b.at[b_rows(zz, 1 - c), :], rb.at[zz], sibling) for zz in range(4)]
    weight_grad(flat(hg), flat(dp), gi, gi_b, 768)
    c_ri = [send(gi_b.at[core_rows(b, 1 - c), :], ri.at[b], sibling) for b in range(2)]
    in_grad = jnp.sum(flat(dp).astype(f32), axis=0, keepdims=True)

    all_in(c_dh)
    dhidden = (
        ds2[...] + own_part + ro[2, 0].astype(f32) + ro[2, 1].astype(f32) + ro[2, 2].astype(f32)
    )
    gain1_grad = jnp.sum(dhidden * xh1[...], axis=0, keepdims=True)
    shift1_grad = jnp.sum(dhidden, axis=0, keepdims=True)
    dsum1 = norm_back(dhidden, xh1[...], iv1[:, :1], gain1)
    ds1[...] = dsum1
    low = dsum1.astype(bf16)
    tg[q] = low
    out_grad = jnp.sum(low.astype(f32), axis=0, keepdims=True)
    c_tg = gather(tg)

    def row_sums(c_in, partial_sum, recv, low, landing):
        all_in(c_in)
        copies = []
        for zz in range(4):
            rows = b_rows(zz, c)
            low[zz] = (partial_sum[rows, :] + recv[zz].astype(f32)).astype(bf16)
        for dz in (1, 2, 3):
            copies.append(send(low.at[(z + dz) % 4], landing.at[dz - 1], plane(dz)))
        return copies

    def col_sums(c_in, partial_sum, recv, low, landing):
        all_in(c_in)
        for zz in range(4):
            for b in range(2):
                mine = partial_sum[own_rows(b, zz), :]
                theirs = recv[b, 48 * zz:48 * zz + 48, :].astype(f32)
                low[zz, b] = (mine + theirs).astype(bf16)
        return [send(low.at[(z + dz) % 4], landing.at[dz - 1], plane(dz)) for dz in (1, 2, 3)]

    c_zgb = row_sums(c_rb, gb, rb, s_b, zb)
    c_zgi = col_sums(c_ri, gi, ri, s_i, zi)

    def mixed_back(j):
        cols = pl.ds(pl.multiple_of(128 * j, 128), 128)
        dmt[:, cols] = dot(wo_f[...], tg[j], 1, 1)

    mixed_back(q)
    for m in (1, 2, 3):
        c_tg[m - 1].wait_recv()
        mixed_back(mate_q(m))
    part = dot(mt[...].astype(bf16), flat(tg))
    for j in range(8):
        go[j] = part[24 * j:24 * j + 24]
        go_b[j] = part[24 * j:24 * j + 24].astype(bf16)
    c_rgo = [send(go_b.at[2 * zz + 1 - c], r_o.at[zz], sibling) for zz in range(4)]

    dqt[...] = jnp.zeros_like(dqt)

    def backward_chunk(half, slot, part):
        rows = slice(256 * part, 256 * part + 256)
        keys_values = kv[half, rows, :]
        dkeys, dvalues = [], []
        for h in range(3):
            span = slice(64 * h, 64 * h + 64)
            key = keys_values[:, span]
            value = keys_values[:, 192 + 64 * h:256 + 64 * h]
            query = qs[:, span]
            over = 1.0 / tot[h:h + 1, :]
            dmixed = dmt[span, :]
            dsummed = (dmixed * over).astype(bf16)
            delta = jnp.sum(dmixed * mt[span, :], axis=0, keepdims=True) * over
            expo = ee[expo_rows(h, slot, part), :]
            across = dot(value, dsummed)
            slopes = (expo.astype(f32) * (across - delta)).astype(bf16)
            dvalues.append(dot(expo, dsummed, 1, 1))
            dkeys.append(dot(slopes, query))
            dqt[span, :] += dot(key, slopes, 0, 0)
        dkv[half, rows, :] = jnp.concatenate(dkeys + dvalues, axis=1)

    backward_chunk(1 - c, 1, 0)
    backward_chunk(1 - c, 1, 1)
    c_dkv = send(dkv.at[1 - c], kvr, sibling)
    backward_chunk(c, 0, 0)
    backward_chunk(c, 0, 1)
    dall[:, :192] = jnp.transpose(dqt[...] * 0.125).astype(bf16)
    arrived(c_dkv)
    dall[:, 192:] = (dkv[c] + kvr[...]).astype(bf16)

    def input_back(m, _):
        j = mate_q(m)
        rows = pl.ds(pl.multiple_of(128 * j, 128), 128)
        po[12 + j] = dot(dall[rows, :], wa_f[...], 1, 1).astype(bf16)
        return 0

    lax.fori_loop(1, 4, input_back, 0)
    c_dx = scatter(po, 12, ro.at[3])
    own_part = dot(dall[own, :], wa_f[...], 1, 1)

    weight_grad(flat(xg), dall[...], ga, ga_b, 768)
    c_rga = [send(ga_b.at[core_rows(b, 1 - c), :], ra.at[b], sibling) for b in range(2)]
    sums = jnp.sum(dall[...].astype(f32), axis=0, keepdims=True)

    rest = jnp.zeros((1, 576), f32)
    head_rows = jnp.concatenate(
        [jnp.concatenate([sums[:, :192], rest], axis=1),
         jnp.concatenate([sums[:, 384:], rest], axis=1),
         jnp.zeros((6, 768), f32)], axis=0,
    )
    gs0[...] = jnp.zeros_like(gs0)
    gs0[0:8, :] = pltpu.roll(head_rows, 192 * q, 1)
    gs0[2:3, :] = out_grad
    gs0[3:4, :] = gain1_grad
    gs0[4:5, :] = shift1_grad
    gs0[5:6, :] = back_grad
    gs0[6:7, :] = gain2_grad
    gs0[7:8, :] = shift2_grad
    row2 = lax.broadcasted_iota(jnp.int32, (8, 768), 0)
    gs0[8:16, :] = (
        jnp.where(row2 == q, in_grad, 0.0)
        + jnp.where(row2 == 4, squares_x, 0.0)
        + jnp.where(row2 == 5, squares_s, 0.0)
    )
    c_gs = [send(gs0, gsr.at[m - 1], mate(m)) for m in (1, 2, 3)]

    all_in(c_rgo)
    for zz in range(4):
        s_o[zz] = (go[2 * zz + c] + r_o[zz].astype(f32)).astype(bf16)
    c_zgo = [send(s_o.at[(z + dz) % 4], z_o.at[dz - 1], plane(dz)) for dz in (1, 2, 3)]
    c_zga = col_sums(c_rga, ga, ra, s_a, za)

    all_in(c_dx)
    input_grad = (
        ds1[...] + own_part + ro[3, 0].astype(f32) + ro[3, 1].astype(f32) + ro[3, 2].astype(f32)
    )
    igs[1] = input_grad.astype(bf16)
    c_ig = send(igs.at[1], igr, partner, alone)

    all_in(c_gs)
    gs1[...] = gs0[...] + gsr[0] + gsr[1] + gsr[2]
    c_gsz = [send(gs1, gsz.at[dz - 1], plane(dz)) for dz in (1, 2, 3)]

    all_in(c_zgb)
    fb[...] = (
        s_b[z].astype(f32) + zb[0].astype(f32) + zb[1].astype(f32) + zb[2].astype(f32)
    )
    c_fb = send(fb, db_out, cross, stays)

    def col_final(c_in, low, landing, out):
        all_in(c_in)
        for b in range(2):
            whole = (
                low[z, b].astype(f32) + landing[0, b].astype(f32)
                + landing[1, b].astype(f32) + landing[2, b].astype(f32)
            )
            out[2 * b] = whole[:24]
            out[2 * b + 1] = whole[24:]

    col_final(c_zgi, s_i, zi, fi)

    def out_cols(j):
        return di_out.at[:, pl.ds(pl.multiple_of(768 * j, 768), 768)]

    c_fi = [send(fi.at[mate_q(m)], out_cols(q), mate(m)) for m in (1, 2, 3)]
    di_out[:, pl.ds(pl.multiple_of(768 * q, 768), 768)] = fi[q]

    all_in(c_zgo)
    fo[...] = (
        s_o[z].astype(f32) + z_o[0].astype(f32) + z_o[1].astype(f32) + z_o[2].astype(f32)
    )
    c_fo = send(fo, do_out, cross, stays)

    all_in(c_gsz)
    gs2[...] = gs1[...] + gsz[0] + gsz[1] + gsz[2]
    c_gss = send(gs2, gss, sibling)

    col_final(c_zga, s_a, za, fa)
    la[q] = fa[q]
    c_fa = [send(fa.at[mate_q(m)], la.at[q], mate(m)) for m in (1, 2, 3)]

    arrived(c_ig, alone)
    ig_out[...] = igr[...].astype(f32)

    arrived(c_gss)
    whole = gs2[...] + gss[...]
    sm_out[0:8, :] = pltpu.roll(whole, lax.rem(768 - 24 * r, 768), 1)[:8, :128]
    mine = jnp.sum(
        jnp.where(lax.broadcasted_iota(jnp.int32, (16, 768), 0) == 8 + r // 8, whole, 0.0),
        axis=0, keepdims=True,
    )
    mine = pltpu.roll(jnp.broadcast_to(mine, (8, 768)), lax.rem(768 - 96 * (r % 8), 768), 1)
    row3 = lax.broadcasted_iota(jnp.int32, (8, 128), 0)
    sm_out[8:16, :] = jnp.where(row3 < 4, mine[:, :128], whole[8:16, :128])

    all_in(c_fa)
    for j in range(4):
        cols = slice(192 * j, 192 * j + 192)
        dq_out[:, cols] = la[j, :, :192]
        dk_out[:, cols] = la[j, :, 192:384]
        dv_out[:, cols] = la[j, :, 384:]

    arrived(c_lo, alone)
    arrived(c_fb, stays)
    arrived(c_fo, stays)
    all_in(c_fi)
    for cp, own_copy in sends:
        if own_copy is None:
            cp.wait_send()
        else:
            @pl.when(jnp.logical_not(own_copy))
            def _():
                cp.wait_send()


COPIES = 200


def fused(
    tokens, w_query, w_key, w_value, w_out, b_query, b_value, b_out, norm1_gain, norm1_shift,
    w_in, b_in, w_back, b_back, norm2_gain, norm2_shift, cotangent,
):
    vectors = jnp.stack(
        [b_query, b_value, b_out, norm1_gain, norm1_shift, b_back, norm2_gain, norm2_shift]
    )
    vec = jnp.concatenate(
        [
            jnp.pad(vectors, ((0, 0), (0, 768 - 24))),
            jnp.pad(b_in[None, :], ((0, 7), (0, 768 - 96))),
        ],
        axis=0,
    )
    vm = pl.BlockSpec(memory_space=pltpu.VMEM)

    def v(*shape, t=bf16):
        return pltpu.VMEM(shape, t)

    outs = (
        jax.ShapeDtypeStruct((128, 768), bf16),
        jax.ShapeDtypeStruct((128, 768), f32),
        jax.ShapeDtypeStruct((24, 768), f32),
        jax.ShapeDtypeStruct((24, 768), f32),
        jax.ShapeDtypeStruct((24, 768), f32),
        jax.ShapeDtypeStruct((24, 768), f32),
        jax.ShapeDtypeStruct((24, 3072), f32),
        jax.ShapeDtypeStruct((96, 768), f32),
        jax.ShapeDtypeStruct((16, 128), f32),
    )
    scratch = [
        v(128, 768), v(128, 768), v(4, 128, 768), v(4, 24, 576), v(4, 24, 576), v(4, 24, 768),
        v(96, 768), v(24, 768), v(768, 576), v(768, 768), v(768, 768), v(8, 24, 768), v(192, 768),
        v(16, 768), v(3, 16, 768), v(16, 768), v(3, 16, 768), v(16, 768), v(16, 768),
        v(16, 768, t=f32),
        v(512, 192), v(2, 512, 384), v(3072, 512), v(192, 512, t=f32), v(8, 512, t=f32),
        v(512, 192), v(16, 128, 768), v(4, 3, 128, 768),
        v(128, 768, t=f32), v(128, 768, t=f32), v(128, 128, t=f32), v(4, 128, 768),
        v(4, 128, 768, t=f32), v(4, 128, 768), v(128, 768, t=f32), v(4, 128, 768),
        v(4, 128, 768), v(4, 128, 768), v(192, 512, t=f32), v(192, 512, t=f32),
        v(2, 512, 384, t=f32), v(512, 384, t=f32), v(512, 576), v(128, 768, t=f32),
        v(768, 576, t=f32), v(768, 576), v(2, 192, 576), v(4, 2, 48, 576), v(3, 2, 48, 576),
        v(4, 24, 576, t=f32), v(4, 24, 576, t=f32),
        v(768, 768, t=f32), v(768, 768), v(2, 192, 768), v(4, 2, 48, 768), v(3, 2, 48, 768),
        v(4, 24, 768, t=f32),
        v(768, 768, t=f32), v(768, 768), v(4, 96, 768), v(4, 96, 768), v(3, 96, 768),
        v(96, 768, t=f32),
        v(8, 24, 768, t=f32), v(8, 24, 768), v(4, 24, 768), v(4, 24, 768), v(3, 24, 768),
        v(24, 768, t=f32),
        v(2, 128, 768), v(128, 768), v(16, 768, t=f32), v(3, 16, 768, t=f32),
        v(16, 768, t=f32), v(3, 16, 768, t=f32), v(16, 768, t=f32), v(16, 768, t=f32),
        pltpu.SemaphoreType.DMA((COPIES,)), pltpu.SemaphoreType.DMA((COPIES,)),
    ]
    lo, ig, dq, dk, dv, do, di, db, sm = pl.pallas_call(
        layer_kernel,
        out_shape=outs,
        in_specs=[vm] * 9,
        out_specs=[vm] * 9,
        scratch_shapes=scratch,
        compiler_params=pltpu.CompilerParams(
            collective_id=0, has_side_effects=True, vmem_limit_bytes=60 << 20
        ),
        name="layer",
    )(tokens, cotangent, w_query, w_key, w_value, w_out, w_in, w_back, vec)
    small = [sm[i, :24] for i in range(8)]
    rms = jnp.sqrt(jnp.stack([sm[12, 0], sm[13, 0]]) / (4096 * 768))
    return (
        lo, ig, dq, dk, dv, do, small[0], small[1], small[2], small[3], small[4], di, sm[8, :96],
        db, small[5], small[6], small[7], rms,
    )


def normalize(values, gain, shift):
    average = jnp.mean(values, axis=-1, keepdims=True)
    centered = values - average
    spread = jnp.mean(centered * centered, axis=-1, keepdims=True)
    inverse = lax.rsqrt(spread + epsilon)
    scaled = centered * inverse
    return (scaled * gain + shift, scaled, inverse)


def normalize_back(incoming, scaled, inverse, gain):
    along = incoming * gain
    inner = (
        along
        - jnp.mean(along, axis=-1, keepdims=True)
        - scaled * jnp.mean(along * scaled, axis=-1, keepdims=True)
    )
    return (inverse * inner, jnp.sum(incoming * scaled, axis=0), jnp.sum(incoming, axis=0))


def split_heads(row_array):
    return row_array.reshape(row_array.shape[0], -1, DH)


def general(
    tokens,
    w_query,
    w_key,
    w_value,
    w_out,
    b_query,
    b_value,
    b_out,
    norm1_gain,
    norm1_shift,
    w_in,
    b_in,
    w_back,
    b_back,
    norm2_gain,
    norm2_shift,
    cotangent,
):
    f32 = jnp.float32
    bf16 = jnp.bfloat16
    attn_parts = (
        lax.all_gather(w_query, ("dp", "ctx"), axis=0, tiled=True),
        lax.all_gather(w_key, ("dp", "ctx"), axis=0, tiled=True),
        lax.all_gather(w_value, ("dp", "ctx"), axis=0, tiled=True),
        lax.all_gather(w_out, ("dp", "ctx"), axis=0, tiled=True),
        lax.all_gather(b_query, ("dp", "ctx"), axis=0, tiled=True),
        lax.all_gather(b_value, ("dp", "ctx"), axis=0, tiled=True),
        lax.all_gather(b_out, ("dp", "ctx"), axis=0, tiled=True),
        lax.all_gather(norm1_gain, ("dp", "ctx"), axis=0, tiled=True),
        lax.all_gather(norm1_shift, ("dp", "ctx"), axis=0, tiled=True),
    )
    wq_full, wk_full, wv_full, wo_full, bq_full, bv_full, bo_full, gain_one, shift_one = attn_parts
    row_count = tokens.shape[0]
    model_width = tokens.shape[1]
    residual = tokens.astype(f32)
    query_rows = (
        jnp.dot(tokens, wq_full, preferred_element_type=f32) + bq_full.astype(f32)
    ).astype(bf16)
    key_rows = jnp.dot(tokens, wk_full, preferred_element_type=f32).astype(bf16)
    value_rows = (
        jnp.dot(tokens, wv_full, preferred_element_type=f32) + bv_full.astype(f32)
    ).astype(bf16)
    query_heads = split_heads(query_rows)
    key_local = split_heads(key_rows)
    value_local = split_heads(value_rows)
    portion = (
        lax.all_gather(key_rows, "ctx", axis=0, tiled=True),
        lax.all_gather(value_rows, "ctx", axis=0, tiled=True),
    )
    key_heads = split_heads(portion[0])
    value_heads = split_heads(portion[1])
    scores = jnp.einsum("qhd,khd->hqk", query_heads, key_heads, preferred_element_type=f32) * 0.125
    weights = jnp.exp(scores)
    summed = jnp.einsum(
        "hqk,khd->qhd", weights.astype(bf16), value_heads, preferred_element_type=f32
    )
    summed_all = summed.reshape(row_count, model_width)
    totals = jnp.sum(weights, axis=-1)
    totals_rows = jnp.transpose(totals)
    mixed_heads = split_heads(summed_all) / totals_rows[:, :, None]
    mixed = mixed_heads.reshape(row_count, model_width)
    mixed_low = mixed.astype(bf16)
    branch_attn = jnp.dot(mixed_low, wo_full, preferred_element_type=f32) + bo_full.astype(f32)
    gain_one32 = gain_one.astype(f32)
    stream_one = residual + branch_attn
    hidden, scaled_one, inverse_one = normalize(stream_one, gain_one32, shift_one.astype(f32))
    ffn_parts = (
        lax.all_gather(w_in, ("dp", "ctx"), axis=0, tiled=True),
        lax.all_gather(w_back, ("dp", "ctx"), axis=0, tiled=True),
        lax.all_gather(b_in, ("dp", "ctx"), axis=0, tiled=True),
        lax.all_gather(b_back, ("dp", "ctx"), axis=0, tiled=True),
        lax.all_gather(norm2_gain, ("dp", "ctx"), axis=0, tiled=True),
        lax.all_gather(norm2_shift, ("dp", "ctx"), axis=0, tiled=True),
    )
    w1_full, w2_full, b1_full, b2_full, gain_two, shift_two = ffn_parts
    hidden_low = hidden.astype(bf16)
    pre_act = jnp.dot(hidden_low, w1_full, preferred_element_type=f32) + b1_full.astype(f32)
    activated, gelu_pull = jax.vjp(partial(jax.nn.gelu, approximate=False), pre_act)
    act_low = activated.astype(bf16)
    branch_ffn = jnp.dot(act_low, w2_full, preferred_element_type=f32) + b2_full.astype(f32)
    gain_two32 = gain_two.astype(f32)
    normed_out, scaled_two, inverse_two = normalize(
        hidden + branch_ffn, gain_two32, shift_two.astype(f32)
    )
    layer_out = normed_out.astype(bf16)
    square_sums = lax.psum(
        (jnp.sum(residual * residual), jnp.sum(stream_one * stream_one)), ("dp", "ctx")
    )
    entries = row_count * model_width * lax.axis_size("dp") * lax.axis_size("ctx")
    rms_values = jnp.sqrt(jnp.stack(square_sums) / entries)
    upstream = cotangent.astype(f32)
    dsum_two, gain_two_grad, shift_two_grad = normalize_back(
        upstream, scaled_two, inverse_two, gain_two32
    )
    ffn_grad = dsum_two.astype(bf16)
    b2_grad = jnp.sum(ffn_grad, axis=0, dtype=f32)
    w2_grad = jnp.einsum("tf,td->fd", act_low, ffn_grad, preferred_element_type=f32)
    act_grad = jnp.einsum("td,fd->tf", ffn_grad, w2_full, preferred_element_type=f32)
    pre_grad = gelu_pull(act_grad)[0].astype(bf16)
    b1_grad = jnp.sum(pre_grad, axis=0, dtype=f32)
    w1_grad = jnp.einsum("td,tf->df", hidden_low, pre_grad, preferred_element_type=f32)
    hidden_grad = dsum_two + jnp.einsum("tf,df->td", pre_grad, w1_full, preferred_element_type=f32)
    dsum_one, gain_one_grad, shift_one_grad = normalize_back(
        hidden_grad, scaled_one, inverse_one, gain_one32
    )
    attn_grad = dsum_one.astype(bf16)
    bo_grad = jnp.sum(attn_grad, axis=0, dtype=f32)
    wo_grad = jnp.einsum("te,td->ed", mixed_low, attn_grad, preferred_element_type=f32)
    mixed_grad = split_heads(
        jnp.einsum("td,ed->te", attn_grad, wo_full, preferred_element_type=f32)
    )
    grad_heads = (mixed_grad / totals_rows[:, :, None]).astype(bf16)
    delta_rows = jnp.sum(mixed_grad * mixed_heads, axis=-1) / totals_rows
    delta_heads = jnp.transpose(delta_rows)
    grad_rows = grad_heads.reshape(row_count, model_width)
    portion = (
        lax.all_gather(key_rows, "ctx", axis=0, tiled=True),
        lax.all_gather(value_rows, "ctx", axis=0, tiled=True),
    )
    key_heads = split_heads(portion[0])
    value_heads = split_heads(portion[1])
    scores = jnp.einsum("qhd,khd->hqk", query_heads, key_heads, preferred_element_type=f32) * 0.125
    weights = jnp.exp(scores)
    across = jnp.einsum("qhd,khd->hqk", grad_heads, value_heads, preferred_element_type=f32)
    slopes = (weights * (across - delta_heads[:, :, None])).astype(bf16)
    part_grad = jnp.einsum("hqk,khd->qhd", slopes, key_heads, preferred_element_type=f32)
    query_acc = part_grad.reshape(row_count, model_width)
    delta_all = lax.all_gather(delta_rows, "ctx", axis=0, tiled=True)
    portion = (
        lax.all_gather(query_rows, "ctx", axis=0, tiled=True),
        lax.all_gather(grad_rows, "ctx", axis=0, tiled=True),
    )
    query_part = split_heads(portion[0])
    grad_part = split_heads(portion[1])
    scores = jnp.einsum("qhd,khd->hqk", query_part, key_local, preferred_element_type=f32) * 0.125
    weights = jnp.exp(scores)
    value_part = jnp.einsum(
        "hqk,qhd->khd", weights.astype(bf16), grad_part, preferred_element_type=f32
    )
    across = jnp.einsum("qhd,khd->hqk", grad_part, value_local, preferred_element_type=f32)
    slopes = (weights * (across - jnp.transpose(delta_all)[:, :, None])).astype(bf16)
    key_part = jnp.einsum("hqk,qhd->khd", slopes, query_part, preferred_element_type=f32)
    key_acc = key_part.reshape(row_count, model_width)
    value_acc = value_part.reshape(row_count, model_width)
    query_grad = (0.125 * query_acc).astype(bf16)
    key_grad = (0.125 * key_acc).astype(bf16)
    value_grad = value_acc.astype(bf16)
    wq_grad = jnp.einsum("td,te->de", tokens, query_grad, preferred_element_type=f32)
    wk_grad = jnp.einsum("td,te->de", tokens, key_grad, preferred_element_type=f32)
    wv_grad = jnp.einsum("td,te->de", tokens, value_grad, preferred_element_type=f32)
    bq_grad = jnp.sum(query_grad, axis=0, dtype=f32)
    bv_grad = jnp.sum(value_grad, axis=0, dtype=f32)
    input_grad = (
        dsum_one
        + jnp.einsum("te,de->td", query_grad, wq_full, preferred_element_type=f32)
        + jnp.einsum("te,de->td", key_grad, wk_full, preferred_element_type=f32)
        + jnp.einsum("te,de->td", value_grad, wv_full, preferred_element_type=f32)
    )
    attn_owned = (
        lax.psum_scatter(wq_grad, ("dp", "ctx"), scatter_dimension=0, tiled=True),
        lax.psum_scatter(wk_grad, ("dp", "ctx"), scatter_dimension=0, tiled=True),
        lax.psum_scatter(wv_grad, ("dp", "ctx"), scatter_dimension=0, tiled=True),
        lax.psum_scatter(wo_grad, ("dp", "ctx"), scatter_dimension=0, tiled=True),
        lax.psum_scatter(bq_grad, ("dp", "ctx"), scatter_dimension=0, tiled=True),
        lax.psum_scatter(bv_grad, ("dp", "ctx"), scatter_dimension=0, tiled=True),
        lax.psum_scatter(bo_grad, ("dp", "ctx"), scatter_dimension=0, tiled=True),
        lax.psum_scatter(gain_one_grad, ("dp", "ctx"), scatter_dimension=0, tiled=True),
        lax.psum_scatter(shift_one_grad, ("dp", "ctx"), scatter_dimension=0, tiled=True),
    )
    ffn_owned = (
        lax.psum_scatter(w1_grad, ("dp", "ctx"), scatter_dimension=0, tiled=True),
        lax.psum_scatter(b1_grad, ("dp", "ctx"), scatter_dimension=0, tiled=True),
        lax.psum_scatter(w2_grad, ("dp", "ctx"), scatter_dimension=0, tiled=True),
        lax.psum_scatter(b2_grad, ("dp", "ctx"), scatter_dimension=0, tiled=True),
        lax.psum_scatter(gain_two_grad, ("dp", "ctx"), scatter_dimension=0, tiled=True),
        lax.psum_scatter(shift_two_grad, ("dp", "ctx"), scatter_dimension=0, tiled=True),
    )
    return (
        layer_out,
        input_grad,
        attn_owned[0],
        attn_owned[1],
        attn_owned[2],
        attn_owned[3],
        attn_owned[4],
        attn_owned[5],
        attn_owned[6],
        attn_owned[7],
        attn_owned[8],
        ffn_owned[0],
        ffn_owned[1],
        ffn_owned[2],
        ffn_owned[3],
        ffn_owned[4],
        ffn_owned[5],
        rms_values,
    )


def solution(mesh):
    rows, flat = P(("dp", "ctx"), None), P(("dp", "ctx"))
    in_specs = (rows,) * 5 + (flat,) * 5 + (rows, flat, rows) + (flat,) * 3 + (rows,)
    out_specs = (rows,) * 6 + (flat,) * 5 + (rows, flat, rows) + (flat,) * 3 + (P(),)
    body = fused if (mesh.shape["dp"], mesh.shape["ctx"]) == (4, 8) else general
    return jax.shard_map(body, mesh=mesh, in_specs=in_specs, out_specs=out_specs, check_vma=False)
```

```python
from functools import partial

import jax
import jax.numpy as jnp
from jax import lax
from jax.experimental import pallas as pl
from jax.experimental.pallas import tpu as pltpu
from jax.sharding import PartitionSpec as P

MESH = pl.DeviceIdType.MESH
f32 = jnp.float32
bf16 = jnp.bfloat16
DH = 64
epsilon = 1e-12
COPIES = 87


def dot(a, b, ca=1, cb=0):
    return lax.dot_general(a, b, (((ca,), (cb,)), ((), ())), preferred_element_type=f32)


def norm_parts(values):
    average = jnp.mean(values, axis=-1, keepdims=True)
    centered = values - average
    spread = jnp.mean(centered * centered, axis=-1, keepdims=True)
    inverse = lax.rsqrt(spread + epsilon)
    return centered * inverse, inverse


def norm_back(incoming, scaled, inverse, gain):
    along = incoming * gain
    return inverse * (
        along
        - jnp.mean(along, axis=-1, keepdims=True)
        - scaled * jnp.mean(along * scaled, axis=-1, keepdims=True)
    )


def wide(*refs):
    total = refs[0].astype(f32)
    for ref in refs[1:]:
        total = total + ref.astype(f32)
    return total


class Copy:
    def __init__(self, parts, whole, goes, comes):
        self.parts, self.whole, self.goes, self.comes, self.waited = parts, whole, goes, comes, False

    def _if(self, condition, act):
        if condition is None:
            act()
        else:
            pl.when(condition)(act)

    def start(self):
        def act():
            for part in self.parts:
                part.start()

        self._if(self.goes, act)

    def landed(self):
        self.waited = True
        self._if(self.comes, self.whole.wait_recv)

    def left(self):
        self._if(self.goes, self.whole.wait_send)


def landed(copies):
    for copy in copies:
        copy.landed()


ORDER = [
    16 * ((b // 8) % 2) + 4 * (2 * (b // 16) + b % 2) + (b % 8) // 2 for b in range(32)
]


def layer_kernel(
    tok, cot, wq, wk, wv, wo, wi, wb, bq, bv, bo, g1, s1, bb, g2, s2, bi,
    lo_out, igr, la, do_out, di_out, db_out, sm_out,
    xr, cr, xg, pa, sa, si, sb, wa_f, wi_f, wb_f, wo_b, wo_f,
    vec32, sm0, smr, sm1, smz, sm2, sms, vf,
    qs, kv, ee, mt, tot, mxs, mix, po, ro, hid, xh1, iv1, hg, gp, act, ds2, dg, dp, da, dms, dmi,
    dmt, dqt, dkv, kvr, dall, ds1,
    ga, ga_b, ra, s_a, za, fa,
    gi, gi_b, ri, s_i, zi, fi,
    gb, gb_b, rb, s_b, zb, fb,
    go_b, r_o, s_o, p_o, t_o, z_o,
    los, igs, gs0, gsr, gs1, gsz, gs2, gss,
    ssem, rsem,
):
    d = lax.axis_index("dp")
    k = lax.axis_index("ctx")
    y, c = d // 2, d % 2
    z, x = k // 2, k % 2
    q = 2 * y + x
    r = 8 * d + k

    def dev(xx, yy, cc, zz):
        return (2 * yy + cc, 2 * zz + xx)

    def mate_q(m):
        a, b = m % 2, m // 2
        return 2 * ((y + b) % 2) + (x + a) % 2

    def mate(m):
        a, b = m % 2, m // 2
        return dev((x + a) % 2, (y + b) % 2, c, z)

    def plane(dz):
        return dev(x, y, c, (z + dz) % 4)

    sibling = dev(x, y, 1 - c, z)
    pd, pz = 2 * (z % 2) + z // 2, 2 * c + y
    partner = (pd, 2 * pz + x)
    alone = (pd == d) & (pz == z)
    moves = jnp.logical_not(alone)
    cross = dev(c, y, x, z)
    stays = x == c
    crosses = jnp.logical_not(stays)

    bar = pltpu.get_barrier_semaphore()
    near = [mate(1), mate(2), mate(3), sibling, plane(1), plane(2), plane(3)]
    for other in near:
        pl.semaphore_signal(bar, inc=1, device_id=other, device_id_type=MESH)

    @pl.when(moves)
    def _():
        pl.semaphore_signal(bar, inc=1, device_id=partner, device_id_type=MESH)

    @pl.when(crosses)
    def _():
        pl.semaphore_signal(bar, inc=1, device_id=cross, device_id_type=MESH)

    pl.semaphore_wait(bar, len(near) + 2 - alone.astype(jnp.int32) - stays.astype(jnp.int32))

    sends = []

    def send(*transfers, size=None, goes=None, comes=None):
        i = len(sends)

        def copy_of(src, dst, to):
            return pltpu.make_async_remote_copy(
                src_ref=src, dst_ref=dst, send_sem=ssem.at[i], recv_sem=rsem.at[i],
                device_id=to, device_id_type=MESH,
            )

        parts = [copy_of(*transfer) for transfer in transfers]
        whole = parts[0] if size is None else copy_of(size, size, transfers[0][2])
        copy = Copy(parts, whole, goes, comes)
        copy.start()
        sends.append(copy)
        return copy

    def swap(src, dst, to, here):
        there = jnp.logical_not(here)
        copy = send((src, dst, to), goes=there, comes=there)

        @pl.when(here)
        def _():
            dst[...] = src[...]

        return copy

    def gather(ref):
        return [send((ref.at[q], ref.at[q], mate(m))) for m in (1, 2, 3)]

    def to_mates(src, dst):
        return send(
            *[(src.at[mate_q(m)], dst.at[q], mate(m)) for m in (1, 2, 3)], size=src.at[pl.ds(0, 3)]
        )

    def share(src, dst, others):
        return send(*[(src, dst.at[i], other) for i, other in enumerate(others)], size=dst)

    mates = [mate(1), mate(2), mate(3)]
    planes = [plane(1), plane(2), plane(3)]
    ends = (z == 0) | (z == 3)
    middle = jnp.logical_not(ends)

    def spread(part, size):
        def copy(to, goes, comes):
            return send(*[(ref, ref, to) for ref in part(z)], size=size, goes=goes, comes=comes)

        return [
            copy(plane(2), None, None), copy(plane(1), z < 3, z > 0), copy(plane(3), z > 0, z < 3)
        ]

    def spread_on(copies, part, size):
        copies[0].landed()
        to = dev(x, y, c, lax.rem(3 * (z + 3), 4))
        far = lax.rem(z + 2, 4)
        last = send(*[(ref, ref, to) for ref in part(far)], size=size, goes=middle, comes=ends)
        return copies[1:] + [last]

    def collect(low, landing):
        return [
            send((low.at[3 - z], landing.at[3], dev(x, y, c, lax.rem(z + 1 + 2 * (z // 3), 4))),
                 goes=ends, comes=middle),
            send((low.at[lax.rem(z + 1, 4)], landing.at[0], plane(1)), goes=z < 3, comes=z > 0),
            send((low.at[lax.rem(z + 3, 4)], landing.at[1], plane(3)), goes=z > 0, comes=z < 3),
        ]

    def collect_on(copies, low, landing):
        copies[0].landed()
        far = lax.rem(z + 2, 4)

        @pl.when(middle)
        def _():
            low[far] = wide(low[far], landing[3]).astype(bf16)

        return copies[1:] + [send((low.at[far], landing.at[2], plane(2)))]

    @pl.when(z == 0)
    def _():
        for ref in (za, zi, zb, z_o):
            ref[0] = jnp.zeros_like(ref[0])

    @pl.when(z == 3)
    def _():
        for ref in (za, zi, zb, z_o):
            ref[1] = jnp.zeros_like(ref[1])

    halves = [slice(0, 64), slice(64, 128)]
    c_tok = [swap(tok.at[rows, :], xr.at[rows, :], partner, alone) for rows in halves]
    for j in range(4):
        cols = slice(192 * j, 192 * j + 192)
        pa[j] = jnp.concatenate([wq[:, cols], wk[:, cols], wv[:, cols]], axis=1)
    sa[q] = pa[q]
    c_sa = to_mates(pa, sa)
    vec32[...] = jnp.zeros_like(vec32)
    for i, ref in enumerate((bq, bv, bo, g1, s1, bb, g2, s2)):
        vec32[i:i + 1, :24] = ref[...].astype(f32)
    vec32[8:9, :96] = bi[...].astype(f32)
    row = lax.broadcasted_iota(jnp.int32, (16, 768), 0)
    placed = jnp.where(row < 8, pltpu.roll(vec32[...], 24 * r, 1), 0.0)
    b_in_row = pltpu.roll(vec32[...], 96 * (r % 8), 1)[8:9]
    placed = placed + jnp.where(row == 8 + r // 8, b_in_row, 0.0)
    sm0[...] = placed.astype(bf16)
    c_sm = share(sm0, smr, mates)

    def in_cols(ref, j):
        return ref.at[:, pl.ds(pl.multiple_of(768 * j, 768), 768)]

    si[q] = wi[:, pl.ds(pl.multiple_of(768 * q, 768), 768)]
    c_si = send(
        *[(in_cols(wi, mate_q(m)), si.at[q], mate(m)) for m in (1, 2, 3)], size=si.at[pl.ds(0, 3)]
    )
    c_sb = swap(wb, sb, cross, stays)

    def own_rows(b, zz):
        return pl.ds(pl.multiple_of(384 * b + 192 * c + 48 * zz, 16), 48)

    def core_rows(b, cc):
        return pl.ds(pl.multiple_of(384 * b + 192 * cc, 16), 192)

    def b_rows(b, zz, cc):
        return pl.ds(pl.multiple_of(96 * (2 * zz + cc), 96), 96)

    def bundle(arrived, full):
        for b in range(2):
            full[own_rows(b, z), :] = jnp.concatenate([arrived[2 * b], arrived[2 * b + 1]], axis=0)

    def rows_a(zz):
        return [wa_f.at[own_rows(b, zz), :] for b in range(2)]

    def rows_i(zz):
        return [wi_f.at[own_rows(b, zz), :] for b in range(2)]

    def rows_b(zz):
        return [wb_f.at[b_rows(0, zz, c), :]]

    def rows_o(zz):
        return [wo_b.at[16 * c + 4 * q + zz]]

    size_a, size_i = wa_f.at[pl.ds(0, 96), :], wi_f.at[pl.ds(0, 96), :]

    c_sa.landed()
    bundle(sa, wa_f)
    c_za = spread(rows_a, size_a)

    c_sm.landed()
    sm1[...] = wide(sm0[...], smr[0], smr[1], smr[2]).astype(bf16)
    c_smz = share(sm1, smz, planes)

    c_xg = []
    for h, rows in enumerate(halves):
        c_tok[h].landed()
        xg[q, rows, :] = xr[rows, :]
        c_xg.append([send((xg.at[q, rows, :], xg.at[q, rows, :], to)) for to in mates])

    c_smz.landed()
    sm2[...] = wide(sm1[...], smz[0], smz[1], smz[2]).astype(bf16)
    c_sms = send((sm2, sms, sibling))

    c_za = spread_on(c_za, rows_a, size_a)
    wo_b[16 * c + 4 * q + z] = wo[...]
    c_zo = spread(rows_o, None)
    landed(c_za)
    c_ca = send(
        *[(wa_f.at[core_rows(b, c), :], wa_f.at[core_rows(b, c), :], sibling) for b in range(2)],
        size=wa_f.at[pl.ds(0, 384), :],
    )

    c_si.landed()
    bundle(si, wi_f)
    c_zi = spread(rows_i, size_i)
    c_sb.landed()
    wb_f[b_rows(0, z, c), :] = sb[...]
    c_zb = spread(rows_b, None)
    c_zo = spread_on(c_zo, rows_o, None)

    c_sms.landed()
    vf[...] = wide(sm2[...], sms[...])
    b_out, gain1, shift1 = vf[2:3], vf[3:4], vf[4:5]
    b_back, gain2, shift2 = vf[5:6], vf[6:7], vf[7:8]
    turned = pltpu.roll(vf[...], lax.rem(768 - 192 * q, 768), 1)
    b_qkv = jnp.concatenate(
        [turned[0:1, :192], jnp.zeros((1, 192), f32), turned[1:2, :192]], axis=1
    )
    b_in = jnp.sum(jnp.where(row == 8 + q, vf[...], 0.0), axis=0, keepdims=True)

    c_ca.landed()
    c_kv = []
    for m in range(4):
        j = mate_q(m)
        if m:
            for copies in c_xg:
                copies[m - 1].landed()
        out = dot(xg[j], wa_f[...]) + b_qkv
        rows = pl.ds(pl.multiple_of(128 * j, 128), 128)
        qs[rows, :] = (out[:, :192].astype(bf16).astype(f32) * 0.125).astype(bf16)
        kv[c, rows, :] = out[:, 192:].astype(bf16)
        c_kv.append(send((kv.at[c, rows, :], kv.at[c, rows, :], sibling)))

    landed(c_zo)
    chip_o = pl.ds(pl.multiple_of(16 * c + 4 * q, 4), 4)
    core_o = pl.ds(pl.multiple_of(16 * c, 16), 16)
    c_po = send(
        *[(wo_b.at[chip_o], wo_b.at[chip_o], to) for to in mates], size=wo_b.at[pl.ds(0, 12)]
    )
    c_zi = spread_on(c_zi, rows_i, size_i)

    mt[...] = jnp.zeros_like(mt)
    tot[...] = jnp.zeros_like(tot)

    def expo_rows(h, slot, part):
        return slice(1024 * h + 512 * slot + 256 * part, 1024 * h + 512 * slot + 256 * part + 256)

    def forward_chunk(half, slot, part):
        rows = slice(256 * part, 256 * part + 256)
        keys_values = kv[half, rows, :]
        for h in range(3):
            key = keys_values[:, 64 * h:64 * h + 64]
            value = keys_values[:, 192 + 64 * h:256 + 64 * h]
            query = qs[:, 64 * h:64 * h + 64]
            expo = jnp.exp(dot(key, query, 1, 1))
            low = expo.astype(bf16)
            ee[expo_rows(h, slot, part), :] = low
            tot[h:h + 1, :] += jnp.sum(expo, axis=0, keepdims=True)
            mt[64 * h:64 * h + 64, :] += dot(value, low, 0, 0)

    forward_chunk(c, 0, 0)
    forward_chunk(c, 0, 1)
    c_zb = spread_on(c_zb, rows_b, None)
    landed(c_kv)
    forward_chunk(1 - c, 1, 0)
    forward_chunk(1 - c, 1, 1)
    for h in range(3):
        part = slice(64 * h, 64 * h + 64)
        mt[part, :] = mt[part, :] / tot[h:h + 1, :]
    for j in range(4):
        mxs[j] = mt[:, 128 * j:128 * j + 128].astype(bf16)
    mix[q] = mxs[q]
    c_mix = to_mates(mxs, mix)

    c_po.landed()
    c_co = send((wo_b.at[core_o], wo_b.at[core_o], sibling))
    c_cot = swap(cot, cr, partner, alone)
    c_co.landed()
    for b in range(32):
        wo_f[24 * b:24 * b + 24, :] = wo_b[ORDER[b]]
    c_mix.landed()
    mixed = mix[...].reshape(768, 128)
    attn = dot(mixed, wo_f[...], 0, 0) + b_out
    x32 = xr[...].astype(f32)
    stream = x32 + attn
    squares_x = jnp.sum(x32 * x32)
    squares_s = jnp.sum(stream * stream)
    scaled, inverse = norm_parts(stream)
    xh1[...] = scaled
    iv1[...] = jnp.broadcast_to(inverse, iv1.shape)
    hidden = scaled * gain1 + shift1
    hid[...] = hidden
    hg[q] = hidden.astype(bf16)
    c_hg = gather(hg)

    landed(c_zi)
    c_ci = send(
        *[(wi_f.at[core_rows(b, c), :], wi_f.at[core_rows(b, c), :], sibling) for b in range(2)],
        size=wi_f.at[pl.ds(0, 384), :],
    )
    landed(c_zb)
    c_cb = send(
        *[(wb_f.at[b_rows(0, zz, c), :], wb_f.at[b_rows(0, zz, c), :], sibling) for zz in range(4)],
        size=wb_f.at[pl.ds(0, 384), :],
    )
    c_ci.landed()
    c_cb.landed()

    def ffn(j):
        pre = dot(hg[j], wi_f[...]) + b_in
        phi = 0.5 + 0.5 * lax.erf(pre * 0.7071067811865476)
        gp[j] = phi + pre * jnp.exp(-0.5 * pre * pre) * 0.3989422804014327
        act[j] = (pre * phi).astype(bf16)
        return dot(act[j], wb_f[...])

    own_part = ffn(q)
    c_ffn = []
    for m in (1, 2, 3):
        c_hg[m - 1].landed()
        j = mate_q(m)
        po[j] = ffn(j).astype(bf16)
        c_ffn.append(send((po.at[j], ro.at[m - 1], mate(m))))
    landed(c_ffn)
    out = own_part + b_back + wide(ro[0], ro[1], ro[2])
    scaled2, inverse2 = norm_parts(hid[...] + out)
    los[...] = (scaled2 * gain2 + shift2).astype(bf16)
    c_cot.landed()
    dy = cr[...].astype(f32)
    gain2_grad = jnp.sum(dy * scaled2, axis=0, keepdims=True)
    shift2_grad = jnp.sum(dy, axis=0, keepdims=True)
    dsum2 = norm_back(dy, scaled2, inverse2, gain2)
    ds2[...] = dsum2
    low = dsum2.astype(bf16)
    dg[q] = low
    back_grad = jnp.sum(low.astype(f32), axis=0, keepdims=True)
    c_dg = gather(dg)
    c_lo = swap(los, lo_out, partner, alone)

    def ffn_back(j):
        dact = dot(dg[j], wb_f[...], 1, 1)
        dp[j] = (dact * gp[j]).astype(bf16)
        return dot(dp[j], wi_f[...], 1, 1)

    own_part = ffn_back(q)
    c_dh = []
    for m in (1, 2, 3):
        c_dg[m - 1].landed()
        j = mate_q(m)
        po[4 + j] = ffn_back(j).astype(bf16)
        c_dh.append(send((po.at[4 + j], ro.at[2 + m], mate(m))))

    def weight_grad(left, right, out, low, rows):
        for i in range(rows // 256):
            cols = slice(256 * i, 256 * i + 256)
            part = dot(left[:, cols], right, 0, 0)
            out[cols, :] = part
            low[cols, :] = part.astype(bf16)

    def flat(ref):
        return ref[...].reshape(512, ref.shape[-1])

    weight_grad(flat(act), flat(dg), gb, gb_b, 768)
    c_rb = send(
        *[(gb_b.at[b_rows(0, zz, 1 - c), :], rb.at[zz], sibling) for zz in range(4)], size=rb
    )
    weight_grad(flat(hg), flat(dp), gi, gi_b, 768)
    c_ri = send(
        *[(gi_b.at[core_rows(b, 1 - c), :], ri.at[b], sibling) for b in range(2)], size=ri
    )
    in_grad = jnp.sum(flat(dp).astype(f32), axis=0, keepdims=True)

    def row_sums(copy, mine, theirs, low, landing):
        copy.landed()
        for zz in range(4):
            low[zz] = wide(mine[b_rows(0, zz, c), :], theirs[zz]).astype(bf16)
        return collect(low, landing)

    def col_sums(copy, mine, theirs, low, landing):
        copy.landed()
        for zz in range(4):
            for b in range(2):
                part = wide(mine[own_rows(b, zz), :], theirs[b, 48 * zz:48 * zz + 48, :])
                low[zz, 48 * b:48 * b + 48, :] = part.astype(bf16)
        return collect(low, landing)

    c_zgb = row_sums(c_rb, gb, rb, s_b, zb)
    c_zgi = col_sums(c_ri, gi, ri, s_i, zi)

    landed(c_dh)
    dhidden = ds2[...] + own_part + wide(ro[3], ro[4], ro[5])
    gain1_grad = jnp.sum(dhidden * xh1[...], axis=0, keepdims=True)
    shift1_grad = jnp.sum(dhidden, axis=0, keepdims=True)
    dsum1 = norm_back(dhidden, xh1[...], iv1[:, :1], gain1)
    ds1[...] = dsum1
    low = dsum1.astype(bf16)
    da[...] = low
    out_grad = jnp.sum(low.astype(f32), axis=0, keepdims=True)
    dmixed_t = dot(wo_f[...], da[...], 1, 1)
    for j in range(4):
        dms[j] = dmixed_t[192 * j:192 * j + 192].astype(bf16)
    dmi[q] = dms[q]
    c_dm = to_mates(dms, dmi)
    c_zgb = collect_on(c_zgb, s_b, zb)

    part = dot(mix[...].reshape(768, 128), da[...])
    for b in range(32):
        go_b[ORDER[b]] = part[24 * b:24 * b + 24].astype(bf16)
    other_o = pl.ds(pl.multiple_of(16 * (1 - c), 16), 16)
    c_rgo = send((go_b.at[other_o], r_o, sibling))

    c_dm.landed()
    for j in range(4):
        dmt[:, 128 * j:128 * j + 128] = dmi[j].astype(f32)
    dqt[...] = jnp.zeros_like(dqt)
    c_zgi = collect_on(c_zgi, s_i, zi)

    def backward_chunk(half, slot, part):
        rows = slice(256 * part, 256 * part + 256)
        keys_values = kv[half, rows, :]
        dkeys, dvalues = [], []
        for h in range(3):
            span = slice(64 * h, 64 * h + 64)
            key = keys_values[:, span]
            value = keys_values[:, 192 + 64 * h:256 + 64 * h]
            query = qs[:, span]
            over = 1.0 / tot[h:h + 1, :]
            dmixed = dmt[span, :]
            dsummed = (dmixed * over).astype(bf16)
            delta = jnp.sum(dmixed * mt[span, :], axis=0, keepdims=True) * over
            expo = ee[expo_rows(h, slot, part), :]
            across = dot(value, dsummed)
            slopes = (expo.astype(f32) * (across - delta)).astype(bf16)
            dvalues.append(dot(expo, dsummed, 1, 1))
            dkeys.append(dot(slopes, query))
            dqt[span, :] += dot(key, slopes, 0, 0)
        dkv[half, rows, :] = jnp.concatenate(dkeys + dvalues, axis=1)

    backward_chunk(1 - c, 1, 0)
    backward_chunk(1 - c, 1, 1)
    c_dkv = send((dkv.at[1 - c], kvr, sibling))
    c_rgo.landed()
    for i in range(16):
        s_o[i] = wide(go_b[16 * c + i], r_o[i]).astype(bf16)
    c_pgo = send(
        *[(s_o.at[pl.ds(4 * mate_q(m), 4)], p_o.at[m - 1], mate(m)) for m in (1, 2, 3)], size=p_o
    )
    backward_chunk(c, 0, 0)
    backward_chunk(c, 0, 1)
    dall[:, :192] = jnp.transpose(dqt[...] * 0.125).astype(bf16)
    c_dkv.landed()
    dall[:, 192:] = (dkv[c] + kvr[...]).astype(bf16)

    own = pl.ds(pl.multiple_of(128 * q, 128), 128)
    for m in (1, 2, 3):
        j = mate_q(m)
        rows = pl.ds(pl.multiple_of(128 * j, 128), 128)
        po[8 + j] = dot(dall[rows, :], wa_f[...], 1, 1).astype(bf16)
    c_dx = [
        send(
            *[(po.at[8 + mate_q(m), rows, :], ro.at[5 + m, rows, :], mate(m)) for m in (1, 2, 3)],
            size=ro.at[pl.ds(6, 3), rows, :],
        )
        for rows in halves
    ]
    ds1[...] += dot(dall[own, :], wa_f[...], 1, 1)

    weight_grad(flat(xg), dall[...], ga, ga_b, 768)
    c_rga = send(
        *[(ga_b.at[core_rows(b, 1 - c), :], ra.at[b], sibling) for b in range(2)], size=ra
    )
    sums = jnp.sum(dall[...].astype(f32), axis=0, keepdims=True)

    rest = jnp.zeros((1, 576), f32)
    head_rows = jnp.concatenate(
        [jnp.concatenate([sums[:, :192], rest], axis=1),
         jnp.concatenate([sums[:, 384:], rest], axis=1),
         jnp.zeros((6, 768), f32)], axis=0,
    )
    gs0[0:8, :] = pltpu.roll(head_rows, 192 * q, 1)
    gs0[2:3, :] = out_grad
    gs0[3:4, :] = gain1_grad
    gs0[4:5, :] = shift1_grad
    gs0[5:6, :] = back_grad
    gs0[6:7, :] = gain2_grad
    gs0[7:8, :] = shift2_grad
    row2 = lax.broadcasted_iota(jnp.int32, (8, 768), 0)
    gs0[8:16, :] = (
        jnp.where(row2 == q, in_grad, 0.0)
        + jnp.where(row2 == 4, squares_x, 0.0)
        + jnp.where(row2 == 5, squares_s, 0.0)
    )
    c_gs = share(gs0, gsr, mates)

    c_zga = col_sums(c_rga, ga, ra, s_a, za)
    c_pgo.landed()
    for i in range(4):
        t_o[i] = wide(s_o[4 * q + i], p_o[0, i], p_o[1, i], p_o[2, i]).astype(bf16)
    c_zgo = collect(t_o, z_o)

    c_ig = []
    for h, rows in enumerate(halves):
        c_dx[h].landed()
        grad = ds1[rows, :] + wide(ro[6, rows, :], ro[7, rows, :], ro[8, rows, :])
        igs[rows, :] = grad.astype(bf16)
        c_ig.append(swap(igs.at[rows, :], igr.at[rows, :], partner, alone))

    c_zga = collect_on(c_zga, s_a, za)
    c_zgo = collect_on(c_zgo, t_o, z_o)
    c_gs.landed()
    gs1[...] = gs0[...] + gsr[0] + gsr[1] + gsr[2]
    c_gsz = share(gs1, gsz, planes)

    landed(c_zgb)
    fb[...] = wide(s_b[z], zb[0], zb[1], zb[2]).astype(bf16)
    c_fb = swap(fb, db_out, cross, stays)

    def col_final(copies, low, landing, out):
        landed(copies)
        for i in range(4):
            rows = slice(24 * i, 24 * i + 24)
            out[i] = wide(
                low[z, rows, :], landing[0, rows, :], landing[1, rows, :], landing[2, rows, :]
            ).astype(bf16)

    col_final(c_zgi, s_i, zi, fi)
    c_fi = send(
        *[(fi.at[mate_q(m)], in_cols(di_out, q), mate(m)) for m in (1, 2, 3)],
        size=fi.at[pl.ds(0, 3)],
    )
    di_out[:, pl.ds(pl.multiple_of(768 * q, 768), 768)] = fi[q]

    col_final(c_zga, s_a, za, fa)
    la[q] = fa[q]
    c_fa = to_mates(fa, la)

    landed(c_zgo)
    do_out[...] = wide(t_o[z], z_o[0], z_o[1], z_o[2])

    c_gsz.landed()
    gs2[...] = gs1[...] + gsz[0] + gsz[1] + gsz[2]
    c_gss = send((gs2, gss, sibling))
    c_gss.landed()
    whole = gs2[...] + gss[...]
    sm_out[0:8, :] = pltpu.roll(whole, lax.rem(768 - 24 * r, 768), 1)[:8, :128]
    mine = jnp.sum(jnp.where(row == 8 + r // 8, whole, 0.0), axis=0, keepdims=True)
    mine = pltpu.roll(jnp.broadcast_to(mine, (8, 768)), lax.rem(768 - 96 * (r % 8), 768), 1)
    row3 = lax.broadcasted_iota(jnp.int32, (8, 128), 0)
    sm_out[8:16, :] = jnp.where(row3 < 4, mine[:, :128], whole[8:16, :128])

    c_lo.landed()
    c_fb.landed()
    c_fi.landed()
    c_fa.landed()
    landed(c_ig)
    assert len(sends) == COPIES, len(sends)
    for copy in sends:
        copy.left()


def finish_kernel(
    lo, ig, la, do, di, db, sm,
    lo_out, ig_out, dq_out, dk_out, dv_out, do_out, bq, bv, bo, g1, s1, di_out, bi, db_out, bb,
    g2, s2, rms_out,
):
    lo_out[...] = lo[...]
    ig_out[...] = ig[...].astype(f32)
    for j in range(4):
        cols = slice(192 * j, 192 * j + 192)
        dq_out[:, cols] = la[j, :, :192].astype(f32)
        dk_out[:, cols] = la[j, :, 192:384].astype(f32)
        dv_out[:, cols] = la[j, :, 384:].astype(f32)
    do_out[...] = do[...]
    di_out[...] = di[...].astype(f32)
    db_out[...] = db[...].astype(f32)
    for i, out in enumerate((bq, bv, bo, g1, s1, bb, g2, s2)):
        out[...] = sm[i:i + 1, :24]
    bi[...] = sm[8:9, :96]
    lane = lax.broadcasted_iota(jnp.int32, (1, 128), 1)
    means = jnp.where(lane == 0, sm[12:13, :], sm[13:14, :]) / (4096 * 768)
    rms_out[...] = jnp.sqrt(means)[:, :2]


def fused(
    tokens, w_query, w_key, w_value, w_out, b_query, b_value, b_out, norm1_gain, norm1_shift,
    w_in, b_in, w_back, b_back, norm2_gain, norm2_shift, cotangent,
):
    vectors = (
        b_query, b_value, b_out, norm1_gain, norm1_shift, b_back, norm2_gain, norm2_shift, b_in
    )
    vm = pl.BlockSpec(memory_space=pltpu.VMEM)

    def v(*shape, t=bf16):
        return pltpu.VMEM(shape, t)

    def s(*shape, t=f32):
        return jax.ShapeDtypeStruct(shape, t)

    scratch = [
        v(128, 768), v(128, 768), v(4, 128, 768), v(4, 24, 576), v(4, 24, 576), v(4, 24, 768),
        v(96, 768), v(768, 576), v(768, 768), v(768, 768), v(32, 24, 768), v(768, 768),
        v(16, 768, t=f32),
        v(16, 768), v(3, 16, 768), v(16, 768), v(3, 16, 768), v(16, 768), v(16, 768),
        v(16, 768, t=f32),
        v(512, 192), v(2, 512, 384), v(3072, 512), v(192, 512, t=f32), v(8, 512, t=f32),
        v(4, 192, 128), v(4, 192, 128), v(12, 128, 768), v(9, 128, 768),
        v(128, 768, t=f32), v(128, 768, t=f32), v(128, 128, t=f32), v(4, 128, 768),
        v(4, 128, 768, t=f32), v(4, 128, 768), v(128, 768, t=f32), v(4, 128, 768),
        v(4, 128, 768), v(128, 768), v(4, 192, 128), v(4, 192, 128),
        v(192, 512, t=f32), v(192, 512, t=f32), v(2, 512, 384, t=f32), v(512, 384, t=f32),
        v(512, 576), v(128, 768, t=f32),
        v(768, 576, t=f32), v(768, 576), v(2, 192, 576), v(4, 96, 576), v(4, 96, 576),
        v(4, 24, 576),
        v(768, 768, t=f32), v(768, 768), v(2, 192, 768), v(4, 96, 768), v(4, 96, 768),
        v(4, 24, 768),
        v(768, 768, t=f32), v(768, 768), v(4, 96, 768), v(4, 96, 768), v(4, 96, 768),
        v(96, 768),
        v(32, 24, 768), v(16, 24, 768), v(16, 24, 768), v(3, 4, 24, 768), v(4, 24, 768),
        v(4, 24, 768),
        v(128, 768), v(128, 768), v(16, 768, t=f32), v(3, 16, 768, t=f32),
        v(16, 768, t=f32), v(3, 16, 768, t=f32), v(16, 768, t=f32), v(16, 768, t=f32),
        pltpu.SemaphoreType.DMA((COPIES,)), pltpu.SemaphoreType.DMA((COPIES,)),
    ]
    parts = pl.pallas_call(
        layer_kernel,
        out_shape=(
            s(128, 768, t=bf16), s(128, 768, t=bf16), s(4, 24, 576, t=bf16), s(24, 768),
            s(24, 3072, t=bf16), s(96, 768, t=bf16), s(16, 128),
        ),
        in_specs=[vm] * 17,
        out_specs=[vm] * 7,
        scratch_shapes=scratch,
        compiler_params=pltpu.CompilerParams(
            collective_id=0, has_side_effects=True, vmem_limit_bytes=58 << 20
        ),
        name="layer",
    )(
        tokens, cotangent, w_query, w_key, w_value, w_out, w_in, w_back,
        *[vector.reshape(1, -1) for vector in vectors],
    )
    square, small = s(24, 768), s(1, 24)
    outs = pl.pallas_call(
        finish_kernel,
        out_shape=(
            (s(128, 768, t=bf16), s(128, 768)) + (square,) * 4 + (small,) * 5
            + (s(24, 3072), s(1, 96), s(96, 768)) + (small,) * 3 + (s(1, 2),)
        ),
        in_specs=[vm] * 7,
        out_specs=[vm] * 18,
        name="finish",
    )(*parts)
    return tuple(o.reshape(o.shape[1:]) if o.shape[0] == 1 else o for o in outs)


def normalize(values, gain, shift):
    average = jnp.mean(values, axis=-1, keepdims=True)
    centered = values - average
    spread = jnp.mean(centered * centered, axis=-1, keepdims=True)
    inverse = lax.rsqrt(spread + epsilon)
    scaled = centered * inverse
    return (scaled * gain + shift, scaled, inverse)


def normalize_back(incoming, scaled, inverse, gain):
    along = incoming * gain
    inner = (
        along
        - jnp.mean(along, axis=-1, keepdims=True)
        - scaled * jnp.mean(along * scaled, axis=-1, keepdims=True)
    )
    return (inverse * inner, jnp.sum(incoming * scaled, axis=0), jnp.sum(incoming, axis=0))


def split_heads(row_array):
    return row_array.reshape(row_array.shape[0], -1, DH)


def general(
    tokens,
    w_query,
    w_key,
    w_value,
    w_out,
    b_query,
    b_value,
    b_out,
    norm1_gain,
    norm1_shift,
    w_in,
    b_in,
    w_back,
    b_back,
    norm2_gain,
    norm2_shift,
    cotangent,
):
    f32 = jnp.float32
    bf16 = jnp.bfloat16
    attn_parts = (
        lax.all_gather(w_query, ("dp", "ctx"), axis=0, tiled=True),
        lax.all_gather(w_key, ("dp", "ctx"), axis=0, tiled=True),
        lax.all_gather(w_value, ("dp", "ctx"), axis=0, tiled=True),
        lax.all_gather(w_out, ("dp", "ctx"), axis=0, tiled=True),
        lax.all_gather(b_query, ("dp", "ctx"), axis=0, tiled=True),
        lax.all_gather(b_value, ("dp", "ctx"), axis=0, tiled=True),
        lax.all_gather(b_out, ("dp", "ctx"), axis=0, tiled=True),
        lax.all_gather(norm1_gain, ("dp", "ctx"), axis=0, tiled=True),
        lax.all_gather(norm1_shift, ("dp", "ctx"), axis=0, tiled=True),
    )
    wq_full, wk_full, wv_full, wo_full, bq_full, bv_full, bo_full, gain_one, shift_one = attn_parts
    row_count = tokens.shape[0]
    model_width = tokens.shape[1]
    residual = tokens.astype(f32)
    query_rows = (
        jnp.dot(tokens, wq_full, preferred_element_type=f32) + bq_full.astype(f32)
    ).astype(bf16)
    key_rows = jnp.dot(tokens, wk_full, preferred_element_type=f32).astype(bf16)
    value_rows = (
        jnp.dot(tokens, wv_full, preferred_element_type=f32) + bv_full.astype(f32)
    ).astype(bf16)
    query_heads = split_heads(query_rows)
    key_local = split_heads(key_rows)
    value_local = split_heads(value_rows)
    portion = (
        lax.all_gather(key_rows, "ctx", axis=0, tiled=True),
        lax.all_gather(value_rows, "ctx", axis=0, tiled=True),
    )
    key_heads = split_heads(portion[0])
    value_heads = split_heads(portion[1])
    scores = jnp.einsum("qhd,khd->hqk", query_heads, key_heads, preferred_element_type=f32) * 0.125
    weights = jnp.exp(scores)
    summed = jnp.einsum(
        "hqk,khd->qhd", weights.astype(bf16), value_heads, preferred_element_type=f32
    )
    summed_all = summed.reshape(row_count, model_width)
    totals = jnp.sum(weights, axis=-1)
    totals_rows = jnp.transpose(totals)
    mixed_heads = split_heads(summed_all) / totals_rows[:, :, None]
    mixed = mixed_heads.reshape(row_count, model_width)
    mixed_low = mixed.astype(bf16)
    branch_attn = jnp.dot(mixed_low, wo_full, preferred_element_type=f32) + bo_full.astype(f32)
    gain_one32 = gain_one.astype(f32)
    stream_one = residual + branch_attn
    hidden, scaled_one, inverse_one = normalize(stream_one, gain_one32, shift_one.astype(f32))
    ffn_parts = (
        lax.all_gather(w_in, ("dp", "ctx"), axis=0, tiled=True),
        lax.all_gather(w_back, ("dp", "ctx"), axis=0, tiled=True),
        lax.all_gather(b_in, ("dp", "ctx"), axis=0, tiled=True),
        lax.all_gather(b_back, ("dp", "ctx"), axis=0, tiled=True),
        lax.all_gather(norm2_gain, ("dp", "ctx"), axis=0, tiled=True),
        lax.all_gather(norm2_shift, ("dp", "ctx"), axis=0, tiled=True),
    )
    w1_full, w2_full, b1_full, b2_full, gain_two, shift_two = ffn_parts
    hidden_low = hidden.astype(bf16)
    pre_act = jnp.dot(hidden_low, w1_full, preferred_element_type=f32) + b1_full.astype(f32)
    activated, gelu_pull = jax.vjp(partial(jax.nn.gelu, approximate=False), pre_act)
    act_low = activated.astype(bf16)
    branch_ffn = jnp.dot(act_low, w2_full, preferred_element_type=f32) + b2_full.astype(f32)
    gain_two32 = gain_two.astype(f32)
    normed_out, scaled_two, inverse_two = normalize(
        hidden + branch_ffn, gain_two32, shift_two.astype(f32)
    )
    layer_out = normed_out.astype(bf16)
    square_sums = lax.psum(
        (jnp.sum(residual * residual), jnp.sum(stream_one * stream_one)), ("dp", "ctx")
    )
    entries = row_count * model_width * lax.axis_size("dp") * lax.axis_size("ctx")
    rms_values = jnp.sqrt(jnp.stack(square_sums) / entries)
    upstream = cotangent.astype(f32)
    dsum_two, gain_two_grad, shift_two_grad = normalize_back(
        upstream, scaled_two, inverse_two, gain_two32
    )
    ffn_grad = dsum_two.astype(bf16)
    b2_grad = jnp.sum(ffn_grad, axis=0, dtype=f32)
    w2_grad = jnp.einsum("tf,td->fd", act_low, ffn_grad, preferred_element_type=f32)
    act_grad = jnp.einsum("td,fd->tf", ffn_grad, w2_full, preferred_element_type=f32)
    pre_grad = gelu_pull(act_grad)[0].astype(bf16)
    b1_grad = jnp.sum(pre_grad, axis=0, dtype=f32)
    w1_grad = jnp.einsum("td,tf->df", hidden_low, pre_grad, preferred_element_type=f32)
    hidden_grad = dsum_two + jnp.einsum("tf,df->td", pre_grad, w1_full, preferred_element_type=f32)
    dsum_one, gain_one_grad, shift_one_grad = normalize_back(
        hidden_grad, scaled_one, inverse_one, gain_one32
    )
    attn_grad = dsum_one.astype(bf16)
    bo_grad = jnp.sum(attn_grad, axis=0, dtype=f32)
    wo_grad = jnp.einsum("te,td->ed", mixed_low, attn_grad, preferred_element_type=f32)
    mixed_grad = split_heads(
        jnp.einsum("td,ed->te", attn_grad, wo_full, preferred_element_type=f32)
    )
    grad_heads = (mixed_grad / totals_rows[:, :, None]).astype(bf16)
    delta_rows = jnp.sum(mixed_grad * mixed_heads, axis=-1) / totals_rows
    delta_heads = jnp.transpose(delta_rows)
    grad_rows = grad_heads.reshape(row_count, model_width)
    portion = (
        lax.all_gather(key_rows, "ctx", axis=0, tiled=True),
        lax.all_gather(value_rows, "ctx", axis=0, tiled=True),
    )
    key_heads = split_heads(portion[0])
    value_heads = split_heads(portion[1])
    scores = jnp.einsum("qhd,khd->hqk", query_heads, key_heads, preferred_element_type=f32) * 0.125
    weights = jnp.exp(scores)
    across = jnp.einsum("qhd,khd->hqk", grad_heads, value_heads, preferred_element_type=f32)
    slopes = (weights * (across - delta_heads[:, :, None])).astype(bf16)
    part_grad = jnp.einsum("hqk,khd->qhd", slopes, key_heads, preferred_element_type=f32)
    query_acc = part_grad.reshape(row_count, model_width)
    delta_all = lax.all_gather(delta_rows, "ctx", axis=0, tiled=True)
    portion = (
        lax.all_gather(query_rows, "ctx", axis=0, tiled=True),
        lax.all_gather(grad_rows, "ctx", axis=0, tiled=True),
    )
    query_part = split_heads(portion[0])
    grad_part = split_heads(portion[1])
    scores = jnp.einsum("qhd,khd->hqk", query_part, key_local, preferred_element_type=f32) * 0.125
    weights = jnp.exp(scores)
    value_part = jnp.einsum(
        "hqk,qhd->khd", weights.astype(bf16), grad_part, preferred_element_type=f32
    )
    across = jnp.einsum("qhd,khd->hqk", grad_part, value_local, preferred_element_type=f32)
    slopes = (weights * (across - jnp.transpose(delta_all)[:, :, None])).astype(bf16)
    key_part = jnp.einsum("hqk,qhd->khd", slopes, query_part, preferred_element_type=f32)
    key_acc = key_part.reshape(row_count, model_width)
    value_acc = value_part.reshape(row_count, model_width)
    query_grad = (0.125 * query_acc).astype(bf16)
    key_grad = (0.125 * key_acc).astype(bf16)
    value_grad = value_acc.astype(bf16)
    wq_grad = jnp.einsum("td,te->de", tokens, query_grad, preferred_element_type=f32)
    wk_grad = jnp.einsum("td,te->de", tokens, key_grad, preferred_element_type=f32)
    wv_grad = jnp.einsum("td,te->de", tokens, value_grad, preferred_element_type=f32)
    bq_grad = jnp.sum(query_grad, axis=0, dtype=f32)
    bv_grad = jnp.sum(value_grad, axis=0, dtype=f32)
    input_grad = (
        dsum_one
        + jnp.einsum("te,de->td", query_grad, wq_full, preferred_element_type=f32)
        + jnp.einsum("te,de->td", key_grad, wk_full, preferred_element_type=f32)
        + jnp.einsum("te,de->td", value_grad, wv_full, preferred_element_type=f32)
    )
    attn_owned = (
        lax.psum_scatter(wq_grad, ("dp", "ctx"), scatter_dimension=0, tiled=True),
        lax.psum_scatter(wk_grad, ("dp", "ctx"), scatter_dimension=0, tiled=True),
        lax.psum_scatter(wv_grad, ("dp", "ctx"), scatter_dimension=0, tiled=True),
        lax.psum_scatter(wo_grad, ("dp", "ctx"), scatter_dimension=0, tiled=True),
        lax.psum_scatter(bq_grad, ("dp", "ctx"), scatter_dimension=0, tiled=True),
        lax.psum_scatter(bv_grad, ("dp", "ctx"), scatter_dimension=0, tiled=True),
        lax.psum_scatter(bo_grad, ("dp", "ctx"), scatter_dimension=0, tiled=True),
        lax.psum_scatter(gain_one_grad, ("dp", "ctx"), scatter_dimension=0, tiled=True),
        lax.psum_scatter(shift_one_grad, ("dp", "ctx"), scatter_dimension=0, tiled=True),
    )
    ffn_owned = (
        lax.psum_scatter(w1_grad, ("dp", "ctx"), scatter_dimension=0, tiled=True),
        lax.psum_scatter(b1_grad, ("dp", "ctx"), scatter_dimension=0, tiled=True),
        lax.psum_scatter(w2_grad, ("dp", "ctx"), scatter_dimension=0, tiled=True),
        lax.psum_scatter(b2_grad, ("dp", "ctx"), scatter_dimension=0, tiled=True),
        lax.psum_scatter(gain_two_grad, ("dp", "ctx"), scatter_dimension=0, tiled=True),
        lax.psum_scatter(shift_two_grad, ("dp", "ctx"), scatter_dimension=0, tiled=True),
    )
    return (
        layer_out,
        input_grad,
        attn_owned[0],
        attn_owned[1],
        attn_owned[2],
        attn_owned[3],
        attn_owned[4],
        attn_owned[5],
        attn_owned[6],
        attn_owned[7],
        attn_owned[8],
        ffn_owned[0],
        ffn_owned[1],
        ffn_owned[2],
        ffn_owned[3],
        ffn_owned[4],
        ffn_owned[5],
        rms_values,
    )


def solution(mesh):
    rows, flat = P(("dp", "ctx"), None), P(("dp", "ctx"))
    in_specs = (rows,) * 5 + (flat,) * 5 + (rows, flat, rows) + (flat,) * 3 + (rows,)
    out_specs = (rows,) * 6 + (flat,) * 5 + (rows, flat, rows) + (flat,) * 3 + (P(),)
    body = fused if (mesh.shape["dp"], mesh.shape["ctx"]) == (4, 8) else general
    return jax.shard_map(body, mesh=mesh, in_specs=in_specs, out_specs=out_specs, check_vma=False)
```

```python
from functools import partial

import jax
import jax.numpy as jnp
from jax import lax
from jax.experimental import pallas as pl
from jax.experimental.pallas import tpu as pltpu
from jax.sharding import PartitionSpec as P

MESH = pl.DeviceIdType.MESH
f32 = jnp.float32
bf16 = jnp.bfloat16
DH = 64
epsilon = 1e-12
COPIES = 84


def dot(a, b, ca=1, cb=0):
    return lax.dot_general(a, b, (((ca,), (cb,)), ((), ())), preferred_element_type=f32)


def norm_parts(values):
    average = jnp.mean(values, axis=-1, keepdims=True)
    centered = values - average
    spread = jnp.mean(centered * centered, axis=-1, keepdims=True)
    inverse = lax.rsqrt(spread + epsilon)
    return centered * inverse, inverse


def norm_back(incoming, scaled, inverse, gain):
    along = incoming * gain
    return inverse * (
        along
        - jnp.mean(along, axis=-1, keepdims=True)
        - scaled * jnp.mean(along * scaled, axis=-1, keepdims=True)
    )


def wide(*refs):
    total = refs[0].astype(f32)
    for ref in refs[1:]:
        total = total + ref.astype(f32)
    return total


class Copy:
    def __init__(self, parts, whole, goes, comes):
        self.parts, self.whole, self.goes, self.comes, self.waited = parts, whole, goes, comes, False

    def _if(self, condition, act):
        if condition is None:
            act()
        else:
            pl.when(condition)(act)

    def start(self):
        def act():
            for part in self.parts:
                part.start()

        self._if(self.goes, act)

    def landed(self):
        self.waited = True
        self._if(self.comes, self.whole.wait_recv)

    def left(self):
        self._if(self.goes, self.whole.wait_send)


def landed(copies):
    for copy in copies:
        copy.landed()


ORDER = [
    16 * ((b // 8) % 2) + 4 * (2 * (b // 16) + b % 2) + (b % 8) // 2 for b in range(32)
]


def layer_kernel(
    tok, cot, wq, wk, wv, wo, wi, wb, bq, bv, bo, g1, s1, bb, g2, s2, bi,
    lo_out, igr, la, do_out, di_out, db_out, sm_out,
    xr, cr, xg, pa, sa, si, sb, wa_f, wi_f, wb_f, wo_b, wo_f,
    vec32, vecs, vf,
    qs, kv, ee, mt, tot, mxs, mix, po, ro, hid, xh1, iv1, hg, gp, act, ds2, dg, dp, da, dms, dmi,
    dmt, dqt, dkv, kvr, dall, ds1,
    ga, ga_b, ra, s_a, za, fa,
    gi, gi_b, ri, s_i, zi, fi,
    gb, gb_b, rb, s_b, zb, fb,
    go_b, r_o, s_o, p_o, t_o, z_o,
    los, igs, gs0, gsb, gsr, gst, gsm, gsu, gsz,
    ssem, rsem,
):
    d = lax.axis_index("dp")
    k = lax.axis_index("ctx")
    y, c = d // 2, d % 2
    z, x = k // 2, k % 2
    q = 2 * y + x
    r = 8 * d + k

    def dev(xx, yy, cc, zz):
        return (2 * yy + cc, 2 * zz + xx)

    def mate_q(m):
        a, b = m % 2, m // 2
        return 2 * ((y + b) % 2) + (x + a) % 2

    def mate(m):
        a, b = m % 2, m // 2
        return dev((x + a) % 2, (y + b) % 2, c, z)

    def plane(dz):
        return dev(x, y, c, (z + dz) % 4)

    sibling = dev(x, y, 1 - c, z)
    pd, pz = 2 * (z % 2) + z // 2, 2 * c + y
    partner = (pd, 2 * pz + x)
    alone = (pd == d) & (pz == z)
    moves = jnp.logical_not(alone)
    cross = dev(c, y, x, z)
    stays = x == c
    crosses = jnp.logical_not(stays)

    bar = pltpu.get_barrier_semaphore()
    near = [mate(1), mate(2), mate(3), sibling, plane(1), plane(2), plane(3)]
    for other in near:
        pl.semaphore_signal(bar, inc=1, device_id=other, device_id_type=MESH)

    @pl.when(moves)
    def _():
        pl.semaphore_signal(bar, inc=1, device_id=partner, device_id_type=MESH)

    @pl.when(crosses)
    def _():
        pl.semaphore_signal(bar, inc=1, device_id=cross, device_id_type=MESH)

    pl.semaphore_wait(bar, len(near) + 2 - alone.astype(jnp.int32) - stays.astype(jnp.int32))

    sends = []

    def send(*transfers, size=None, goes=None, comes=None):
        i = len(sends)

        def copy_of(src, dst, to):
            return pltpu.make_async_remote_copy(
                src_ref=src, dst_ref=dst, send_sem=ssem.at[i], recv_sem=rsem.at[i],
                device_id=to, device_id_type=MESH,
            )

        parts = [copy_of(*transfer) for transfer in transfers]
        whole = parts[0] if size is None else copy_of(size, size, transfers[0][2])
        copy = Copy(parts, whole, goes, comes)
        copy.start()
        sends.append(copy)
        return copy

    def swap(src, dst, to, here):
        there = jnp.logical_not(here)
        copy = send((src, dst, to), goes=there, comes=there)

        @pl.when(here)
        def _():
            dst[...] = src[...]

        return copy

    def gather(ref):
        return [send((ref.at[q], ref.at[q], mate(m))) for m in (1, 2, 3)]

    def to_mates(src, dst):
        return send(
            *[(src.at[mate_q(m)], dst.at[q], mate(m)) for m in (1, 2, 3)], size=src.at[pl.ds(0, 3)]
        )

    def share(src, dst, others):
        return send(*[(src, dst.at[i], other) for i, other in enumerate(others)], size=dst)

    mates = [mate(1), mate(2), mate(3)]
    planes = [plane(1), plane(2), plane(3)]
    ends = (z == 0) | (z == 3)
    middle = jnp.logical_not(ends)

    def spread(part, size):
        def copy(to, goes, comes):
            return send(*[(ref, ref, to) for ref in part(z)], size=size, goes=goes, comes=comes)

        return [
            copy(plane(2), None, None), copy(plane(1), z < 3, z > 0), copy(plane(3), z > 0, z < 3)
        ]

    def spread_all(part, size):
        return [
            send(*[(ref, ref, to) for ref in part(z)], size=size) for to in planes
        ]

    def spread_on(copies, part, size):
        copies[0].landed()
        to = dev(x, y, c, lax.rem(3 * (z + 3), 4))
        far = lax.rem(z + 2, 4)
        last = send(*[(ref, ref, to) for ref in part(far)], size=size, goes=middle, comes=ends)
        return copies[1:] + [last]

    def collect(low, landing):
        return [
            send((low.at[3 - z], landing.at[3], dev(x, y, c, lax.rem(z + 1 + 2 * (z // 3), 4))),
                 goes=ends, comes=middle),
            send((low.at[lax.rem(z + 1, 4)], landing.at[0], plane(1)), goes=z < 3, comes=z > 0),
            send((low.at[lax.rem(z + 3, 4)], landing.at[1], plane(3)), goes=z > 0, comes=z < 3),
        ]

    def collect_on(copies, low, landing):
        copies[0].landed()
        far = lax.rem(z + 2, 4)

        @pl.when(middle)
        def _():
            low[far] = wide(low[far], landing[3]).astype(bf16)

        return copies[1:] + [send((low.at[far], landing.at[2], plane(2)))]

    @pl.when(z == 0)
    def _():
        for ref in (zi, zb, z_o):
            ref[0] = jnp.zeros_like(ref[0])

    @pl.when(z == 3)
    def _():
        for ref in (zi, zb, z_o):
            ref[1] = jnp.zeros_like(ref[1])

    vec32[...] = jnp.zeros_like(vec32)
    for i, ref in enumerate((bq, bv, bo, g1, s1, bb, g2, s2)):
        vec32[i:i + 1, :24] = ref[...].astype(f32)
    vec32[8:9, :96] = bi[...].astype(f32)
    slot = 16 * c + 4 * q + z
    chip_slots = pl.ds(pl.multiple_of(16 * c + 4 * q, 4), 4)
    core_slots = pl.ds(pl.multiple_of(16 * c, 16), 16)
    vecs[slot] = vec32[...].astype(bf16)
    c_vz = send(
        *[(vecs.at[slot], vecs.at[slot], to) for to in planes], size=vecs.at[pl.ds(0, 3)]
    )
    halves = [slice(0, 64), slice(64, 128)]
    c_tok = [swap(tok.at[rows, :], xr.at[rows, :], partner, alone) for rows in halves]
    for j in range(4):
        cols = slice(192 * j, 192 * j + 192)
        pa[j] = jnp.concatenate([wq[:, cols], wk[:, cols], wv[:, cols]], axis=1)
    sa[q] = pa[q]
    c_sa = to_mates(pa, sa)

    def in_cols(ref, j):
        return ref.at[:, pl.ds(pl.multiple_of(768 * j, 768), 768)]

    si[q] = wi[:, pl.ds(pl.multiple_of(768 * q, 768), 768)]
    c_si = send(
        *[(in_cols(wi, mate_q(m)), si.at[q], mate(m)) for m in (1, 2, 3)], size=si.at[pl.ds(0, 3)]
    )
    c_sb = swap(wb, sb, cross, stays)

    def own_rows(b, zz):
        return pl.ds(pl.multiple_of(384 * b + 192 * c + 48 * zz, 16), 48)

    def core_rows(b, cc):
        return pl.ds(pl.multiple_of(384 * b + 192 * cc, 16), 192)

    def b_rows(b, zz, cc):
        return pl.ds(pl.multiple_of(96 * (2 * zz + cc), 96), 96)

    def bundle(arrived, full):
        for b in range(2):
            full[own_rows(b, z), :] = jnp.concatenate([arrived[2 * b], arrived[2 * b + 1]], axis=0)

    def rows_a(zz):
        return [wa_f.at[own_rows(b, zz), :] for b in range(2)]

    def rows_i(zz):
        return [wi_f.at[own_rows(b, zz), :] for b in range(2)]

    def rows_b(zz):
        return [wb_f.at[b_rows(0, zz, c), :]]

    def rows_o(zz):
        return [wo_b.at[16 * c + 4 * q + zz]]

    size_a, size_i = wa_f.at[pl.ds(0, 96), :], wi_f.at[pl.ds(0, 96), :]

    c_vz.landed()
    gsb[...] = jnp.zeros_like(gsb)
    c_vm = send(
        *[(vecs.at[chip_slots], vecs.at[chip_slots], to) for to in mates],
        size=vecs.at[pl.ds(0, 12)],
    )
    c_sa.landed()
    bundle(sa, wa_f)
    c_za = spread_all(rows_a, size_a)
    c_vm.landed()
    c_vs = send((vecs.at[core_slots], vecs.at[core_slots], sibling))
    wo_b[slot] = wo[...]
    c_zo = spread_all(rows_o, None)
    c_si.landed()
    bundle(si, wi_f)
    c_zi = spread(rows_i, size_i)
    c_sb.landed()
    wb_f[b_rows(0, z, c), :] = sb[...]
    c_zb = spread(rows_b, None)
    c_xg = []
    for h, rows in enumerate(halves):
        c_tok[h].landed()
        xg[q, rows, :] = xr[rows, :]
        c_xg.append([send((xg.at[q, rows, :], xg.at[q, rows, :], to)) for to in mates])

    c_vs.landed()
    every = [vecs[ORDER[b]].astype(f32) for b in range(32)]
    vf[0:8, :] = jnp.concatenate([part[:8, :24] for part in every], axis=1)
    for i in range(4):
        vf[8 + i:9 + i, :] = jnp.concatenate(
            [part[8:9, :96] for part in every[8 * i:8 * i + 8]], axis=1
        )
    vf[12:16, :] = jnp.zeros((4, 768), f32)
    row = lax.broadcasted_iota(jnp.int32, (16, 768), 0)
    b_out, gain1, shift1 = vf[2:3], vf[3:4], vf[4:5]
    b_back, gain2, shift2 = vf[5:6], vf[6:7], vf[7:8]
    turned = pltpu.roll(vf[...], lax.rem(768 - 192 * q, 768), 1)
    b_qkv = jnp.concatenate(
        [turned[0:1, :192], jnp.zeros((1, 192), f32), turned[1:2, :192]], axis=1
    )
    b_in = jnp.sum(jnp.where(row == 8 + q, vf[...], 0.0), axis=0, keepdims=True)
    landed(c_za)
    c_ca = send(
        *[(wa_f.at[core_rows(b, c), :], wa_f.at[core_rows(b, c), :], sibling) for b in range(2)],
        size=wa_f.at[pl.ds(0, 384), :],
    )


    landed(c_zo)
    c_po = send(
        *[(wo_b.at[chip_slots], wo_b.at[chip_slots], to) for to in mates], size=wo_b.at[pl.ds(0, 12)]
    )

    c_ca.landed()
    c_kv = []
    for m in range(4):
        j = mate_q(m)
        if m:
            for copies in c_xg:
                copies[m - 1].landed()
        out = dot(xg[j], wa_f[...]) + b_qkv
        rows = pl.ds(pl.multiple_of(128 * j, 128), 128)
        qs[rows, :] = (out[:, :192].astype(bf16).astype(f32) * 0.125).astype(bf16)
        kv[c, rows, :] = out[:, 192:].astype(bf16)
        c_kv.append(send((kv.at[c, rows, :], kv.at[c, rows, :], sibling)))


    mt[...] = jnp.zeros_like(mt)
    tot[...] = jnp.zeros_like(tot)

    def expo_rows(h, slot, part):
        return slice(1024 * h + 512 * slot + 256 * part, 1024 * h + 512 * slot + 256 * part + 256)

    def forward_chunk(half, slot, part):
        rows = slice(256 * part, 256 * part + 256)
        keys_values = kv[half, rows, :]
        for h in range(3):
            key = keys_values[:, 64 * h:64 * h + 64]
            value = keys_values[:, 192 + 64 * h:256 + 64 * h]
            query = qs[:, 64 * h:64 * h + 64]
            expo = jnp.exp(dot(key, query, 1, 1))
            low = expo.astype(bf16)
            ee[expo_rows(h, slot, part), :] = low
            tot[h:h + 1, :] += jnp.sum(expo, axis=0, keepdims=True)
            mt[64 * h:64 * h + 64, :] += dot(value, low, 0, 0)

    forward_chunk(c, 0, 0)
    forward_chunk(c, 0, 1)
    c_po.landed()
    c_co = send((wo_b.at[core_slots], wo_b.at[core_slots], sibling))
    landed(c_kv)
    forward_chunk(1 - c, 1, 0)
    forward_chunk(1 - c, 1, 1)
    for h in range(3):
        part = slice(64 * h, 64 * h + 64)
        mt[part, :] = mt[part, :] / tot[h:h + 1, :]
    for j in range(4):
        mxs[j] = mt[:, 128 * j:128 * j + 128].astype(bf16)
    mix[q] = mxs[q]
    c_mix = to_mates(mxs, mix)
    c_zi = spread_on(c_zi, rows_i, size_i)

    c_co.landed()
    for b in range(32):
        wo_f[24 * b:24 * b + 24, :] = wo_b[ORDER[b]]
    c_mix.landed()
    mixed = mix[...].reshape(768, 128)
    attn = dot(mixed, wo_f[...], 0, 0) + b_out
    x32 = xr[...].astype(f32)
    stream = x32 + attn
    squares_x = jnp.sum(x32 * x32)
    squares_s = jnp.sum(stream * stream)
    scaled, inverse = norm_parts(stream)
    xh1[...] = scaled
    iv1[...] = jnp.broadcast_to(inverse, iv1.shape)
    hidden = scaled * gain1 + shift1
    hid[...] = hidden
    hg[q] = hidden.astype(bf16)
    c_hg = gather(hg)
    c_zb = spread_on(c_zb, rows_b, None)
    c_cot = swap(cot, cr, partner, alone)

    landed(c_zi)
    c_ci = send(
        *[(wi_f.at[core_rows(b, c), :], wi_f.at[core_rows(b, c), :], sibling) for b in range(2)],
        size=wi_f.at[pl.ds(0, 384), :],
    )
    landed(c_zb)
    c_cb = send(
        *[(wb_f.at[b_rows(0, zz, c), :], wb_f.at[b_rows(0, zz, c), :], sibling) for zz in range(4)],
        size=wb_f.at[pl.ds(0, 384), :],
    )
    c_ci.landed()

    def ffn(j):
        pre = dot(hg[j], wi_f[...]) + b_in
        phi = 0.5 + 0.5 * lax.erf(pre * 0.7071067811865476)
        gp[j] = phi + pre * jnp.exp(-0.5 * pre * pre) * 0.3989422804014327
        act[j] = (pre * phi).astype(bf16)

    def ffn_out(j):
        return dot(act[j], wb_f[...])

    ffn(q)
    c_cb.landed()
    own_part = ffn_out(q)
    c_ffn = []
    for m in (1, 2, 3):
        c_hg[m - 1].landed()
        j = mate_q(m)
        ffn(j)
        po[j] = ffn_out(j).astype(bf16)
        c_ffn.append(send((po.at[j], ro.at[m - 1], mate(m))))
    landed(c_ffn)
    out = own_part + b_back + wide(ro[0], ro[1], ro[2])
    scaled2, inverse2 = norm_parts(hid[...] + out)
    los[...] = (scaled2 * gain2 + shift2).astype(bf16)
    c_cot.landed()
    dy = cr[...].astype(f32)
    gain2_grad = jnp.sum(dy * scaled2, axis=0, keepdims=True)
    shift2_grad = jnp.sum(dy, axis=0, keepdims=True)
    dsum2 = norm_back(dy, scaled2, inverse2, gain2)
    ds2[...] = dsum2
    low = dsum2.astype(bf16)
    dg[q] = low
    back_grad = jnp.sum(low.astype(f32), axis=0, keepdims=True)
    c_dg = gather(dg)
    c_lo = swap(los, lo_out, partner, alone)

    def ffn_back(j):
        dact = dot(dg[j], wb_f[...], 1, 1)
        dp[j] = (dact * gp[j]).astype(bf16)
        return dot(dp[j], wi_f[...], 1, 1)

    own_part = ffn_back(q)
    c_dh = []
    for m in (1, 2, 3):
        c_dg[m - 1].landed()
        j = mate_q(m)
        po[4 + j] = ffn_back(j).astype(bf16)
        c_dh.append(send((po.at[4 + j], ro.at[2 + m], mate(m))))

    def weight_grad(left, right, out, low, rows):
        for i in range(rows // 256):
            cols = slice(256 * i, 256 * i + 256)
            part = dot(left[:, cols], right, 0, 0)
            out[cols, :] = part
            low[cols, :] = part.astype(bf16)

    def flat(ref):
        return ref[...].reshape(512, ref.shape[-1])

    weight_grad(flat(act), flat(dg), gb, gb_b, 768)
    c_rb = send(
        *[(gb_b.at[b_rows(0, zz, 1 - c), :], rb.at[zz], sibling) for zz in range(4)], size=rb
    )
    weight_grad(flat(hg), flat(dp), gi, gi_b, 768)
    c_ri = send(
        *[(gi_b.at[core_rows(b, 1 - c), :], ri.at[b], sibling) for b in range(2)], size=ri
    )
    in_grad = jnp.sum(flat(dp).astype(f32), axis=0, keepdims=True)

    def row_sums(copy, mine, theirs, low, landing):
        copy.landed()
        for zz in range(4):
            low[zz] = wide(mine[b_rows(0, zz, c), :], theirs[zz]).astype(bf16)
        return collect(low, landing)

    def col_sums(copy, mine, theirs, low):
        copy.landed()
        for zz in range(4):
            for b in range(2):
                part = wide(mine[own_rows(b, zz), :], theirs[b, 48 * zz:48 * zz + 48, :])
                low[zz, 48 * b:48 * b + 48, :] = part.astype(bf16)

    c_zgb = row_sums(c_rb, gb, rb, s_b, zb)
    col_sums(c_ri, gi, ri, s_i)
    c_zgi = collect(s_i, zi)

    landed(c_dh)
    dhidden = ds2[...] + own_part + wide(ro[3], ro[4], ro[5])
    gain1_grad = jnp.sum(dhidden * xh1[...], axis=0, keepdims=True)
    shift1_grad = jnp.sum(dhidden, axis=0, keepdims=True)
    dsum1 = norm_back(dhidden, xh1[...], iv1[:, :1], gain1)
    ds1[...] = dsum1
    low = dsum1.astype(bf16)
    da[...] = low
    out_grad = jnp.sum(low.astype(f32), axis=0, keepdims=True)
    dmixed_t = dot(wo_f[...], da[...], 1, 1)
    for j in range(4):
        dms[j] = dmixed_t[192 * j:192 * j + 192].astype(bf16)
    dmi[q] = dms[q]
    c_dm = to_mates(dms, dmi)
    c_zgb = collect_on(c_zgb, s_b, zb)

    part = dot(mix[...].reshape(768, 128), da[...])
    for b in range(32):
        go_b[ORDER[b]] = part[24 * b:24 * b + 24].astype(bf16)
    other_o = pl.ds(pl.multiple_of(16 * (1 - c), 16), 16)
    c_rgo = send((go_b.at[other_o], r_o, sibling))

    c_dm.landed()
    for j in range(4):
        dmt[:, 128 * j:128 * j + 128] = dmi[j].astype(f32)
    dqt[...] = jnp.zeros_like(dqt)
    c_zgi = collect_on(c_zgi, s_i, zi)

    def backward_chunk(half, slot, part):
        rows = slice(256 * part, 256 * part + 256)
        keys_values = kv[half, rows, :]
        dkeys, dvalues = [], []
        for h in range(3):
            span = slice(64 * h, 64 * h + 64)
            key = keys_values[:, span]
            value = keys_values[:, 192 + 64 * h:256 + 64 * h]
            query = qs[:, span]
            over = 1.0 / tot[h:h + 1, :]
            dmixed = dmt[span, :]
            dsummed = (dmixed * over).astype(bf16)
            delta = jnp.sum(dmixed * mt[span, :], axis=0, keepdims=True) * over
            expo = ee[expo_rows(h, slot, part), :]
            across = dot(value, dsummed)
            slopes = (expo.astype(f32) * (across - delta)).astype(bf16)
            dvalues.append(dot(expo, dsummed, 1, 1))
            dkeys.append(dot(slopes, query))
            dqt[span, :] += dot(key, slopes, 0, 0)
        dkv[half, rows, :] = jnp.concatenate(dkeys + dvalues, axis=1)

    backward_chunk(1 - c, 1, 0)
    backward_chunk(1 - c, 1, 1)
    c_dkv = send((dkv.at[1 - c], kvr, sibling))
    c_rgo.landed()
    for i in range(16):
        s_o[i] = wide(go_b[16 * c + i], r_o[i]).astype(bf16)
    c_pgo = send(
        *[(s_o.at[pl.ds(4 * mate_q(m), 4)], p_o.at[m - 1], mate(m)) for m in (1, 2, 3)], size=p_o
    )
    backward_chunk(c, 0, 0)
    backward_chunk(c, 0, 1)
    dall[:, :192] = jnp.transpose(dqt[...] * 0.125).astype(bf16)
    c_dkv.landed()
    dall[:, 192:] = (dkv[c] + kvr[...]).astype(bf16)

    sums = jnp.sum(dall[...].astype(f32), axis=0, keepdims=True)
    rest = jnp.zeros((1, 576), f32)
    head_rows = jnp.concatenate(
        [jnp.concatenate([sums[:, :192], rest], axis=1),
         jnp.concatenate([sums[:, 384:], rest], axis=1),
         jnp.zeros((6, 768), f32)], axis=0,
    )
    gs0[0:8, :] = pltpu.roll(head_rows, 192 * q, 1)
    gs0[2:3, :] = out_grad
    gs0[3:4, :] = gain1_grad
    gs0[4:5, :] = shift1_grad
    gs0[5:6, :] = back_grad
    gs0[6:7, :] = gain2_grad
    gs0[7:8, :] = shift2_grad
    row2 = lax.broadcasted_iota(jnp.int32, (8, 768), 0)
    gs0[8:16, :] = (
        jnp.where(row2 == q, in_grad, 0.0)
        + jnp.where(row2 == 4, squares_x, 0.0)
        + jnp.where(row2 == 5, squares_s, 0.0)
    )
    for b in range(32):
        gsb[ORDER[b], 0:8, 0:24] = gs0[0:8, 24 * b:24 * b + 24]
        at = 96 * (b % 8)
        gsb[ORDER[b], 8:9, 0:96] = gs0[8 + b // 8:9 + b // 8, at:at + 96]
        gsb[ORDER[b], 12:14, :] = gs0[12:14, 0:128]
    other_slots = pl.ds(pl.multiple_of(16 * (1 - c), 16), 16)
    c_gs = send((gsb.at[other_slots], gsr, sibling))
    c_pgo.landed()
    for i in range(4):
        t_o[i] = wide(s_o[4 * q + i], p_o[0, i], p_o[1, i], p_o[2, i]).astype(bf16)
    c_zgo = collect(t_o, z_o)

    weight_grad(flat(xg), dall[...], ga, ga_b, 768)
    c_rga = send(
        *[(ga_b.at[core_rows(b, 1 - c), :], ra.at[b], sibling) for b in range(2)], size=ra
    )
    c_gs.landed()
    for i in range(16):
        gst[i] = gsb[16 * c + i] + gsr[i]
    c_gm = send(
        *[(gst.at[pl.ds(4 * mate_q(m), 4)], gsm.at[m - 1], mate(m)) for m in (1, 2, 3)], size=gsm
    )
    own = pl.ds(pl.multiple_of(128 * q, 128), 128)
    for m in (1, 2, 3):
        j = mate_q(m)
        rows = pl.ds(pl.multiple_of(128 * j, 128), 128)
        po[8 + j] = dot(dall[rows, :], wa_f[...], 1, 1).astype(bf16)
    c_dx = [
        send(
            *[(po.at[8 + mate_q(m), rows, :], ro.at[5 + m, rows, :], mate(m)) for m in (1, 2, 3)],
            size=ro.at[pl.ds(6, 3), rows, :],
        )
        for rows in halves
    ]
    col_sums(c_rga, ga, ra, s_a)
    c_zga = [send((s_a.at[lax.rem(z + 1 + i, 4)], za.at[i], to)) for i, to in enumerate(planes)]
    ds1[...] += dot(dall[own, :], wa_f[...], 1, 1)

    c_gm.landed()
    for i in range(4):
        gsu[i] = gst[4 * q + i] + gsm[0, i] + gsm[1, i] + gsm[2, i]
    c_gsz = send(
        *[(gsu.at[lax.rem(z + 1 + i, 4)], gsz.at[i], to) for i, to in enumerate(planes)], size=gsz
    )
    c_zgo = collect_on(c_zgo, t_o, z_o)

    landed(c_zgb)
    fb[...] = wide(s_b[z], zb[0], zb[1], zb[2]).astype(bf16)
    c_fb = swap(fb, db_out, cross, stays)

    def col_final(copies, low, landing, out):
        landed(copies)
        for i in range(4):
            rows = slice(24 * i, 24 * i + 24)
            out[i] = wide(
                low[z, rows, :], landing[0, rows, :], landing[1, rows, :], landing[2, rows, :]
            ).astype(bf16)

    col_final(c_zgi, s_i, zi, fi)
    c_fi = send(
        *[(fi.at[mate_q(m)], in_cols(di_out, q), mate(m)) for m in (1, 2, 3)],
        size=fi.at[pl.ds(0, 3)],
    )
    di_out[:, pl.ds(pl.multiple_of(768 * q, 768), 768)] = fi[q]

    c_ig = []
    for h, rows in enumerate(halves):
        c_dx[h].landed()
        grad = ds1[rows, :] + wide(ro[6, rows, :], ro[7, rows, :], ro[8, rows, :])
        igs[rows, :] = grad.astype(bf16)
        c_ig.append(swap(igs.at[rows, :], igr.at[rows, :], partner, alone))


    col_final(c_zga, s_a, za, fa)
    la[q] = fa[q]
    c_fa = to_mates(fa, la)

    landed(c_zgo)
    do_out[...] = wide(t_o[z], z_o[0], z_o[1], z_o[2])

    c_gsz.landed()
    sm_out[...] = gsu[z] + gsz[0] + gsz[1] + gsz[2]

    c_lo.landed()
    c_fb.landed()
    c_fi.landed()
    c_fa.landed()
    landed(c_ig)
    assert len(sends) == COPIES, len(sends)
    for copy in sends:
        copy.left()


def finish_kernel(
    lo, ig, la, do, di, db, sm,
    lo_out, ig_out, dq_out, dk_out, dv_out, do_out, bq, bv, bo, g1, s1, di_out, bi, db_out, bb,
    g2, s2, rms_out,
):
    lo_out[...] = lo[...]
    ig_out[...] = ig[...].astype(f32)
    for j in range(4):
        cols = slice(192 * j, 192 * j + 192)
        dq_out[:, cols] = la[j, :, :192].astype(f32)
        dk_out[:, cols] = la[j, :, 192:384].astype(f32)
        dv_out[:, cols] = la[j, :, 384:].astype(f32)
    do_out[...] = do[...]
    di_out[...] = di[...].astype(f32)
    db_out[...] = db[...].astype(f32)
    for i, out in enumerate((bq, bv, bo, g1, s1, bb, g2, s2)):
        out[...] = sm[i:i + 1, :24]
    bi[...] = sm[8:9, :96]
    lane = lax.broadcasted_iota(jnp.int32, (1, 128), 1)
    means = jnp.where(lane == 0, sm[12:13, :], sm[13:14, :]) / (4096 * 768)
    rms_out[...] = jnp.sqrt(means)[:, :2]


def fused(
    tokens, w_query, w_key, w_value, w_out, b_query, b_value, b_out, norm1_gain, norm1_shift,
    w_in, b_in, w_back, b_back, norm2_gain, norm2_shift, cotangent,
):
    vectors = (
        b_query, b_value, b_out, norm1_gain, norm1_shift, b_back, norm2_gain, norm2_shift, b_in
    )
    vm = pl.BlockSpec(memory_space=pltpu.VMEM)

    def v(*shape, t=bf16):
        return pltpu.VMEM(shape, t)

    def s(*shape, t=f32):
        return jax.ShapeDtypeStruct(shape, t)

    scratch = [
        v(128, 768), v(128, 768), v(4, 128, 768), v(4, 24, 576), v(4, 24, 576), v(4, 24, 768),
        v(96, 768), v(768, 576), v(768, 768), v(768, 768), v(32, 24, 768), v(768, 768),
        v(16, 128, t=f32), v(32, 16, 128),
        v(16, 768, t=f32),
        v(512, 192), v(2, 512, 384), v(3072, 512), v(192, 512, t=f32), v(8, 512, t=f32),
        v(4, 192, 128), v(4, 192, 128), v(12, 128, 768), v(9, 128, 768),
        v(128, 768, t=f32), v(128, 768, t=f32), v(128, 128, t=f32), v(4, 128, 768),
        v(4, 128, 768, t=f32), v(4, 128, 768), v(128, 768, t=f32), v(4, 128, 768),
        v(4, 128, 768), v(128, 768), v(4, 192, 128), v(4, 192, 128),
        v(192, 512, t=f32), v(192, 512, t=f32), v(2, 512, 384, t=f32), v(512, 384, t=f32),
        v(512, 576), v(128, 768, t=f32),
        v(768, 576, t=f32), v(768, 576), v(2, 192, 576), v(4, 96, 576), v(4, 96, 576),
        v(4, 24, 576),
        v(768, 768, t=f32), v(768, 768), v(2, 192, 768), v(4, 96, 768), v(4, 96, 768),
        v(4, 24, 768),
        v(768, 768, t=f32), v(768, 768), v(4, 96, 768), v(4, 96, 768), v(4, 96, 768),
        v(96, 768),
        v(32, 24, 768), v(16, 24, 768), v(16, 24, 768), v(3, 4, 24, 768), v(4, 24, 768),
        v(4, 24, 768),
        v(128, 768), v(128, 768), v(16, 768, t=f32), v(32, 16, 128, t=f32),
        v(16, 16, 128, t=f32), v(16, 16, 128, t=f32), v(3, 4, 16, 128, t=f32),
        v(4, 16, 128, t=f32), v(3, 16, 128, t=f32),
        pltpu.SemaphoreType.DMA((COPIES,)), pltpu.SemaphoreType.DMA((COPIES,)),
    ]
    parts = pl.pallas_call(
        layer_kernel,
        out_shape=(
            s(128, 768, t=bf16), s(128, 768, t=bf16), s(4, 24, 576, t=bf16), s(24, 768),
            s(24, 3072, t=bf16), s(96, 768, t=bf16), s(16, 128),
        ),
        in_specs=[vm] * 17,
        out_specs=[vm] * 7,
        scratch_shapes=scratch,
        compiler_params=pltpu.CompilerParams(
            collective_id=0, has_side_effects=True, vmem_limit_bytes=58 << 20
        ),
        name="layer",
    )(
        tokens, cotangent, w_query, w_key, w_value, w_out, w_in, w_back,
        *[vector.reshape(1, -1) for vector in vectors],
    )
    square, small = s(24, 768), s(1, 24)
    outs = pl.pallas_call(
        finish_kernel,
        out_shape=(
            (s(128, 768, t=bf16), s(128, 768)) + (square,) * 4 + (small,) * 5
            + (s(24, 3072), s(1, 96), s(96, 768)) + (small,) * 3 + (s(1, 2),)
        ),
        in_specs=[vm] * 7,
        out_specs=[vm] * 18,
        name="finish",
    )(*parts)
    return tuple(o.reshape(o.shape[1:]) if o.shape[0] == 1 else o for o in outs)


def normalize(values, gain, shift):
    average = jnp.mean(values, axis=-1, keepdims=True)
    centered = values - average
    spread = jnp.mean(centered * centered, axis=-1, keepdims=True)
    inverse = lax.rsqrt(spread + epsilon)
    scaled = centered * inverse
    return (scaled * gain + shift, scaled, inverse)


def normalize_back(incoming, scaled, inverse, gain):
    along = incoming * gain
    inner = (
        along
        - jnp.mean(along, axis=-1, keepdims=True)
        - scaled * jnp.mean(along * scaled, axis=-1, keepdims=True)
    )
    return (inverse * inner, jnp.sum(incoming * scaled, axis=0), jnp.sum(incoming, axis=0))


def split_heads(row_array):
    return row_array.reshape(row_array.shape[0], -1, DH)


def general(
    tokens,
    w_query,
    w_key,
    w_value,
    w_out,
    b_query,
    b_value,
    b_out,
    norm1_gain,
    norm1_shift,
    w_in,
    b_in,
    w_back,
    b_back,
    norm2_gain,
    norm2_shift,
    cotangent,
):
    f32 = jnp.float32
    bf16 = jnp.bfloat16
    attn_parts = (
        lax.all_gather(w_query, ("dp", "ctx"), axis=0, tiled=True),
        lax.all_gather(w_key, ("dp", "ctx"), axis=0, tiled=True),
        lax.all_gather(w_value, ("dp", "ctx"), axis=0, tiled=True),
        lax.all_gather(w_out, ("dp", "ctx"), axis=0, tiled=True),
        lax.all_gather(b_query, ("dp", "ctx"), axis=0, tiled=True),
        lax.all_gather(b_value, ("dp", "ctx"), axis=0, tiled=True),
        lax.all_gather(b_out, ("dp", "ctx"), axis=0, tiled=True),
        lax.all_gather(norm1_gain, ("dp", "ctx"), axis=0, tiled=True),
        lax.all_gather(norm1_shift, ("dp", "ctx"), axis=0, tiled=True),
    )
    wq_full, wk_full, wv_full, wo_full, bq_full, bv_full, bo_full, gain_one, shift_one = attn_parts
    row_count = tokens.shape[0]
    model_width = tokens.shape[1]
    residual = tokens.astype(f32)
    query_rows = (
        jnp.dot(tokens, wq_full, preferred_element_type=f32) + bq_full.astype(f32)
    ).astype(bf16)
    key_rows = jnp.dot(tokens, wk_full, preferred_element_type=f32).astype(bf16)
    value_rows = (
        jnp.dot(tokens, wv_full, preferred_element_type=f32) + bv_full.astype(f32)
    ).astype(bf16)
    query_heads = split_heads(query_rows)
    key_local = split_heads(key_rows)
    value_local = split_heads(value_rows)
    portion = (
        lax.all_gather(key_rows, "ctx", axis=0, tiled=True),
        lax.all_gather(value_rows, "ctx", axis=0, tiled=True),
    )
    key_heads = split_heads(portion[0])
    value_heads = split_heads(portion[1])
    scores = jnp.einsum("qhd,khd->hqk", query_heads, key_heads, preferred_element_type=f32) * 0.125
    weights = jnp.exp(scores)
    summed = jnp.einsum(
        "hqk,khd->qhd", weights.astype(bf16), value_heads, preferred_element_type=f32
    )
    summed_all = summed.reshape(row_count, model_width)
    totals = jnp.sum(weights, axis=-1)
    totals_rows = jnp.transpose(totals)
    mixed_heads = split_heads(summed_all) / totals_rows[:, :, None]
    mixed = mixed_heads.reshape(row_count, model_width)
    mixed_low = mixed.astype(bf16)
    branch_attn = jnp.dot(mixed_low, wo_full, preferred_element_type=f32) + bo_full.astype(f32)
    gain_one32 = gain_one.astype(f32)
    stream_one = residual + branch_attn
    hidden, scaled_one, inverse_one = normalize(stream_one, gain_one32, shift_one.astype(f32))
    ffn_parts = (
        lax.all_gather(w_in, ("dp", "ctx"), axis=0, tiled=True),
        lax.all_gather(w_back, ("dp", "ctx"), axis=0, tiled=True),
        lax.all_gather(b_in, ("dp", "ctx"), axis=0, tiled=True),
        lax.all_gather(b_back, ("dp", "ctx"), axis=0, tiled=True),
        lax.all_gather(norm2_gain, ("dp", "ctx"), axis=0, tiled=True),
        lax.all_gather(norm2_shift, ("dp", "ctx"), axis=0, tiled=True),
    )
    w1_full, w2_full, b1_full, b2_full, gain_two, shift_two = ffn_parts
    hidden_low = hidden.astype(bf16)
    pre_act = jnp.dot(hidden_low, w1_full, preferred_element_type=f32) + b1_full.astype(f32)
    activated, gelu_pull = jax.vjp(partial(jax.nn.gelu, approximate=False), pre_act)
    act_low = activated.astype(bf16)
    branch_ffn = jnp.dot(act_low, w2_full, preferred_element_type=f32) + b2_full.astype(f32)
    gain_two32 = gain_two.astype(f32)
    normed_out, scaled_two, inverse_two = normalize(
        hidden + branch_ffn, gain_two32, shift_two.astype(f32)
    )
    layer_out = normed_out.astype(bf16)
    square_sums = lax.psum(
        (jnp.sum(residual * residual), jnp.sum(stream_one * stream_one)), ("dp", "ctx")
    )
    entries = row_count * model_width * lax.axis_size("dp") * lax.axis_size("ctx")
    rms_values = jnp.sqrt(jnp.stack(square_sums) / entries)
    upstream = cotangent.astype(f32)
    dsum_two, gain_two_grad, shift_two_grad = normalize_back(
        upstream, scaled_two, inverse_two, gain_two32
    )
    ffn_grad = dsum_two.astype(bf16)
    b2_grad = jnp.sum(ffn_grad, axis=0, dtype=f32)
    w2_grad = jnp.einsum("tf,td->fd", act_low, ffn_grad, preferred_element_type=f32)
    act_grad = jnp.einsum("td,fd->tf", ffn_grad, w2_full, preferred_element_type=f32)
    pre_grad = gelu_pull(act_grad)[0].astype(bf16)
    b1_grad = jnp.sum(pre_grad, axis=0, dtype=f32)
    w1_grad = jnp.einsum("td,tf->df", hidden_low, pre_grad, preferred_element_type=f32)
    hidden_grad = dsum_two + jnp.einsum("tf,df->td", pre_grad, w1_full, preferred_element_type=f32)
    dsum_one, gain_one_grad, shift_one_grad = normalize_back(
        hidden_grad, scaled_one, inverse_one, gain_one32
    )
    attn_grad = dsum_one.astype(bf16)
    bo_grad = jnp.sum(attn_grad, axis=0, dtype=f32)
    wo_grad = jnp.einsum("te,td->ed", mixed_low, attn_grad, preferred_element_type=f32)
    mixed_grad = split_heads(
        jnp.einsum("td,ed->te", attn_grad, wo_full, preferred_element_type=f32)
    )
    grad_heads = (mixed_grad / totals_rows[:, :, None]).astype(bf16)
    delta_rows = jnp.sum(mixed_grad * mixed_heads, axis=-1) / totals_rows
    delta_heads = jnp.transpose(delta_rows)
    grad_rows = grad_heads.reshape(row_count, model_width)
    portion = (
        lax.all_gather(key_rows, "ctx", axis=0, tiled=True),
        lax.all_gather(value_rows, "ctx", axis=0, tiled=True),
    )
    key_heads = split_heads(portion[0])
    value_heads = split_heads(portion[1])
    scores = jnp.einsum("qhd,khd->hqk", query_heads, key_heads, preferred_element_type=f32) * 0.125
    weights = jnp.exp(scores)
    across = jnp.einsum("qhd,khd->hqk", grad_heads, value_heads, preferred_element_type=f32)
    slopes = (weights * (across - delta_heads[:, :, None])).astype(bf16)
    part_grad = jnp.einsum("hqk,khd->qhd", slopes, key_heads, preferred_element_type=f32)
    query_acc = part_grad.reshape(row_count, model_width)
    delta_all = lax.all_gather(delta_rows, "ctx", axis=0, tiled=True)
    portion = (
        lax.all_gather(query_rows, "ctx", axis=0, tiled=True),
        lax.all_gather(grad_rows, "ctx", axis=0, tiled=True),
    )
    query_part = split_heads(portion[0])
    grad_part = split_heads(portion[1])
    scores = jnp.einsum("qhd,khd->hqk", query_part, key_local, preferred_element_type=f32) * 0.125
    weights = jnp.exp(scores)
    value_part = jnp.einsum(
        "hqk,qhd->khd", weights.astype(bf16), grad_part, preferred_element_type=f32
    )
    across = jnp.einsum("qhd,khd->hqk", grad_part, value_local, preferred_element_type=f32)
    slopes = (weights * (across - jnp.transpose(delta_all)[:, :, None])).astype(bf16)
    key_part = jnp.einsum("hqk,qhd->khd", slopes, query_part, preferred_element_type=f32)
    key_acc = key_part.reshape(row_count, model_width)
    value_acc = value_part.reshape(row_count, model_width)
    query_grad = (0.125 * query_acc).astype(bf16)
    key_grad = (0.125 * key_acc).astype(bf16)
    value_grad = value_acc.astype(bf16)
    wq_grad = jnp.einsum("td,te->de", tokens, query_grad, preferred_element_type=f32)
    wk_grad = jnp.einsum("td,te->de", tokens, key_grad, preferred_element_type=f32)
    wv_grad = jnp.einsum("td,te->de", tokens, value_grad, preferred_element_type=f32)
    bq_grad = jnp.sum(query_grad, axis=0, dtype=f32)
    bv_grad = jnp.sum(value_grad, axis=0, dtype=f32)
    input_grad = (
        dsum_one
        + jnp.einsum("te,de->td", query_grad, wq_full, preferred_element_type=f32)
        + jnp.einsum("te,de->td", key_grad, wk_full, preferred_element_type=f32)
        + jnp.einsum("te,de->td", value_grad, wv_full, preferred_element_type=f32)
    )
    attn_owned = (
        lax.psum_scatter(wq_grad, ("dp", "ctx"), scatter_dimension=0, tiled=True),
        lax.psum_scatter(wk_grad, ("dp", "ctx"), scatter_dimension=0, tiled=True),
        lax.psum_scatter(wv_grad, ("dp", "ctx"), scatter_dimension=0, tiled=True),
        lax.psum_scatter(wo_grad, ("dp", "ctx"), scatter_dimension=0, tiled=True),
        lax.psum_scatter(bq_grad, ("dp", "ctx"), scatter_dimension=0, tiled=True),
        lax.psum_scatter(bv_grad, ("dp", "ctx"), scatter_dimension=0, tiled=True),
        lax.psum_scatter(bo_grad, ("dp", "ctx"), scatter_dimension=0, tiled=True),
        lax.psum_scatter(gain_one_grad, ("dp", "ctx"), scatter_dimension=0, tiled=True),
        lax.psum_scatter(shift_one_grad, ("dp", "ctx"), scatter_dimension=0, tiled=True),
    )
    ffn_owned = (
        lax.psum_scatter(w1_grad, ("dp", "ctx"), scatter_dimension=0, tiled=True),
        lax.psum_scatter(b1_grad, ("dp", "ctx"), scatter_dimension=0, tiled=True),
        lax.psum_scatter(w2_grad, ("dp", "ctx"), scatter_dimension=0, tiled=True),
        lax.psum_scatter(b2_grad, ("dp", "ctx"), scatter_dimension=0, tiled=True),
        lax.psum_scatter(gain_two_grad, ("dp", "ctx"), scatter_dimension=0, tiled=True),
        lax.psum_scatter(shift_two_grad, ("dp", "ctx"), scatter_dimension=0, tiled=True),
    )
    return (
        layer_out,
        input_grad,
        attn_owned[0],
        attn_owned[1],
        attn_owned[2],
        attn_owned[3],
        attn_owned[4],
        attn_owned[5],
        attn_owned[6],
        attn_owned[7],
        attn_owned[8],
        ffn_owned[0],
        ffn_owned[1],
        ffn_owned[2],
        ffn_owned[3],
        ffn_owned[4],
        ffn_owned[5],
        rms_values,
    )


def solution(mesh):
    rows, flat = P(("dp", "ctx"), None), P(("dp", "ctx"))
    in_specs = (rows,) * 5 + (flat,) * 5 + (rows, flat, rows) + (flat,) * 3 + (rows,)
    out_specs = (rows,) * 6 + (flat,) * 5 + (rows, flat, rows) + (flat,) * 3 + (P(),)
    body = fused if (mesh.shape["dp"], mesh.shape["ctx"]) == (4, 8) else general
    return jax.shard_map(body, mesh=mesh, in_specs=in_specs, out_specs=out_specs, check_vma=False)
```

```python
from functools import partial

import jax
import jax.numpy as jnp
from jax import lax
from jax.experimental import pallas as pl
from jax.experimental.pallas import tpu as pltpu
from jax.sharding import PartitionSpec as P

MESH = pl.DeviceIdType.MESH
f32 = jnp.float32
bf16 = jnp.bfloat16
DH = 64
epsilon = 1e-12
COPIES = 90


def dot(a, b, ca=1, cb=0):
    return lax.dot_general(a, b, (((ca,), (cb,)), ((), ())), preferred_element_type=f32)


def norm_parts(values):
    average = jnp.mean(values, axis=-1, keepdims=True)
    centered = values - average
    spread = jnp.mean(centered * centered, axis=-1, keepdims=True)
    inverse = lax.rsqrt(spread + epsilon)
    return centered * inverse, inverse


def norm_back(incoming, scaled, inverse, gain):
    along = incoming * gain
    return inverse * (
        along
        - jnp.mean(along, axis=-1, keepdims=True)
        - scaled * jnp.mean(along * scaled, axis=-1, keepdims=True)
    )


def wide(*refs):
    total = refs[0].astype(f32)
    for ref in refs[1:]:
        total = total + ref.astype(f32)
    return total


class Copy:
    def __init__(self, parts, whole, goes, comes):
        self.parts, self.whole, self.goes, self.comes, self.waited = parts, whole, goes, comes, False

    def _if(self, condition, act):
        if condition is None:
            act()
        else:
            pl.when(condition)(act)

    def start(self):
        def act():
            for part in self.parts:
                part.start()

        self._if(self.goes, act)

    def landed(self):
        self.waited = True
        self._if(self.comes, self.whole.wait_recv)

    def left(self):
        self._if(self.goes, self.whole.wait_send)


def landed(copies):
    for copy in copies:
        copy.landed()


ORDER = [
    16 * ((b // 8) % 2) + 4 * (2 * (b // 16) + b % 2) + (b % 8) // 2 for b in range(32)
]


def layer_kernel(
    tok, cot, wq, wk, wv, wo, wi, wb, bq, bv, bo, g1, s1, bb, g2, s2, bi,
    lo_out, igr, la, do_out, di_out, db_out, sm_out,
    xr, cr, xg, pa, sa, si, sb, wa_f, wi_f, wb_f, wo_b, wo_f,
    vec32, vecs, vf,
    qs, kv, ee, mt, tot, mix, po, ro, hid, xh1, iv1, hg, gp, act, ds2, dg, dp, da, dms, dmi,
    dmt, dqt, dkv, kvr, dall, ds1,
    ga, ga_b, ra, s_a, za, fa,
    gi, gi_b, ri, s_i, zi, fi,
    gb, gb_b, rb, s_b, zb, fb,
    go_b, r_o, s_o, p_o, t_o, z_o,
    los, igs, gs0, gsb, gsr, gst, gsm, gsu, gsz,
    ssem, rsem,
):
    d = lax.axis_index("dp")
    k = lax.axis_index("ctx")
    y, c = d // 2, d % 2
    z, x = k // 2, k % 2
    q = 2 * y + x
    r = 8 * d + k

    def dev(xx, yy, cc, zz):
        return (2 * yy + cc, 2 * zz + xx)

    def mate_q(m):
        a, b = m % 2, m // 2
        return 2 * ((y + b) % 2) + (x + a) % 2

    def mate(m):
        a, b = m % 2, m // 2
        return dev((x + a) % 2, (y + b) % 2, c, z)

    def plane(dz):
        return dev(x, y, c, (z + dz) % 4)

    sibling = dev(x, y, 1 - c, z)
    pd, pz = 2 * (z % 2) + z // 2, 2 * c + y
    partner = (pd, 2 * pz + x)
    alone = (pd == d) & (pz == z)
    moves = jnp.logical_not(alone)
    cross = dev(c, y, x, z)
    stays = x == c
    crosses = jnp.logical_not(stays)

    bar = pltpu.get_barrier_semaphore()
    near = [mate(1), mate(2), mate(3), sibling, plane(1), plane(2), plane(3)]
    for other in near:
        pl.semaphore_signal(bar, inc=1, device_id=other, device_id_type=MESH)

    @pl.when(moves)
    def _():
        pl.semaphore_signal(bar, inc=1, device_id=partner, device_id_type=MESH)

    @pl.when(crosses)
    def _():
        pl.semaphore_signal(bar, inc=1, device_id=cross, device_id_type=MESH)

    pl.semaphore_wait(bar, len(near) + 2 - alone.astype(jnp.int32) - stays.astype(jnp.int32))

    sends = []

    def send(*transfers, size=None, goes=None, comes=None):
        i = len(sends)

        def copy_of(src, dst, to):
            return pltpu.make_async_remote_copy(
                src_ref=src, dst_ref=dst, send_sem=ssem.at[i], recv_sem=rsem.at[i],
                device_id=to, device_id_type=MESH,
            )

        parts = [copy_of(*transfer) for transfer in transfers]
        whole = parts[0] if size is None else copy_of(size, size, transfers[0][2])
        copy = Copy(parts, whole, goes, comes)
        copy.start()
        sends.append(copy)
        return copy

    def swap(src, dst, to, here):
        there = jnp.logical_not(here)
        copy = send((src, dst, to), goes=there, comes=there)

        @pl.when(here)
        def _():
            dst[...] = src[...]

        return copy

    def gather(part):
        return [
            send((part(q, h), part(q, h), mate(m))) for h, m in ((0, 1), (1, 2), (1, 1), (0, 2))
        ]

    def gather_on(copies, part):
        copies[0].landed()
        first = part(mate_q(1), 0)
        over_y = send((first, first, mate(2)))
        copies[1].landed()
        second = part(mate_q(2), 1)
        over_x = send((second, second, mate(1)))
        return [[copies[2]], [copies[3]], [over_y, over_x]]

    def to_mates(src, dst):
        return send(
            *[(src.at[mate_q(m)], dst.at[q], mate(m)) for m in (1, 2, 3)], size=src.at[pl.ds(0, 3)]
        )

    def share(src, dst, others):
        return send(*[(src, dst.at[i], other) for i, other in enumerate(others)], size=dst)

    mates = [mate(1), mate(2), mate(3)]
    planes = [plane(1), plane(2), plane(3)]
    ends = (z == 0) | (z == 3)
    middle = jnp.logical_not(ends)

    def spread(part, size):
        def copy(to, goes, comes):
            return send(*[(ref, ref, to) for ref in part(z)], size=size, goes=goes, comes=comes)

        return [
            copy(plane(2), None, None), copy(plane(1), z < 3, z > 0), copy(plane(3), z > 0, z < 3)
        ]

    def spread_all(part, size):
        return [
            send(*[(ref, ref, to) for ref in part(z)], size=size) for to in planes
        ]

    def spread_on(copies, part, size):
        copies[0].landed()
        to = dev(x, y, c, lax.rem(3 * (z + 3), 4))
        far = lax.rem(z + 2, 4)
        last = send(*[(ref, ref, to) for ref in part(far)], size=size, goes=middle, comes=ends)
        return copies[1:] + [last]

    def collect(low, landing):
        return [
            send((low.at[3 - z], landing.at[3], dev(x, y, c, lax.rem(z + 1 + 2 * (z // 3), 4))),
                 goes=ends, comes=middle),
            send((low.at[lax.rem(z + 1, 4)], landing.at[0], plane(1)), goes=z < 3, comes=z > 0),
            send((low.at[lax.rem(z + 3, 4)], landing.at[1], plane(3)), goes=z > 0, comes=z < 3),
        ]

    def collect_on(copies, low, landing):
        copies[0].landed()
        far = lax.rem(z + 2, 4)

        @pl.when(middle)
        def _():
            low[far] = wide(low[far], landing[3]).astype(bf16)

        return copies[1:] + [send((low.at[far], landing.at[2], plane(2)))]

    @pl.when(z == 0)
    def _():
        for ref in (zi, zb, z_o):
            ref[0] = jnp.zeros_like(ref[0])

    @pl.when(z == 3)
    def _():
        for ref in (zi, zb, z_o):
            ref[1] = jnp.zeros_like(ref[1])

    vec32[...] = jnp.zeros_like(vec32)
    for i, ref in enumerate((bq, bv, bo, g1, s1, bb, g2, s2)):
        vec32[i:i + 1, :24] = ref[...].astype(f32)
    vec32[8:9, :96] = bi[...].astype(f32)
    slot = 16 * c + 4 * q + z
    chip_slots = pl.ds(pl.multiple_of(16 * c + 4 * q, 4), 4)
    core_slots = pl.ds(pl.multiple_of(16 * c, 16), 16)
    vecs[slot] = vec32[...].astype(bf16)
    c_vz = send(
        *[(vecs.at[slot], vecs.at[slot], to) for to in planes], size=vecs.at[pl.ds(0, 3)]
    )
    halves = [slice(0, 64), slice(64, 128)]
    c_tok = [swap(tok.at[rows, :], xr.at[rows, :], partner, alone) for rows in halves]
    for j in range(4):
        cols = slice(192 * j, 192 * j + 192)
        pa[j] = jnp.concatenate([wq[:, cols], wk[:, cols], wv[:, cols]], axis=1)
    sa[q] = pa[q]
    c_sa = to_mates(pa, sa)

    def in_cols(ref, j):
        return ref.at[:, pl.ds(pl.multiple_of(768 * j, 768), 768)]

    si[q] = wi[:, pl.ds(pl.multiple_of(768 * q, 768), 768)]
    c_si = send(
        *[(in_cols(wi, mate_q(m)), si.at[q], mate(m)) for m in (1, 2, 3)], size=si.at[pl.ds(0, 3)]
    )
    c_sb = swap(wb, sb, cross, stays)

    def own_rows(b, zz):
        return pl.ds(pl.multiple_of(384 * b + 192 * c + 48 * zz, 16), 48)

    def core_rows(b, cc):
        return pl.ds(pl.multiple_of(384 * b + 192 * cc, 16), 192)

    def b_rows(b, zz, cc):
        return pl.ds(pl.multiple_of(96 * (2 * zz + cc), 96), 96)

    def bundle(arrived, full):
        for b in range(2):
            full[own_rows(b, z), :] = jnp.concatenate([arrived[2 * b], arrived[2 * b + 1]], axis=0)

    def rows_a(zz):
        return [wa_f.at[own_rows(b, zz), :] for b in range(2)]

    def rows_i(zz):
        return [wi_f.at[own_rows(b, zz), :] for b in range(2)]

    def rows_b(zz):
        return [wb_f.at[b_rows(0, zz, c), :]]

    def rows_o(zz):
        return [wo_b.at[16 * c + 4 * q + zz]]

    size_a, size_i = wa_f.at[pl.ds(0, 96), :], wi_f.at[pl.ds(0, 96), :]

    c_vz.landed()
    gsb[...] = jnp.zeros_like(gsb)
    c_vm = send(
        *[(vecs.at[chip_slots], vecs.at[chip_slots], to) for to in mates],
        size=vecs.at[pl.ds(0, 12)],
    )
    c_sa.landed()
    bundle(sa, wa_f)
    c_za = spread(rows_a, size_a)
    c_vm.landed()
    c_vs = send((vecs.at[core_slots], vecs.at[core_slots], sibling))

    def part_x(j, h):
        return xg.at[j, halves[h], :]

    c_xg = []
    for h, order in ((0, (1, 2)), (1, (2, 1))):
        c_tok[h].landed()
        xg[q, halves[h], :] = xr[halves[h], :]
        c_xg += [send((part_x(q, h), part_x(q, h), mate(m))) for m in order]
    c_xg = [c_xg[0], c_xg[2], c_xg[3], c_xg[1]]

    c_za = spread_on(c_za, rows_a, size_a)
    wo_b[slot] = wo[...]
    c_zo = spread_all(rows_o, None)
    c_si.landed()
    bundle(si, wi_f)
    c_zi = spread(rows_i, size_i)
    c_sb.landed()
    wb_f[b_rows(0, z, c), :] = sb[...]
    c_zb = spread(rows_b, None)
    c_vs.landed()
    every = [vecs[ORDER[b]].astype(f32) for b in range(32)]
    vf[0:8, :] = jnp.concatenate([part[:8, :24] for part in every], axis=1)
    for i in range(4):
        vf[8 + i:9 + i, :] = jnp.concatenate(
            [part[8:9, :96] for part in every[8 * i:8 * i + 8]], axis=1
        )
    vf[12:16, :] = jnp.zeros((4, 768), f32)
    row = lax.broadcasted_iota(jnp.int32, (16, 768), 0)
    b_out, gain1, shift1 = vf[2:3], vf[3:4], vf[4:5]
    b_back, gain2, shift2 = vf[5:6], vf[6:7], vf[7:8]
    turned = pltpu.roll(vf[...], lax.rem(768 - 192 * q, 768), 1)
    b_qkv = jnp.concatenate(
        [turned[0:1, :192], jnp.zeros((1, 192), f32), turned[1:2, :192]], axis=1
    )
    b_in = jnp.sum(jnp.where(row == 8 + q, vf[...], 0.0), axis=0, keepdims=True)
    c_xg = gather_on(c_xg, part_x)
    landed(c_za)
    c_ca = send(
        *[(wa_f.at[core_rows(b, c), :], wa_f.at[core_rows(b, c), :], sibling) for b in range(2)],
        size=wa_f.at[pl.ds(0, 384), :],
    )


    landed(c_zo)
    c_po = send(
        *[(wo_b.at[chip_slots], wo_b.at[chip_slots], to) for to in mates], size=wo_b.at[pl.ds(0, 12)]
    )

    c_ca.landed()
    c_kv = []
    for m in range(4):
        j = mate_q(m)
        if m:
            landed(c_xg[m - 1])
        out = dot(xg[j], wa_f[...]) + b_qkv
        rows = pl.ds(pl.multiple_of(128 * j, 128), 128)
        qs[rows, :] = (out[:, :192].astype(bf16).astype(f32) * 0.125).astype(bf16)
        kv[c, rows, :] = out[:, 192:].astype(bf16)
        c_kv.append(send((kv.at[c, rows, :], kv.at[c, rows, :], sibling)))


    mt[...] = jnp.zeros_like(mt)
    tot[...] = jnp.zeros_like(tot)

    def expo_rows(h, slot, part):
        return slice(1024 * h + 512 * slot + 256 * part, 1024 * h + 512 * slot + 256 * part + 256)

    def forward_chunk(half, slot, part):
        rows = slice(256 * part, 256 * part + 256)
        keys_values = kv[half, rows, :]
        for h in range(3):
            key = keys_values[:, 64 * h:64 * h + 64]
            value = keys_values[:, 192 + 64 * h:256 + 64 * h]
            query = qs[:, 64 * h:64 * h + 64]
            expo = jnp.exp(dot(key, query, 1, 1))
            low = expo.astype(bf16)
            ee[expo_rows(h, slot, part), :] = low
            tot[h:h + 1, :] += jnp.sum(expo, axis=0, keepdims=True)
            mt[64 * h:64 * h + 64, :] += dot(value, low, 0, 0)

    forward_chunk(c, 0, 0)
    forward_chunk(c, 0, 1)
    c_po.landed()
    c_co = send((wo_b.at[core_slots], wo_b.at[core_slots], sibling))
    landed(c_kv)
    forward_chunk(1 - c, 1, 0)
    forward_chunk(1 - c, 1, 1)
    for h in range(3):
        part = slice(64 * h, 64 * h + 64)
        mt[part, :] = mt[part, :] / tot[h:h + 1, :]
    mix[q] = mt[...].astype(bf16)

    def part_m(j, h):
        return mix.at[j, pl.ds(96 * h, 96), :]

    c_mix = gather(part_m)
    c_zi = spread_on(c_zi, rows_i, size_i)
    c_mix = gather_on(c_mix, part_m)

    c_co.landed()
    for b in range(32):
        wo_f[24 * b:24 * b + 24, :] = wo_b[ORDER[b]]
    c_zb = spread_on(c_zb, rows_b, None)
    landed(c_zi)
    c_ci = send(
        *[(wi_f.at[core_rows(b, c), :], wi_f.at[core_rows(b, c), :], sibling) for b in range(2)],
        size=wi_f.at[pl.ds(0, 384), :],
    )
    for copies in c_mix:
        landed(copies)
    c_cot = swap(cot, cr, partner, alone)
    squares_x = squares_s = 0.0
    for j in range(4):
        mixed = mix[:, :, 128 * j:128 * j + 128].reshape(768, 128)
        x32 = xg[j].astype(f32)
        stream = x32 + dot(mixed, wo_f[...], 0, 0) + b_out
        squares_x += jnp.where(q == j, jnp.sum(x32 * x32), 0.0)
        squares_s += jnp.where(q == j, jnp.sum(stream * stream), 0.0)
        scaled, inverse = norm_parts(stream)
        xh1[j] = scaled
        iv1[j] = jnp.broadcast_to(inverse, (128, 128))
        hidden = scaled * gain1 + shift1
        hid[j] = hidden
        hg[j] = hidden.astype(bf16)

    landed(c_zb)
    c_cb = send(
        *[(wb_f.at[b_rows(0, zz, c), :], wb_f.at[b_rows(0, zz, c), :], sibling) for zz in range(4)],
        size=wb_f.at[pl.ds(0, 384), :],
    )
    c_ci.landed()

    def ffn(j):
        pre = dot(hg[j], wi_f[...]) + b_in
        phi = 0.5 + 0.5 * lax.erf(pre * 0.7071067811865476)
        gp[j] = phi + pre * jnp.exp(-0.5 * pre * pre) * 0.3989422804014327
        act[j] = (pre * phi).astype(bf16)

    def ffn_out(j):
        return dot(act[j], wb_f[...])

    c_ffn = []
    for m in (1, 2, 3):
        j = mate_q(m)
        ffn(j)
        if m == 1:
            c_cb.landed()
        po[j] = ffn_out(j).astype(bf16)
        c_ffn.append(send((po.at[j], ro.at[m - 1], mate(m))))
    ffn(q)
    own_part = ffn_out(q)
    landed(c_ffn)
    out = own_part + b_back + wide(ro[0], ro[1], ro[2])
    scaled2, inverse2 = norm_parts(hid[q] + out)
    los[...] = (scaled2 * gain2 + shift2).astype(bf16)
    c_cot.landed()
    dy = cr[...].astype(f32)
    gain2_grad = jnp.sum(dy * scaled2, axis=0, keepdims=True)
    shift2_grad = jnp.sum(dy, axis=0, keepdims=True)
    dsum2 = norm_back(dy, scaled2, inverse2, gain2)
    ds2[...] = dsum2
    low = dsum2.astype(bf16)
    dg[q] = low
    back_grad = jnp.sum(low.astype(f32), axis=0, keepdims=True)

    def part_g(j, h):
        return dg.at[j, halves[h], :]

    c_dg = gather(part_g)
    c_lo = swap(los, lo_out, partner, alone)

    def ffn_back(j):
        dact = dot(dg[j], wb_f[...], 1, 1)
        dp[j] = (dact * gp[j]).astype(bf16)
        return dot(dp[j], wi_f[...], 1, 1)

    own_part = ffn_back(q)
    c_dg = gather_on(c_dg, part_g)
    c_dh = []
    for m in (1, 2, 3):
        landed(c_dg[m - 1])
        j = mate_q(m)
        po[4 + j] = ffn_back(j).astype(bf16)
        c_dh.append(send((po.at[4 + j], ro.at[2 + m], mate(m))))

    def weight_grad(left, right, out, low, rows):
        for i in range(rows // 256):
            cols = slice(256 * i, 256 * i + 256)
            part = dot(left[:, cols], right, 0, 0)
            out[cols, :] = part
            low[cols, :] = part.astype(bf16)

    def flat(ref):
        return ref[...].reshape(512, ref.shape[-1])

    weight_grad(flat(act), flat(dg), gb, gb_b, 768)
    c_rb = send(
        *[(gb_b.at[b_rows(0, zz, 1 - c), :], rb.at[zz], sibling) for zz in range(4)], size=rb
    )
    weight_grad(flat(hg), flat(dp), gi, gi_b, 768)
    c_ri = send(
        *[(gi_b.at[core_rows(b, 1 - c), :], ri.at[b], sibling) for b in range(2)], size=ri
    )
    in_grad = jnp.sum(flat(dp).astype(f32), axis=0, keepdims=True)

    def row_sums(copy, mine, theirs, low, landing):
        copy.landed()
        for zz in range(4):
            low[zz] = wide(mine[b_rows(0, zz, c), :], theirs[zz]).astype(bf16)
        return collect(low, landing)

    def col_sums(copy, mine, theirs, low):
        copy.landed()
        for zz in range(4):
            for b in range(2):
                part = wide(mine[own_rows(b, zz), :], theirs[b, 48 * zz:48 * zz + 48, :])
                low[zz, 48 * b:48 * b + 48, :] = part.astype(bf16)

    c_zgb = row_sums(c_rb, gb, rb, s_b, zb)
    col_sums(c_ri, gi, ri, s_i)
    c_zgi = collect(s_i, zi)

    landed(c_dh)
    dhidden = ds2[...] + own_part + wide(ro[3], ro[4], ro[5])
    gain1_grad = jnp.sum(dhidden * xh1[q], axis=0, keepdims=True)
    shift1_grad = jnp.sum(dhidden, axis=0, keepdims=True)
    dsum1 = norm_back(dhidden, xh1[q], iv1[q][:, :1], gain1)
    ds1[...] = dsum1
    low = dsum1.astype(bf16)
    da[...] = low
    out_grad = jnp.sum(low.astype(f32), axis=0, keepdims=True)
    dmixed_t = dot(wo_f[...], da[...], 1, 1)
    for j in range(4):
        dms[j] = dmixed_t[192 * j:192 * j + 192].astype(bf16)
    dmi[q] = dms[q]
    c_dm = to_mates(dms, dmi)
    c_zgb = collect_on(c_zgb, s_b, zb)

    own_cols = pl.ds(pl.multiple_of(128 * q, 128), 128)
    part = dot(mix[:, :, own_cols].reshape(768, 128), da[...])
    for b in range(32):
        go_b[ORDER[b]] = part[24 * b:24 * b + 24].astype(bf16)
    other_o = pl.ds(pl.multiple_of(16 * (1 - c), 16), 16)
    c_rgo = send((go_b.at[other_o], r_o, sibling))

    c_dm.landed()
    for j in range(4):
        dmt[:, 128 * j:128 * j + 128] = dmi[j].astype(f32)
    dqt[...] = jnp.zeros_like(dqt)
    c_zgi = collect_on(c_zgi, s_i, zi)

    def backward_chunk(half, slot, part):
        rows = slice(256 * part, 256 * part + 256)
        keys_values = kv[half, rows, :]
        dkeys, dvalues = [], []
        for h in range(3):
            span = slice(64 * h, 64 * h + 64)
            key = keys_values[:, span]
            value = keys_values[:, 192 + 64 * h:256 + 64 * h]
            query = qs[:, span]
            over = 1.0 / tot[h:h + 1, :]
            dmixed = dmt[span, :]
            dsummed = (dmixed * over).astype(bf16)
            delta = jnp.sum(dmixed * mt[span, :], axis=0, keepdims=True) * over
            expo = ee[expo_rows(h, slot, part), :]
            across = dot(value, dsummed)
            slopes = (expo.astype(f32) * (across - delta)).astype(bf16)
            dvalues.append(dot(expo, dsummed, 1, 1))
            dkeys.append(dot(slopes, query))
            dqt[span, :] += dot(key, slopes, 0, 0)
        dkv[half, rows, :] = jnp.concatenate(dkeys + dvalues, axis=1)

    backward_chunk(1 - c, 1, 0)
    backward_chunk(1 - c, 1, 1)
    c_dkv = send((dkv.at[1 - c], kvr, sibling))
    c_rgo.landed()
    for i in range(16):
        s_o[i] = wide(go_b[16 * c + i], r_o[i]).astype(bf16)
    c_pgo = send(
        *[(s_o.at[pl.ds(4 * mate_q(m), 4)], p_o.at[m - 1], mate(m)) for m in (1, 2, 3)], size=p_o
    )
    backward_chunk(c, 0, 0)
    backward_chunk(c, 0, 1)
    dall[:, :192] = jnp.transpose(dqt[...] * 0.125).astype(bf16)
    c_dkv.landed()
    dall[:, 192:] = (dkv[c] + kvr[...]).astype(bf16)

    sums = jnp.sum(dall[...].astype(f32), axis=0, keepdims=True)
    rest = jnp.zeros((1, 576), f32)
    head_rows = jnp.concatenate(
        [jnp.concatenate([sums[:, :192], rest], axis=1),
         jnp.concatenate([sums[:, 384:], rest], axis=1),
         jnp.zeros((6, 768), f32)], axis=0,
    )
    gs0[0:8, :] = pltpu.roll(head_rows, 192 * q, 1)
    gs0[2:3, :] = out_grad
    gs0[3:4, :] = gain1_grad
    gs0[4:5, :] = shift1_grad
    gs0[5:6, :] = back_grad
    gs0[6:7, :] = gain2_grad
    gs0[7:8, :] = shift2_grad
    row2 = lax.broadcasted_iota(jnp.int32, (8, 768), 0)
    gs0[8:16, :] = (
        jnp.where(row2 == q, in_grad, 0.0)
        + jnp.where(row2 == 4, squares_x, 0.0)
        + jnp.where(row2 == 5, squares_s, 0.0)
    )
    for b in range(32):
        gsb[ORDER[b], 0:8, 0:24] = gs0[0:8, 24 * b:24 * b + 24]
        at = 96 * (b % 8)
        gsb[ORDER[b], 8:9, 0:96] = gs0[8 + b // 8:9 + b // 8, at:at + 96]
        gsb[ORDER[b], 12:14, :] = gs0[12:14, 0:128]
    other_slots = pl.ds(pl.multiple_of(16 * (1 - c), 16), 16)
    c_gs = send((gsb.at[other_slots], gsr, sibling))
    c_pgo.landed()
    for i in range(4):
        t_o[i] = wide(s_o[4 * q + i], p_o[0, i], p_o[1, i], p_o[2, i]).astype(bf16)
    c_zgo = collect(t_o, z_o)

    weight_grad(flat(xg), dall[...], ga, ga_b, 768)
    c_rga = send(
        *[(ga_b.at[core_rows(b, 1 - c), :], ra.at[b], sibling) for b in range(2)], size=ra
    )
    c_gs.landed()
    for i in range(16):
        gst[i] = gsb[16 * c + i] + gsr[i]
    c_gm = send(
        *[(gst.at[pl.ds(4 * mate_q(m), 4)], gsm.at[m - 1], mate(m)) for m in (1, 2, 3)], size=gsm
    )
    own = pl.ds(pl.multiple_of(128 * q, 128), 128)
    for m in (1, 2, 3):
        j = mate_q(m)
        rows = pl.ds(pl.multiple_of(128 * j, 128), 128)
        po[8 + j] = dot(dall[rows, :], wa_f[...], 1, 1).astype(bf16)
    c_dx = [
        send(
            *[(po.at[8 + mate_q(m), rows, :], ro.at[5 + m, rows, :], mate(m)) for m in (1, 2, 3)],
            size=ro.at[pl.ds(6, 3), rows, :],
        )
        for rows in halves
    ]
    col_sums(c_rga, ga, ra, s_a)
    c_zga = [send((s_a.at[lax.rem(z + 1 + i, 4)], za.at[i], to)) for i, to in enumerate(planes)]
    ds1[...] += dot(dall[own, :], wa_f[...], 1, 1)

    c_gm.landed()
    for i in range(4):
        gsu[i] = gst[4 * q + i] + gsm[0, i] + gsm[1, i] + gsm[2, i]
    c_gsz = send(
        *[(gsu.at[lax.rem(z + 1 + i, 4)], gsz.at[i], to) for i, to in enumerate(planes)], size=gsz
    )
    c_zgo = collect_on(c_zgo, t_o, z_o)

    landed(c_zgb)
    fb[...] = wide(s_b[z], zb[0], zb[1], zb[2]).astype(bf16)
    c_fb = swap(fb, db_out, cross, stays)

    def col_final(copies, low, landing, out):
        landed(copies)
        for i in range(4):
            rows = slice(24 * i, 24 * i + 24)
            out[i] = wide(
                low[z, rows, :], landing[0, rows, :], landing[1, rows, :], landing[2, rows, :]
            ).astype(bf16)

    col_final(c_zgi, s_i, zi, fi)
    c_fi = send(
        *[(fi.at[mate_q(m)], in_cols(di_out, q), mate(m)) for m in (1, 2, 3)],
        size=fi.at[pl.ds(0, 3)],
    )
    di_out[:, pl.ds(pl.multiple_of(768 * q, 768), 768)] = fi[q]

    c_ig = []
    for h, rows in enumerate(halves):
        c_dx[h].landed()
        grad = ds1[rows, :] + wide(ro[6, rows, :], ro[7, rows, :], ro[8, rows, :])
        igs[rows, :] = grad.astype(bf16)
        c_ig.append(swap(igs.at[rows, :], igr.at[rows, :], partner, alone))


    col_final(c_zga, s_a, za, fa)
    la[q] = fa[q]
    c_fa = to_mates(fa, la)

    landed(c_zgo)
    do_out[...] = wide(t_o[z], z_o[0], z_o[1], z_o[2])

    c_gsz.landed()
    sm_out[...] = gsu[z] + gsz[0] + gsz[1] + gsz[2]

    c_lo.landed()
    c_fb.landed()
    c_fi.landed()
    c_fa.landed()
    landed(c_ig)
    assert len(sends) == COPIES, len(sends)
    for copy in sends:
        copy.left()


def finish_kernel(
    lo, ig, la, do, di, db, sm,
    lo_out, ig_out, dq_out, dk_out, dv_out, do_out, bq, bv, bo, g1, s1, di_out, bi, db_out, bb,
    g2, s2, rms_out,
):
    lo_out[...] = lo[...]
    ig_out[...] = ig[...].astype(f32)
    for j in range(4):
        cols = slice(192 * j, 192 * j + 192)
        dq_out[:, cols] = la[j, :, :192].astype(f32)
        dk_out[:, cols] = la[j, :, 192:384].astype(f32)
        dv_out[:, cols] = la[j, :, 384:].astype(f32)
    do_out[...] = do[...]
    di_out[...] = di[...].astype(f32)
    db_out[...] = db[...].astype(f32)
    for i, out in enumerate((bq, bv, bo, g1, s1, bb, g2, s2)):
        out[...] = sm[i:i + 1, :24]
    bi[...] = sm[8:9, :96]
    lane = lax.broadcasted_iota(jnp.int32, (1, 128), 1)
    means = jnp.where(lane == 0, sm[12:13, :], sm[13:14, :]) / (4096 * 768)
    rms_out[...] = jnp.sqrt(means)[:, :2]


def fused(
    tokens, w_query, w_key, w_value, w_out, b_query, b_value, b_out, norm1_gain, norm1_shift,
    w_in, b_in, w_back, b_back, norm2_gain, norm2_shift, cotangent,
):
    vectors = (
        b_query, b_value, b_out, norm1_gain, norm1_shift, b_back, norm2_gain, norm2_shift, b_in
    )
    vm = pl.BlockSpec(memory_space=pltpu.VMEM)

    def v(*shape, t=bf16):
        return pltpu.VMEM(shape, t)

    def s(*shape, t=f32):
        return jax.ShapeDtypeStruct(shape, t)

    scratch = [
        v(128, 768), v(128, 768), v(4, 128, 768), v(4, 24, 576), v(4, 24, 576), v(4, 24, 768),
        v(96, 768), v(768, 576), v(768, 768), v(768, 768), v(32, 24, 768), v(768, 768),
        v(16, 128, t=f32), v(32, 16, 128),
        v(16, 768, t=f32),
        v(512, 192), v(2, 512, 384), v(3072, 512), v(192, 512, t=f32), v(8, 512, t=f32),
        v(4, 192, 512), v(12, 128, 768), v(9, 128, 768),
        v(4, 128, 768, t=f32), v(4, 128, 768, t=f32), v(4, 128, 128, t=f32), v(4, 128, 768),
        v(4, 128, 768, t=f32), v(4, 128, 768), v(128, 768, t=f32), v(4, 128, 768),
        v(4, 128, 768), v(128, 768), v(4, 192, 128), v(4, 192, 128),
        v(192, 512, t=f32), v(192, 512, t=f32), v(2, 512, 384, t=f32), v(512, 384, t=f32),
        v(512, 576), v(128, 768, t=f32),
        v(768, 576, t=f32), v(768, 576), v(2, 192, 576), v(4, 96, 576), v(4, 96, 576),
        v(4, 24, 576),
        v(768, 768, t=f32), v(768, 768), v(2, 192, 768), v(4, 96, 768), v(4, 96, 768),
        v(4, 24, 768),
        v(768, 768, t=f32), v(768, 768), v(4, 96, 768), v(4, 96, 768), v(4, 96, 768),
        v(96, 768),
        v(32, 24, 768), v(16, 24, 768), v(16, 24, 768), v(3, 4, 24, 768), v(4, 24, 768),
        v(4, 24, 768),
        v(128, 768), v(128, 768), v(16, 768, t=f32), v(32, 16, 128, t=f32),
        v(16, 16, 128, t=f32), v(16, 16, 128, t=f32), v(3, 4, 16, 128, t=f32),
        v(4, 16, 128, t=f32), v(3, 16, 128, t=f32),
        pltpu.SemaphoreType.DMA((COPIES,)), pltpu.SemaphoreType.DMA((COPIES,)),
    ]
    parts = pl.pallas_call(
        layer_kernel,
        out_shape=(
            s(128, 768, t=bf16), s(128, 768, t=bf16), s(4, 24, 576, t=bf16), s(24, 768),
            s(24, 3072, t=bf16), s(96, 768, t=bf16), s(16, 128),
        ),
        in_specs=[vm] * 17,
        out_specs=[vm] * 7,
        scratch_shapes=scratch,
        compiler_params=pltpu.CompilerParams(
            collective_id=0, has_side_effects=True, vmem_limit_bytes=58 << 20
        ),
        name="layer",
    )(
        tokens, cotangent, w_query, w_key, w_value, w_out, w_in, w_back,
        *[vector.reshape(1, -1) for vector in vectors],
    )
    square, small = s(24, 768), s(1, 24)
    outs = pl.pallas_call(
        finish_kernel,
        out_shape=(
            (s(128, 768, t=bf16), s(128, 768)) + (square,) * 4 + (small,) * 5
            + (s(24, 3072), s(1, 96), s(96, 768)) + (small,) * 3 + (s(1, 2),)
        ),
        in_specs=[vm] * 7,
        out_specs=[vm] * 18,
        name="finish",
    )(*parts)
    return tuple(o.reshape(o.shape[1:]) if o.shape[0] == 1 else o for o in outs)


def normalize(values, gain, shift):
    average = jnp.mean(values, axis=-1, keepdims=True)
    centered = values - average
    spread = jnp.mean(centered * centered, axis=-1, keepdims=True)
    inverse = lax.rsqrt(spread + epsilon)
    scaled = centered * inverse
    return (scaled * gain + shift, scaled, inverse)


def normalize_back(incoming, scaled, inverse, gain):
    along = incoming * gain
    inner = (
        along
        - jnp.mean(along, axis=-1, keepdims=True)
        - scaled * jnp.mean(along * scaled, axis=-1, keepdims=True)
    )
    return (inverse * inner, jnp.sum(incoming * scaled, axis=0), jnp.sum(incoming, axis=0))


def split_heads(row_array):
    return row_array.reshape(row_array.shape[0], -1, DH)


def general(
    tokens,
    w_query,
    w_key,
    w_value,
    w_out,
    b_query,
    b_value,
    b_out,
    norm1_gain,
    norm1_shift,
    w_in,
    b_in,
    w_back,
    b_back,
    norm2_gain,
    norm2_shift,
    cotangent,
):
    f32 = jnp.float32
    bf16 = jnp.bfloat16
    attn_parts = (
        lax.all_gather(w_query, ("dp", "ctx"), axis=0, tiled=True),
        lax.all_gather(w_key, ("dp", "ctx"), axis=0, tiled=True),
        lax.all_gather(w_value, ("dp", "ctx"), axis=0, tiled=True),
        lax.all_gather(w_out, ("dp", "ctx"), axis=0, tiled=True),
        lax.all_gather(b_query, ("dp", "ctx"), axis=0, tiled=True),
        lax.all_gather(b_value, ("dp", "ctx"), axis=0, tiled=True),
        lax.all_gather(b_out, ("dp", "ctx"), axis=0, tiled=True),
        lax.all_gather(norm1_gain, ("dp", "ctx"), axis=0, tiled=True),
        lax.all_gather(norm1_shift, ("dp", "ctx"), axis=0, tiled=True),
    )
    wq_full, wk_full, wv_full, wo_full, bq_full, bv_full, bo_full, gain_one, shift_one = attn_parts
    row_count = tokens.shape[0]
    model_width = tokens.shape[1]
    residual = tokens.astype(f32)
    query_rows = (
        jnp.dot(tokens, wq_full, preferred_element_type=f32) + bq_full.astype(f32)
    ).astype(bf16)
    key_rows = jnp.dot(tokens, wk_full, preferred_element_type=f32).astype(bf16)
    value_rows = (
        jnp.dot(tokens, wv_full, preferred_element_type=f32) + bv_full.astype(f32)
    ).astype(bf16)
    query_heads = split_heads(query_rows)
    key_local = split_heads(key_rows)
    value_local = split_heads(value_rows)
    portion = (
        lax.all_gather(key_rows, "ctx", axis=0, tiled=True),
        lax.all_gather(value_rows, "ctx", axis=0, tiled=True),
    )
    key_heads = split_heads(portion[0])
    value_heads = split_heads(portion[1])
    scores = jnp.einsum("qhd,khd->hqk", query_heads, key_heads, preferred_element_type=f32) * 0.125
    weights = jnp.exp(scores)
    summed = jnp.einsum(
        "hqk,khd->qhd", weights.astype(bf16), value_heads, preferred_element_type=f32
    )
    summed_all = summed.reshape(row_count, model_width)
    totals = jnp.sum(weights, axis=-1)
    totals_rows = jnp.transpose(totals)
    mixed_heads = split_heads(summed_all) / totals_rows[:, :, None]
    mixed = mixed_heads.reshape(row_count, model_width)
    mixed_low = mixed.astype(bf16)
    branch_attn = jnp.dot(mixed_low, wo_full, preferred_element_type=f32) + bo_full.astype(f32)
    gain_one32 = gain_one.astype(f32)
    stream_one = residual + branch_attn
    hidden, scaled_one, inverse_one = normalize(stream_one, gain_one32, shift_one.astype(f32))
    ffn_parts = (
        lax.all_gather(w_in, ("dp", "ctx"), axis=0, tiled=True),
        lax.all_gather(w_back, ("dp", "ctx"), axis=0, tiled=True),
        lax.all_gather(b_in, ("dp", "ctx"), axis=0, tiled=True),
        lax.all_gather(b_back, ("dp", "ctx"), axis=0, tiled=True),
        lax.all_gather(norm2_gain, ("dp", "ctx"), axis=0, tiled=True),
        lax.all_gather(norm2_shift, ("dp", "ctx"), axis=0, tiled=True),
    )
    w1_full, w2_full, b1_full, b2_full, gain_two, shift_two = ffn_parts
    hidden_low = hidden.astype(bf16)
    pre_act = jnp.dot(hidden_low, w1_full, preferred_element_type=f32) + b1_full.astype(f32)
    activated, gelu_pull = jax.vjp(partial(jax.nn.gelu, approximate=False), pre_act)
    act_low = activated.astype(bf16)
    branch_ffn = jnp.dot(act_low, w2_full, preferred_element_type=f32) + b2_full.astype(f32)
    gain_two32 = gain_two.astype(f32)
    normed_out, scaled_two, inverse_two = normalize(
        hidden + branch_ffn, gain_two32, shift_two.astype(f32)
    )
    layer_out = normed_out.astype(bf16)
    square_sums = lax.psum(
        (jnp.sum(residual * residual), jnp.sum(stream_one * stream_one)), ("dp", "ctx")
    )
    entries = row_count * model_width * lax.axis_size("dp") * lax.axis_size("ctx")
    rms_values = jnp.sqrt(jnp.stack(square_sums) / entries)
    upstream = cotangent.astype(f32)
    dsum_two, gain_two_grad, shift_two_grad = normalize_back(
        upstream, scaled_two, inverse_two, gain_two32
    )
    ffn_grad = dsum_two.astype(bf16)
    b2_grad = jnp.sum(ffn_grad, axis=0, dtype=f32)
    w2_grad = jnp.einsum("tf,td->fd", act_low, ffn_grad, preferred_element_type=f32)
    act_grad = jnp.einsum("td,fd->tf", ffn_grad, w2_full, preferred_element_type=f32)
    pre_grad = gelu_pull(act_grad)[0].astype(bf16)
    b1_grad = jnp.sum(pre_grad, axis=0, dtype=f32)
    w1_grad = jnp.einsum("td,tf->df", hidden_low, pre_grad, preferred_element_type=f32)
    hidden_grad = dsum_two + jnp.einsum("tf,df->td", pre_grad, w1_full, preferred_element_type=f32)
    dsum_one, gain_one_grad, shift_one_grad = normalize_back(
        hidden_grad, scaled_one, inverse_one, gain_one32
    )
    attn_grad = dsum_one.astype(bf16)
    bo_grad = jnp.sum(attn_grad, axis=0, dtype=f32)
    wo_grad = jnp.einsum("te,td->ed", mixed_low, attn_grad, preferred_element_type=f32)
    mixed_grad = split_heads(
        jnp.einsum("td,ed->te", attn_grad, wo_full, preferred_element_type=f32)
    )
    grad_heads = (mixed_grad / totals_rows[:, :, None]).astype(bf16)
    delta_rows = jnp.sum(mixed_grad * mixed_heads, axis=-1) / totals_rows
    delta_heads = jnp.transpose(delta_rows)
    grad_rows = grad_heads.reshape(row_count, model_width)
    portion = (
        lax.all_gather(key_rows, "ctx", axis=0, tiled=True),
        lax.all_gather(value_rows, "ctx", axis=0, tiled=True),
    )
    key_heads = split_heads(portion[0])
    value_heads = split_heads(portion[1])
    scores = jnp.einsum("qhd,khd->hqk", query_heads, key_heads, preferred_element_type=f32) * 0.125
    weights = jnp.exp(scores)
    across = jnp.einsum("qhd,khd->hqk", grad_heads, value_heads, preferred_element_type=f32)
    slopes = (weights * (across - delta_heads[:, :, None])).astype(bf16)
    part_grad = jnp.einsum("hqk,khd->qhd", slopes, key_heads, preferred_element_type=f32)
    query_acc = part_grad.reshape(row_count, model_width)
    delta_all = lax.all_gather(delta_rows, "ctx", axis=0, tiled=True)
    portion = (
        lax.all_gather(query_rows, "ctx", axis=0, tiled=True),
        lax.all_gather(grad_rows, "ctx", axis=0, tiled=True),
    )
    query_part = split_heads(portion[0])
    grad_part = split_heads(portion[1])
    scores = jnp.einsum("qhd,khd->hqk", query_part, key_local, preferred_element_type=f32) * 0.125
    weights = jnp.exp(scores)
    value_part = jnp.einsum(
        "hqk,qhd->khd", weights.astype(bf16), grad_part, preferred_element_type=f32
    )
    across = jnp.einsum("qhd,khd->hqk", grad_part, value_local, preferred_element_type=f32)
    slopes = (weights * (across - jnp.transpose(delta_all)[:, :, None])).astype(bf16)
    key_part = jnp.einsum("hqk,qhd->khd", slopes, query_part, preferred_element_type=f32)
    key_acc = key_part.reshape(row_count, model_width)
    value_acc = value_part.reshape(row_count, model_width)
    query_grad = (0.125 * query_acc).astype(bf16)
    key_grad = (0.125 * key_acc).astype(bf16)
    value_grad = value_acc.astype(bf16)
    wq_grad = jnp.einsum("td,te->de", tokens, query_grad, preferred_element_type=f32)
    wk_grad = jnp.einsum("td,te->de", tokens, key_grad, preferred_element_type=f32)
    wv_grad = jnp.einsum("td,te->de", tokens, value_grad, preferred_element_type=f32)
    bq_grad = jnp.sum(query_grad, axis=0, dtype=f32)
    bv_grad = jnp.sum(value_grad, axis=0, dtype=f32)
    input_grad = (
        dsum_one
        + jnp.einsum("te,de->td", query_grad, wq_full, preferred_element_type=f32)
        + jnp.einsum("te,de->td", key_grad, wk_full, preferred_element_type=f32)
        + jnp.einsum("te,de->td", value_grad, wv_full, preferred_element_type=f32)
    )
    attn_owned = (
        lax.psum_scatter(wq_grad, ("dp", "ctx"), scatter_dimension=0, tiled=True),
        lax.psum_scatter(wk_grad, ("dp", "ctx"), scatter_dimension=0, tiled=True),
        lax.psum_scatter(wv_grad, ("dp", "ctx"), scatter_dimension=0, tiled=True),
        lax.psum_scatter(wo_grad, ("dp", "ctx"), scatter_dimension=0, tiled=True),
        lax.psum_scatter(bq_grad, ("dp", "ctx"), scatter_dimension=0, tiled=True),
        lax.psum_scatter(bv_grad, ("dp", "ctx"), scatter_dimension=0, tiled=True),
        lax.psum_scatter(bo_grad, ("dp", "ctx"), scatter_dimension=0, tiled=True),
        lax.psum_scatter(gain_one_grad, ("dp", "ctx"), scatter_dimension=0, tiled=True),
        lax.psum_scatter(shift_one_grad, ("dp", "ctx"), scatter_dimension=0, tiled=True),
    )
    ffn_owned = (
        lax.psum_scatter(w1_grad, ("dp", "ctx"), scatter_dimension=0, tiled=True),
        lax.psum_scatter(b1_grad, ("dp", "ctx"), scatter_dimension=0, tiled=True),
        lax.psum_scatter(w2_grad, ("dp", "ctx"), scatter_dimension=0, tiled=True),
        lax.psum_scatter(b2_grad, ("dp", "ctx"), scatter_dimension=0, tiled=True),
        lax.psum_scatter(gain_two_grad, ("dp", "ctx"), scatter_dimension=0, tiled=True),
        lax.psum_scatter(shift_two_grad, ("dp", "ctx"), scatter_dimension=0, tiled=True),
    )
    return (
        layer_out,
        input_grad,
        attn_owned[0],
        attn_owned[1],
        attn_owned[2],
        attn_owned[3],
        attn_owned[4],
        attn_owned[5],
        attn_owned[6],
        attn_owned[7],
        attn_owned[8],
        ffn_owned[0],
        ffn_owned[1],
        ffn_owned[2],
        ffn_owned[3],
        ffn_owned[4],
        ffn_owned[5],
        rms_values,
    )


def solution(mesh):
    rows, flat = P(("dp", "ctx"), None), P(("dp", "ctx"))
    in_specs = (rows,) * 5 + (flat,) * 5 + (rows, flat, rows) + (flat,) * 3 + (rows,)
    out_specs = (rows,) * 6 + (flat,) * 5 + (rows, flat, rows) + (flat,) * 3 + (P(),)
    body = fused if (mesh.shape["dp"], mesh.shape["ctx"]) == (4, 8) else general
    return jax.shard_map(body, mesh=mesh, in_specs=in_specs, out_specs=out_specs, check_vma=False)
```

```python
from functools import partial

import jax
import jax.numpy as jnp
from jax import lax
from jax.experimental import pallas as pl
from jax.experimental.pallas import tpu as pltpu
from jax.sharding import PartitionSpec as P

MESH = pl.DeviceIdType.MESH
f32 = jnp.float32
bf16 = jnp.bfloat16
DH = 64
epsilon = 1e-12
COPIES = 93


def dot(a, b, ca=1, cb=0):
    return lax.dot_general(a, b, (((ca,), (cb,)), ((), ())), preferred_element_type=f32)


def norm_parts(values):
    average = jnp.mean(values, axis=-1, keepdims=True)
    centered = values - average
    spread = jnp.mean(centered * centered, axis=-1, keepdims=True)
    inverse = lax.rsqrt(spread + epsilon)
    return centered * inverse, inverse


def norm_back(incoming, scaled, inverse, gain):
    along = incoming * gain
    return inverse * (
        along
        - jnp.mean(along, axis=-1, keepdims=True)
        - scaled * jnp.mean(along * scaled, axis=-1, keepdims=True)
    )


def wide(*refs):
    total = refs[0].astype(f32)
    for ref in refs[1:]:
        total = total + ref.astype(f32)
    return total


class Copy:
    def __init__(self, parts, whole, goes, comes):
        self.parts, self.whole, self.goes, self.comes, self.waited = parts, whole, goes, comes, False

    def _if(self, condition, act):
        if condition is None:
            act()
        else:
            pl.when(condition)(act)

    def start(self):
        def act():
            for part in self.parts:
                part.start()

        self._if(self.goes, act)

    def landed(self):
        self.waited = True
        self._if(self.comes, self.whole.wait_recv)

    def left(self):
        self._if(self.goes, self.whole.wait_send)


def landed(copies):
    for copy in copies:
        copy.landed()


ORDER = [
    16 * ((b // 8) % 2) + 4 * (2 * (b // 16) + b % 2) + (b % 8) // 2 for b in range(32)
]


def layer_kernel(
    tok, cot, wq, wk, wv, wo, wi, wb, bq, bv, bo, g1, s1, bb, g2, s2, bi,
    lo_out, igr, la, do_out, di_out, db_out, sm_out,
    xr, cr, xg, pa, sa, si, sb, wa_f, wi_f, wb_f, wo_b, wo_f,
    vec32, vecs, vf,
    qs, kv, ee, mt, tot, mix, po, pf, rd, ro, hid, xh1, iv1, hg, gp, act, ds2, dg, dp, da, dms, dmi,
    dmt, dqt, dkv, kvs, kvr, dall, ds1,
    ga, ga_b, ra, s_a, za, fa,
    gi, gi_b, ri, s_i, zi, fi,
    gb, gb_b, rb, s_b, zb, fb,
    go_b, r_o, s_o, p_o, t_o, z_o,
    los, igs, gs0, gsb, gsr, gst, gsm, gsu, gsz,
    ssem, rsem,
):
    d = lax.axis_index("dp")
    k = lax.axis_index("ctx")
    y, c = d // 2, d % 2
    z, x = k // 2, k % 2
    q = 2 * y + x
    r = 8 * d + k

    def dev(xx, yy, cc, zz):
        return (2 * yy + cc, 2 * zz + xx)

    def mate_q(m):
        a, b = m % 2, m // 2
        return 2 * ((y + b) % 2) + (x + a) % 2

    def mate(m):
        a, b = m % 2, m // 2
        return dev((x + a) % 2, (y + b) % 2, c, z)

    def plane(dz):
        return dev(x, y, c, (z + dz) % 4)

    sibling = dev(x, y, 1 - c, z)
    pd, pz = 2 * (z % 2) + z // 2, 2 * c + y
    partner = (pd, 2 * pz + x)
    alone = (pd == d) & (pz == z)
    moves = jnp.logical_not(alone)
    cross = dev(c, y, x, z)
    stays = x == c
    crosses = jnp.logical_not(stays)

    bar = pltpu.get_barrier_semaphore()
    near = [mate(1), mate(2), mate(3), sibling, plane(1), plane(2), plane(3)]
    for other in near:
        pl.semaphore_signal(bar, inc=1, device_id=other, device_id_type=MESH)

    @pl.when(moves)
    def _():
        pl.semaphore_signal(bar, inc=1, device_id=partner, device_id_type=MESH)

    @pl.when(crosses)
    def _():
        pl.semaphore_signal(bar, inc=1, device_id=cross, device_id_type=MESH)

    pl.semaphore_wait(bar, len(near) + 2 - alone.astype(jnp.int32) - stays.astype(jnp.int32))

    sends = []

    def send(*transfers, size=None, goes=None, comes=None):
        i = len(sends)

        def copy_of(src, dst, to):
            return pltpu.make_async_remote_copy(
                src_ref=src, dst_ref=dst, send_sem=ssem.at[i], recv_sem=rsem.at[i],
                device_id=to, device_id_type=MESH,
            )

        parts = [copy_of(*transfer) for transfer in transfers]
        whole = parts[0] if size is None else copy_of(size, size, transfers[0][2])
        copy = Copy(parts, whole, goes, comes)
        copy.start()
        sends.append(copy)
        return copy

    def swap(src, dst, to, here):
        there = jnp.logical_not(here)
        copy = send((src, dst, to), goes=there, comes=there)

        @pl.when(here)
        def _():
            dst[...] = src[...]

        return copy

    def gather(part):
        return [
            send((part(q, h), part(q, h), mate(m))) for h, m in ((0, 1), (1, 2), (1, 1), (0, 2))
        ]

    def gather_on(copies, part):
        copies[0].landed()
        first = part(mate_q(1), 0)
        over_y = send((first, first, mate(2)))
        copies[1].landed()
        second = part(mate_q(2), 1)
        over_x = send((second, second, mate(1)))
        return [[copies[2]], [copies[3]], [over_y, over_x]]

    def to_mates(src, dst):
        return send(
            *[(src.at[mate_q(m)], dst.at[q], mate(m)) for m in (1, 2, 3)], size=src.at[pl.ds(0, 3)]
        )

    def share(src, dst, others):
        return send(*[(src, dst.at[i], other) for i, other in enumerate(others)], size=dst)

    mates = [mate(1), mate(2), mate(3)]
    planes = [plane(1), plane(2), plane(3)]
    ends = (z == 0) | (z == 3)
    middle = jnp.logical_not(ends)

    def spread(part, size):
        def copy(to, goes, comes):
            return send(*[(ref, ref, to) for ref in part(z)], size=size, goes=goes, comes=comes)

        return [
            copy(plane(2), None, None), copy(plane(1), z < 3, z > 0), copy(plane(3), z > 0, z < 3)
        ]

    def spread_all(part, size):
        return [
            send(*[(ref, ref, to) for ref in part(z)], size=size) for to in planes
        ]

    def spread_on(copies, part, size):
        copies[0].landed()
        to = dev(x, y, c, lax.rem(3 * (z + 3), 4))
        far = lax.rem(z + 2, 4)
        last = send(*[(ref, ref, to) for ref in part(far)], size=size, goes=middle, comes=ends)
        return copies[1:] + [last]

    def collect(low, landing):
        return [
            send((low.at[3 - z], landing.at[3], dev(x, y, c, lax.rem(z + 1 + 2 * (z // 3), 4))),
                 goes=ends, comes=middle),
            send((low.at[lax.rem(z + 1, 4)], landing.at[0], plane(1)), goes=z < 3, comes=z > 0),
            send((low.at[lax.rem(z + 3, 4)], landing.at[1], plane(3)), goes=z > 0, comes=z < 3),
        ]

    def collect_on(copies, low, landing):
        copies[0].landed()
        far = lax.rem(z + 2, 4)

        @pl.when(middle)
        def _():
            low[far] = wide(low[far], landing[3]).astype(bf16)

        return copies[1:] + [send((low.at[far], landing.at[2], plane(2)))]

    @pl.when(z == 0)
    def _():
        for ref in (zi, zb, z_o):
            ref[0] = jnp.zeros_like(ref[0])

    @pl.when(z == 3)
    def _():
        for ref in (zi, zb, z_o):
            ref[1] = jnp.zeros_like(ref[1])

    vec32[...] = jnp.zeros_like(vec32)
    for i, ref in enumerate((bq, bv, bo, g1, s1, bb, g2, s2)):
        vec32[i:i + 1, :24] = ref[...].astype(f32)
    vec32[8:9, :96] = bi[...].astype(f32)
    slot = 16 * c + 4 * q + z
    chip_slots = pl.ds(pl.multiple_of(16 * c + 4 * q, 4), 4)
    core_slots = pl.ds(pl.multiple_of(16 * c, 16), 16)
    vecs[slot] = vec32[...].astype(bf16)
    c_vz = send(
        *[(vecs.at[slot], vecs.at[slot], to) for to in planes], size=vecs.at[pl.ds(0, 3)]
    )
    halves = [slice(0, 64), slice(64, 128)]
    c_tok = [swap(tok.at[rows, :], xr.at[rows, :], partner, alone) for rows in halves]
    for j in range(4):
        cols = slice(192 * j, 192 * j + 192)
        pa[j] = jnp.concatenate([wq[:, cols], wk[:, cols], wv[:, cols]], axis=1)
    sa[q] = pa[q]
    c_sa = to_mates(pa, sa)

    def in_cols(ref, j):
        return ref.at[:, pl.ds(pl.multiple_of(768 * j, 768), 768)]

    si[q] = wi[:, pl.ds(pl.multiple_of(768 * q, 768), 768)]
    c_si = send(
        *[(in_cols(wi, mate_q(m)), si.at[q], mate(m)) for m in (1, 2, 3)], size=si.at[pl.ds(0, 3)]
    )
    c_sb = swap(wb, sb, cross, stays)

    def own_rows(b, zz):
        return pl.ds(pl.multiple_of(384 * b + 192 * c + 48 * zz, 16), 48)

    def core_rows(b, cc):
        return pl.ds(pl.multiple_of(384 * b + 192 * cc, 16), 192)

    def b_rows(b, zz, cc):
        return pl.ds(pl.multiple_of(96 * (2 * zz + cc), 96), 96)

    def bundle(arrived, full):
        for b in range(2):
            full[own_rows(b, z), :] = jnp.concatenate([arrived[2 * b], arrived[2 * b + 1]], axis=0)

    def rows_a(zz):
        return [wa_f.at[own_rows(b, zz), :] for b in range(2)]

    def rows_i(zz):
        return [wi_f.at[own_rows(b, zz), :] for b in range(2)]

    def rows_b(zz):
        return [wb_f.at[b_rows(0, zz, c), :]]

    def rows_o(zz):
        return [wo_b.at[16 * c + 4 * q + zz]]

    size_a, size_i = wa_f.at[pl.ds(0, 96), :], wi_f.at[pl.ds(0, 96), :]

    c_vz.landed()
    gsb[...] = jnp.zeros_like(gsb)
    c_vm = send(
        *[(vecs.at[chip_slots], vecs.at[chip_slots], to) for to in mates],
        size=vecs.at[pl.ds(0, 12)],
    )
    c_sa.landed()
    bundle(sa, wa_f)
    c_za = spread(rows_a, size_a)
    c_vm.landed()
    c_vs = send((vecs.at[core_slots], vecs.at[core_slots], sibling))

    def part_x(j, h):
        return xg.at[j, halves[h], :]

    c_xg = []
    for h, order in ((0, (1, 2)), (1, (2, 1))):
        c_tok[h].landed()
        xg[q, halves[h], :] = xr[halves[h], :]
        c_xg += [send((part_x(q, h), part_x(q, h), mate(m))) for m in order]
    c_xg = [c_xg[0], c_xg[2], c_xg[3], c_xg[1]]

    c_za = spread_on(c_za, rows_a, size_a)
    wo_b[slot] = wo[...]
    c_zo = spread_all(rows_o, None)
    c_si.landed()
    bundle(si, wi_f)
    c_zi = spread(rows_i, size_i)
    c_sb.landed()
    wb_f[b_rows(0, z, c), :] = sb[...]
    c_zb = spread(rows_b, None)
    c_vs.landed()
    every = [vecs[ORDER[b]].astype(f32) for b in range(32)]
    vf[0:8, :] = jnp.concatenate([part[:8, :24] for part in every], axis=1)
    for i in range(4):
        vf[8 + i:9 + i, :] = jnp.concatenate(
            [part[8:9, :96] for part in every[8 * i:8 * i + 8]], axis=1
        )
    vf[12:16, :] = jnp.zeros((4, 768), f32)
    row = lax.broadcasted_iota(jnp.int32, (16, 768), 0)
    b_out, gain1, shift1 = vf[2:3], vf[3:4], vf[4:5]
    b_back, gain2, shift2 = vf[5:6], vf[6:7], vf[7:8]
    turned = pltpu.roll(vf[...], lax.rem(768 - 192 * q, 768), 1)
    b_qkv = jnp.concatenate(
        [turned[0:1, :192], jnp.zeros((1, 192), f32), turned[1:2, :192]], axis=1
    )
    b_in = jnp.sum(jnp.where(row == 8 + q, vf[...], 0.0), axis=0, keepdims=True)
    c_xg = gather_on(c_xg, part_x)
    landed(c_za)
    c_ca = send(
        *[(wa_f.at[core_rows(b, c), :], wa_f.at[core_rows(b, c), :], sibling) for b in range(2)],
        size=wa_f.at[pl.ds(0, 384), :],
    )


    landed(c_zo)
    c_po = send(
        *[(wo_b.at[chip_slots], wo_b.at[chip_slots], to) for to in mates], size=wo_b.at[pl.ds(0, 12)]
    )

    c_ca.landed()
    c_kv = []
    for m in range(4):
        j = mate_q(m)
        if m:
            landed(c_xg[m - 1])
        out = dot(xg[j], wa_f[...]) + b_qkv
        rows = pl.ds(pl.multiple_of(128 * j, 128), 128)
        qs[rows, :] = (out[:, :192].astype(bf16).astype(f32) * 0.125).astype(bf16)
        kv[c, rows, :] = out[:, 192:].astype(bf16)
        c_kv.append(send((kv.at[c, rows, :], kv.at[c, rows, :], sibling)))


    mt[...] = jnp.zeros_like(mt)
    tot[...] = jnp.zeros_like(tot)

    def expo_rows(h, slot, part):
        return slice(1024 * h + 512 * slot + 256 * part, 1024 * h + 512 * slot + 256 * part + 256)

    def forward_chunk(half, slot, part):
        rows = slice(256 * part, 256 * part + 256)
        keys_values = kv[half, rows, :]
        for h in range(3):
            key = keys_values[:, 64 * h:64 * h + 64]
            value = keys_values[:, 192 + 64 * h:256 + 64 * h]
            query = qs[:, 64 * h:64 * h + 64]
            expo = jnp.exp(dot(key, query, 1, 1))
            low = expo.astype(bf16)
            ee[expo_rows(h, slot, part), :] = low
            tot[h:h + 1, :] += jnp.sum(expo, axis=0, keepdims=True)
            mt[64 * h:64 * h + 64, :] += dot(value, low, 0, 0)

    forward_chunk(c, 0, 0)
    forward_chunk(c, 0, 1)
    c_po.landed()
    c_co = send((wo_b.at[core_slots], wo_b.at[core_slots], sibling))
    landed(c_kv)
    forward_chunk(1 - c, 1, 0)
    forward_chunk(1 - c, 1, 1)
    for h in range(3):
        part = slice(64 * h, 64 * h + 64)
        mt[part, :] = mt[part, :] / tot[h:h + 1, :]
    mix[q] = mt[...].astype(bf16)

    def part_m(j, h):
        return mix.at[j, pl.ds(96 * h, 96), :]

    c_mix = gather(part_m)
    c_zi = spread_on(c_zi, rows_i, size_i)
    c_mix = gather_on(c_mix, part_m)

    c_co.landed()
    for b in range(32):
        wo_f[24 * b:24 * b + 24, :] = wo_b[ORDER[b]]
    c_zb = spread_on(c_zb, rows_b, None)
    landed(c_zi)
    c_ci = send(
        *[(wi_f.at[core_rows(b, c), :], wi_f.at[core_rows(b, c), :], sibling) for b in range(2)],
        size=wi_f.at[pl.ds(0, 384), :],
    )
    for copies in c_mix:
        landed(copies)
    c_cot = swap(cot, cr, partner, alone)
    squares_x = squares_s = 0.0
    for j in range(4):
        mixed = mix[:, :, 128 * j:128 * j + 128].reshape(768, 128)
        x32 = xg[j].astype(f32)
        stream = x32 + dot(mixed, wo_f[...], 0, 0) + b_out
        squares_x += jnp.where(q == j, jnp.sum(x32 * x32), 0.0)
        squares_s += jnp.where(q == j, jnp.sum(stream * stream), 0.0)
        scaled, inverse = norm_parts(stream)
        xh1[j] = scaled
        iv1[j] = jnp.broadcast_to(inverse, (128, 128))
        hidden = scaled * gain1 + shift1
        hid[j] = hidden
        hg[j] = hidden.astype(bf16)

    landed(c_zb)
    c_cb = send(
        *[(wb_f.at[b_rows(0, zz, c), :], wb_f.at[b_rows(0, zz, c), :], sibling) for zz in range(4)],
        size=wb_f.at[pl.ds(0, 384), :],
    )
    c_ci.landed()

    def ffn(j):
        pre = dot(hg[j], wi_f[...]) + b_in
        phi = 0.5 + 0.5 * lax.erf(pre * 0.7071067811865476)
        gp[j] = phi + pre * jnp.exp(-0.5 * pre * pre) * 0.3989422804014327
        act[j] = (pre * phi).astype(bf16)

    def ffn_out(j):
        return dot(act[j], wb_f[...])

    low_half, high_half = halves
    over_x, over_y, across = mate_q(1), mate_q(2), mate_q(3)
    ffn(across)
    c_cb.landed()
    po[across] = ffn_out(across).astype(bf16)
    c_far = [
        send((po.at[across, low_half, :], rd.at[0], mate(1))),
        send((po.at[across, high_half, :], rd.at[1], mate(2))),
    ]
    ffn(over_x)
    pf[0] = ffn_out(over_x)
    po[over_x, low_half, :] = pf[0, low_half, :].astype(bf16)
    c_ffn = [send((po.at[over_x, low_half, :], ro.at[0, low_half, :], mate(1)))]
    ffn(over_y)
    pf[1] = ffn_out(over_y)
    po[over_y, high_half, :] = pf[1, high_half, :].astype(bf16)
    c_ffn.append(send((po.at[over_y, high_half, :], ro.at[1, high_half, :], mate(2))))
    c_far[1].landed()
    po[over_x, high_half, :] = wide(pf[0, high_half, :], rd[1]).astype(bf16)
    c_ffn.append(send((po.at[over_x, high_half, :], ro.at[0, high_half, :], mate(1))))
    c_far[0].landed()
    po[over_y, low_half, :] = wide(pf[1, low_half, :], rd[0]).astype(bf16)
    c_ffn.append(send((po.at[over_y, low_half, :], ro.at[1, low_half, :], mate(2))))
    ffn(q)
    own_part = ffn_out(q)
    landed(c_ffn)
    out = own_part + b_back + wide(ro[0], ro[1])
    scaled2, inverse2 = norm_parts(hid[q] + out)
    los[...] = (scaled2 * gain2 + shift2).astype(bf16)
    c_cot.landed()
    dy = cr[...].astype(f32)
    gain2_grad = jnp.sum(dy * scaled2, axis=0, keepdims=True)
    shift2_grad = jnp.sum(dy, axis=0, keepdims=True)
    dsum2 = norm_back(dy, scaled2, inverse2, gain2)
    ds2[...] = dsum2
    low = dsum2.astype(bf16)
    dg[q] = low
    back_grad = jnp.sum(low.astype(f32), axis=0, keepdims=True)

    def part_g(j, h):
        return dg.at[j, halves[h], :]

    c_dg = gather(part_g)
    c_lo = swap(los, lo_out, partner, alone)

    def ffn_back(j):
        dact = dot(dg[j], wb_f[...], 1, 1)
        dp[j] = (dact * gp[j]).astype(bf16)
        return dot(dp[j], wi_f[...], 1, 1)

    own_part = ffn_back(q)
    c_dg = gather_on(c_dg, part_g)
    c_dh = []
    for m in (1, 2, 3):
        landed(c_dg[m - 1])
        j = mate_q(m)
        po[4 + j] = ffn_back(j).astype(bf16)
        c_dh.append(send((po.at[4 + j], ro.at[2 + m], mate(m))))

    def weight_grad(left, right, out, low, rows):
        for i in range(rows // 256):
            cols = slice(256 * i, 256 * i + 256)
            part = dot(left[:, cols], right, 0, 0)
            out[cols, :] = part
            low[cols, :] = part.astype(bf16)

    def flat(ref):
        return ref[...].reshape(512, ref.shape[-1])

    weight_grad(flat(act), flat(dg), gb, gb_b, 768)
    c_rb = send(
        *[(gb_b.at[b_rows(0, zz, 1 - c), :], rb.at[zz], sibling) for zz in range(4)], size=rb
    )
    weight_grad(flat(hg), flat(dp), gi, gi_b, 768)
    c_ri = send(
        *[(gi_b.at[core_rows(b, 1 - c), :], ri.at[b], sibling) for b in range(2)], size=ri
    )
    in_grad = jnp.sum(flat(dp).astype(f32), axis=0, keepdims=True)

    def row_sums(copy, mine, theirs, low, landing):
        copy.landed()
        for zz in range(4):
            low[zz] = wide(mine[b_rows(0, zz, c), :], theirs[zz]).astype(bf16)
        return collect(low, landing)

    def col_sums(copy, mine, theirs, low):
        copy.landed()
        for zz in range(4):
            for b in range(2):
                part = wide(mine[own_rows(b, zz), :], theirs[b, 48 * zz:48 * zz + 48, :])
                low[zz, 48 * b:48 * b + 48, :] = part.astype(bf16)

    c_zgb = row_sums(c_rb, gb, rb, s_b, zb)
    col_sums(c_ri, gi, ri, s_i)
    c_zgi = collect(s_i, zi)

    landed(c_dh)
    dhidden = ds2[...] + own_part + wide(ro[3], ro[4], ro[5])
    gain1_grad = jnp.sum(dhidden * xh1[q], axis=0, keepdims=True)
    shift1_grad = jnp.sum(dhidden, axis=0, keepdims=True)
    dsum1 = norm_back(dhidden, xh1[q], iv1[q][:, :1], gain1)
    ds1[...] = dsum1
    low = dsum1.astype(bf16)
    da[...] = low
    out_grad = jnp.sum(low.astype(f32), axis=0, keepdims=True)
    dmixed_t = dot(wo_f[...], da[...], 1, 1)
    for j in range(4):
        dms[j] = dmixed_t[192 * j:192 * j + 192].astype(bf16)
    dmi[q] = dms[q]
    c_dm = to_mates(dms, dmi)
    c_zgb = collect_on(c_zgb, s_b, zb)

    own_cols = pl.ds(pl.multiple_of(128 * q, 128), 128)
    part = dot(mix[:, :, own_cols].reshape(768, 128), da[...])
    for b in range(32):
        go_b[ORDER[b]] = part[24 * b:24 * b + 24].astype(bf16)
    other_o = pl.ds(pl.multiple_of(16 * (1 - c), 16), 16)
    c_rgo = send((go_b.at[other_o], r_o, sibling))

    c_rgo.landed()
    for i in range(16):
        s_o[i] = wide(go_b[16 * c + i], r_o[i]).astype(bf16)
    c_pgo = send(
        *[(s_o.at[pl.ds(4 * mate_q(m), 4)], p_o.at[m - 1], mate(m)) for m in (1, 2, 3)], size=p_o
    )
    c_dm.landed()
    for j in range(4):
        dmt[:, 128 * j:128 * j + 128] = dmi[j].astype(f32)
    dqt[...] = jnp.zeros_like(dqt)
    c_zgi = collect_on(c_zgi, s_i, zi)

    def backward_chunk(half, slot, part):
        rows = slice(256 * part, 256 * part + 256)
        keys_values = kv[half, rows, :]
        dkeys, dvalues = [], []
        for h in range(3):
            span = slice(64 * h, 64 * h + 64)
            key = keys_values[:, span]
            value = keys_values[:, 192 + 64 * h:256 + 64 * h]
            query = qs[:, span]
            over = 1.0 / tot[h:h + 1, :]
            dmixed = dmt[span, :]
            dsummed = (dmixed * over).astype(bf16)
            delta = jnp.sum(dmixed * mt[span, :], axis=0, keepdims=True) * over
            expo = ee[expo_rows(h, slot, part), :]
            across = dot(value, dsummed)
            slopes = (expo.astype(f32) * (across - delta)).astype(bf16)
            dvalues.append(dot(expo, dsummed, 1, 1))
            dkeys.append(dot(slopes, query))
            dqt[span, :] += dot(key, slopes, 0, 0)
        dkv[half, rows, :] = jnp.concatenate(dkeys + dvalues, axis=1)

    backward_chunk(1 - c, 1, 0)
    backward_chunk(1 - c, 1, 1)
    kvs[...] = dkv[1 - c].astype(bf16)
    c_dkv = send((kvs, kvr, sibling))
    backward_chunk(c, 0, 0)
    backward_chunk(c, 0, 1)
    dall[:, :192] = jnp.transpose(dqt[...] * 0.125).astype(bf16)
    c_dkv.landed()
    dall[:, 192:] = wide(dkv[c], kvr[...]).astype(bf16)

    sums = jnp.sum(dall[...].astype(f32), axis=0, keepdims=True)
    rest = jnp.zeros((1, 576), f32)
    head_rows = jnp.concatenate(
        [jnp.concatenate([sums[:, :192], rest], axis=1),
         jnp.concatenate([sums[:, 384:], rest], axis=1),
         jnp.zeros((6, 768), f32)], axis=0,
    )
    gs0[0:8, :] = pltpu.roll(head_rows, 192 * q, 1)
    gs0[2:3, :] = out_grad
    gs0[3:4, :] = gain1_grad
    gs0[4:5, :] = shift1_grad
    gs0[5:6, :] = back_grad
    gs0[6:7, :] = gain2_grad
    gs0[7:8, :] = shift2_grad
    row2 = lax.broadcasted_iota(jnp.int32, (8, 768), 0)
    gs0[8:16, :] = (
        jnp.where(row2 == q, in_grad, 0.0)
        + jnp.where(row2 == 4, squares_x, 0.0)
        + jnp.where(row2 == 5, squares_s, 0.0)
    )
    for b in range(32):
        gsb[ORDER[b], 0:8, 0:24] = gs0[0:8, 24 * b:24 * b + 24]
        at = 96 * (b % 8)
        gsb[ORDER[b], 8:9, 0:96] = gs0[8 + b // 8:9 + b // 8, at:at + 96]
        gsb[ORDER[b], 12:14, :] = gs0[12:14, 0:128]
    other_slots = pl.ds(pl.multiple_of(16 * (1 - c), 16), 16)
    c_gs = send((gsb.at[other_slots], gsr, sibling))
    c_pgo.landed()
    for i in range(4):
        t_o[i] = wide(s_o[4 * q + i], p_o[0, i], p_o[1, i], p_o[2, i]).astype(bf16)
    c_zgo = collect(t_o, z_o)

    weight_grad(flat(xg), dall[...], ga, ga_b, 768)
    c_rga = send(
        *[(ga_b.at[core_rows(b, 1 - c), :], ra.at[b], sibling) for b in range(2)], size=ra
    )
    c_gs.landed()
    for i in range(16):
        gst[i] = gsb[16 * c + i] + gsr[i]
    c_gm = send(
        *[(gst.at[pl.ds(4 * mate_q(m), 4)], gsm.at[m - 1], mate(m)) for m in (1, 2, 3)], size=gsm
    )
    own = pl.ds(pl.multiple_of(128 * q, 128), 128)
    for m in (1, 2, 3):
        j = mate_q(m)
        rows = pl.ds(pl.multiple_of(128 * j, 128), 128)
        po[8 + j] = dot(dall[rows, :], wa_f[...], 1, 1).astype(bf16)
    c_dx = [
        send(
            *[(po.at[8 + mate_q(m), rows, :], ro.at[5 + m, rows, :], mate(m)) for m in (1, 2, 3)],
            size=ro.at[pl.ds(6, 3), rows, :],
        )
        for rows in halves
    ]
    col_sums(c_rga, ga, ra, s_a)
    c_zga = [send((s_a.at[lax.rem(z + 1 + i, 4)], za.at[i], to)) for i, to in enumerate(planes)]
    ds1[...] += dot(dall[own, :], wa_f[...], 1, 1)

    c_gm.landed()
    for i in range(4):
        gsu[i] = gst[4 * q + i] + gsm[0, i] + gsm[1, i] + gsm[2, i]
    c_gsz = send(
        *[(gsu.at[lax.rem(z + 1 + i, 4)], gsz.at[i], to) for i, to in enumerate(planes)], size=gsz
    )
    c_zgo = collect_on(c_zgo, t_o, z_o)

    landed(c_zgb)
    fb[...] = wide(s_b[z], zb[0], zb[1], zb[2]).astype(bf16)
    c_fb = swap(fb, db_out, cross, stays)

    def col_final(copies, low, landing, out):
        landed(copies)
        for i in range(4):
            rows = slice(24 * i, 24 * i + 24)
            out[i] = wide(
                low[z, rows, :], landing[0, rows, :], landing[1, rows, :], landing[2, rows, :]
            ).astype(bf16)

    col_final(c_zgi, s_i, zi, fi)
    c_fi = send(
        *[(fi.at[mate_q(m)], in_cols(di_out, q), mate(m)) for m in (1, 2, 3)],
        size=fi.at[pl.ds(0, 3)],
    )
    di_out[:, pl.ds(pl.multiple_of(768 * q, 768), 768)] = fi[q]

    c_ig = []
    for h, rows in enumerate(halves):
        c_dx[h].landed()
        grad = ds1[rows, :] + wide(ro[6, rows, :], ro[7, rows, :], ro[8, rows, :])
        igs[rows, :] = grad.astype(bf16)
        c_ig.append(swap(igs.at[rows, :], igr.at[rows, :], partner, alone))


    col_final(c_zga, s_a, za, fa)
    la[q] = fa[q]
    c_fa = to_mates(fa, la)

    landed(c_zgo)
    do_out[...] = wide(t_o[z], z_o[0], z_o[1], z_o[2])

    c_gsz.landed()
    sm_out[...] = gsu[z] + gsz[0] + gsz[1] + gsz[2]

    c_lo.landed()
    c_fb.landed()
    c_fi.landed()
    c_fa.landed()
    landed(c_ig)
    assert len(sends) == COPIES, len(sends)
    for copy in sends:
        copy.left()


def finish_kernel(
    lo, ig, la, do, di, db, sm,
    lo_out, ig_out, dq_out, dk_out, dv_out, do_out, bq, bv, bo, g1, s1, di_out, bi, db_out, bb,
    g2, s2, rms_out,
):
    lo_out[...] = lo[...]
    ig_out[...] = ig[...].astype(f32)
    for j in range(4):
        cols = slice(192 * j, 192 * j + 192)
        dq_out[:, cols] = la[j, :, :192].astype(f32)
        dk_out[:, cols] = la[j, :, 192:384].astype(f32)
        dv_out[:, cols] = la[j, :, 384:].astype(f32)
    do_out[...] = do[...]
    di_out[...] = di[...].astype(f32)
    db_out[...] = db[...].astype(f32)
    for i, out in enumerate((bq, bv, bo, g1, s1, bb, g2, s2)):
        out[...] = sm[i:i + 1, :24]
    bi[...] = sm[8:9, :96]
    lane = lax.broadcasted_iota(jnp.int32, (1, 128), 1)
    means = jnp.where(lane == 0, sm[12:13, :], sm[13:14, :]) / (4096 * 768)
    rms_out[...] = jnp.sqrt(means)[:, :2]


def fused(
    tokens, w_query, w_key, w_value, w_out, b_query, b_value, b_out, norm1_gain, norm1_shift,
    w_in, b_in, w_back, b_back, norm2_gain, norm2_shift, cotangent,
):
    vectors = (
        b_query, b_value, b_out, norm1_gain, norm1_shift, b_back, norm2_gain, norm2_shift, b_in
    )
    vm = pl.BlockSpec(memory_space=pltpu.VMEM)

    def v(*shape, t=bf16):
        return pltpu.VMEM(shape, t)

    def s(*shape, t=f32):
        return jax.ShapeDtypeStruct(shape, t)

    scratch = [
        v(128, 768), v(128, 768), v(4, 128, 768), v(4, 24, 576), v(4, 24, 576), v(4, 24, 768),
        v(96, 768), v(768, 576), v(768, 768), v(768, 768), v(32, 24, 768), v(768, 768),
        v(16, 128, t=f32), v(32, 16, 128),
        v(16, 768, t=f32),
        v(512, 192), v(2, 512, 384), v(3072, 512), v(192, 512, t=f32), v(8, 512, t=f32),
        v(4, 192, 512), v(12, 128, 768), v(2, 128, 768, t=f32), v(2, 64, 768), v(9, 128, 768),
        v(4, 128, 768, t=f32), v(4, 128, 768, t=f32), v(4, 128, 128, t=f32), v(4, 128, 768),
        v(4, 128, 768, t=f32), v(4, 128, 768), v(128, 768, t=f32), v(4, 128, 768),
        v(4, 128, 768), v(128, 768), v(4, 192, 128), v(4, 192, 128),
        v(192, 512, t=f32), v(192, 512, t=f32), v(2, 512, 384, t=f32), v(512, 384), v(512, 384),
        v(512, 576), v(128, 768, t=f32),
        v(768, 576, t=f32), v(768, 576), v(2, 192, 576), v(4, 96, 576), v(4, 96, 576),
        v(4, 24, 576),
        v(768, 768, t=f32), v(768, 768), v(2, 192, 768), v(4, 96, 768), v(4, 96, 768),
        v(4, 24, 768),
        v(768, 768, t=f32), v(768, 768), v(4, 96, 768), v(4, 96, 768), v(4, 96, 768),
        v(96, 768),
        v(32, 24, 768), v(16, 24, 768), v(16, 24, 768), v(3, 4, 24, 768), v(4, 24, 768),
        v(4, 24, 768),
        v(128, 768), v(128, 768), v(16, 768, t=f32), v(32, 16, 128, t=f32),
        v(16, 16, 128, t=f32), v(16, 16, 128, t=f32), v(3, 4, 16, 128, t=f32),
        v(4, 16, 128, t=f32), v(3, 16, 128, t=f32),
        pltpu.SemaphoreType.DMA((COPIES,)), pltpu.SemaphoreType.DMA((COPIES,)),
    ]
    parts = pl.pallas_call(
        layer_kernel,
        out_shape=(
            s(128, 768, t=bf16), s(128, 768, t=bf16), s(4, 24, 576, t=bf16), s(24, 768),
            s(24, 3072, t=bf16), s(96, 768, t=bf16), s(16, 128),
        ),
        in_specs=[vm] * 17,
        out_specs=[vm] * 7,
        scratch_shapes=scratch,
        compiler_params=pltpu.CompilerParams(
            collective_id=0, has_side_effects=True, vmem_limit_bytes=58 << 20
        ),
        name="layer",
    )(
        tokens, cotangent, w_query, w_key, w_value, w_out, w_in, w_back,
        *[vector.reshape(1, -1) for vector in vectors],
    )
    square, small = s(24, 768), s(1, 24)
    outs = pl.pallas_call(
        finish_kernel,
        out_shape=(
            (s(128, 768, t=bf16), s(128, 768)) + (square,) * 4 + (small,) * 5
            + (s(24, 3072), s(1, 96), s(96, 768)) + (small,) * 3 + (s(1, 2),)
        ),
        in_specs=[vm] * 7,
        out_specs=[vm] * 18,
        name="finish",
    )(*parts)
    return tuple(o.reshape(o.shape[1:]) if o.shape[0] == 1 else o for o in outs)


def normalize(values, gain, shift):
    average = jnp.mean(values, axis=-1, keepdims=True)
    centered = values - average
    spread = jnp.mean(centered * centered, axis=-1, keepdims=True)
    inverse = lax.rsqrt(spread + epsilon)
    scaled = centered * inverse
    return (scaled * gain + shift, scaled, inverse)


def normalize_back(incoming, scaled, inverse, gain):
    along = incoming * gain
    inner = (
        along
        - jnp.mean(along, axis=-1, keepdims=True)
        - scaled * jnp.mean(along * scaled, axis=-1, keepdims=True)
    )
    return (inverse * inner, jnp.sum(incoming * scaled, axis=0), jnp.sum(incoming, axis=0))


def split_heads(row_array):
    return row_array.reshape(row_array.shape[0], -1, DH)


def general(
    tokens,
    w_query,
    w_key,
    w_value,
    w_out,
    b_query,
    b_value,
    b_out,
    norm1_gain,
    norm1_shift,
    w_in,
    b_in,
    w_back,
    b_back,
    norm2_gain,
    norm2_shift,
    cotangent,
):
    f32 = jnp.float32
    bf16 = jnp.bfloat16
    attn_parts = (
        lax.all_gather(w_query, ("dp", "ctx"), axis=0, tiled=True),
        lax.all_gather(w_key, ("dp", "ctx"), axis=0, tiled=True),
        lax.all_gather(w_value, ("dp", "ctx"), axis=0, tiled=True),
        lax.all_gather(w_out, ("dp", "ctx"), axis=0, tiled=True),
        lax.all_gather(b_query, ("dp", "ctx"), axis=0, tiled=True),
        lax.all_gather(b_value, ("dp", "ctx"), axis=0, tiled=True),
        lax.all_gather(b_out, ("dp", "ctx"), axis=0, tiled=True),
        lax.all_gather(norm1_gain, ("dp", "ctx"), axis=0, tiled=True),
        lax.all_gather(norm1_shift, ("dp", "ctx"), axis=0, tiled=True),
    )
    wq_full, wk_full, wv_full, wo_full, bq_full, bv_full, bo_full, gain_one, shift_one = attn_parts
    row_count = tokens.shape[0]
    model_width = tokens.shape[1]
    residual = tokens.astype(f32)
    query_rows = (
        jnp.dot(tokens, wq_full, preferred_element_type=f32) + bq_full.astype(f32)
    ).astype(bf16)
    key_rows = jnp.dot(tokens, wk_full, preferred_element_type=f32).astype(bf16)
    value_rows = (
        jnp.dot(tokens, wv_full, preferred_element_type=f32) + bv_full.astype(f32)
    ).astype(bf16)
    query_heads = split_heads(query_rows)
    key_local = split_heads(key_rows)
    value_local = split_heads(value_rows)
    portion = (
        lax.all_gather(key_rows, "ctx", axis=0, tiled=True),
        lax.all_gather(value_rows, "ctx", axis=0, tiled=True),
    )
    key_heads = split_heads(portion[0])
    value_heads = split_heads(portion[1])
    scores = jnp.einsum("qhd,khd->hqk", query_heads, key_heads, preferred_element_type=f32) * 0.125
    weights = jnp.exp(scores)
    summed = jnp.einsum(
        "hqk,khd->qhd", weights.astype(bf16), value_heads, preferred_element_type=f32
    )
    summed_all = summed.reshape(row_count, model_width)
    totals = jnp.sum(weights, axis=-1)
    totals_rows = jnp.transpose(totals)
    mixed_heads = split_heads(summed_all) / totals_rows[:, :, None]
    mixed = mixed_heads.reshape(row_count, model_width)
    mixed_low = mixed.astype(bf16)
    branch_attn = jnp.dot(mixed_low, wo_full, preferred_element_type=f32) + bo_full.astype(f32)
    gain_one32 = gain_one.astype(f32)
    stream_one = residual + branch_attn
    hidden, scaled_one, inverse_one = normalize(stream_one, gain_one32, shift_one.astype(f32))
    ffn_parts = (
        lax.all_gather(w_in, ("dp", "ctx"), axis=0, tiled=True),
        lax.all_gather(w_back, ("dp", "ctx"), axis=0, tiled=True),
        lax.all_gather(b_in, ("dp", "ctx"), axis=0, tiled=True),
        lax.all_gather(b_back, ("dp", "ctx"), axis=0, tiled=True),
        lax.all_gather(norm2_gain, ("dp", "ctx"), axis=0, tiled=True),
        lax.all_gather(norm2_shift, ("dp", "ctx"), axis=0, tiled=True),
    )
    w1_full, w2_full, b1_full, b2_full, gain_two, shift_two = ffn_parts
    hidden_low = hidden.astype(bf16)
    pre_act = jnp.dot(hidden_low, w1_full, preferred_element_type=f32) + b1_full.astype(f32)
    activated, gelu_pull = jax.vjp(partial(jax.nn.gelu, approximate=False), pre_act)
    act_low = activated.astype(bf16)
    branch_ffn = jnp.dot(act_low, w2_full, preferred_element_type=f32) + b2_full.astype(f32)
    gain_two32 = gain_two.astype(f32)
    normed_out, scaled_two, inverse_two = normalize(
        hidden + branch_ffn, gain_two32, shift_two.astype(f32)
    )
    layer_out = normed_out.astype(bf16)
    square_sums = lax.psum(
        (jnp.sum(residual * residual), jnp.sum(stream_one * stream_one)), ("dp", "ctx")
    )
    entries = row_count * model_width * lax.axis_size("dp") * lax.axis_size("ctx")
    rms_values = jnp.sqrt(jnp.stack(square_sums) / entries)
    upstream = cotangent.astype(f32)
    dsum_two, gain_two_grad, shift_two_grad = normalize_back(
        upstream, scaled_two, inverse_two, gain_two32
    )
    ffn_grad = dsum_two.astype(bf16)
    b2_grad = jnp.sum(ffn_grad, axis=0, dtype=f32)
    w2_grad = jnp.einsum("tf,td->fd", act_low, ffn_grad, preferred_element_type=f32)
    act_grad = jnp.einsum("td,fd->tf", ffn_grad, w2_full, preferred_element_type=f32)
    pre_grad = gelu_pull(act_grad)[0].astype(bf16)
    b1_grad = jnp.sum(pre_grad, axis=0, dtype=f32)
    w1_grad = jnp.einsum("td,tf->df", hidden_low, pre_grad, preferred_element_type=f32)
    hidden_grad = dsum_two + jnp.einsum("tf,df->td", pre_grad, w1_full, preferred_element_type=f32)
    dsum_one, gain_one_grad, shift_one_grad = normalize_back(
        hidden_grad, scaled_one, inverse_one, gain_one32
    )
    attn_grad = dsum_one.astype(bf16)
    bo_grad = jnp.sum(attn_grad, axis=0, dtype=f32)
    wo_grad = jnp.einsum("te,td->ed", mixed_low, attn_grad, preferred_element_type=f32)
    mixed_grad = split_heads(
        jnp.einsum("td,ed->te", attn_grad, wo_full, preferred_element_type=f32)
    )
    grad_heads = (mixed_grad / totals_rows[:, :, None]).astype(bf16)
    delta_rows = jnp.sum(mixed_grad * mixed_heads, axis=-1) / totals_rows
    delta_heads = jnp.transpose(delta_rows)
    grad_rows = grad_heads.reshape(row_count, model_width)
    portion = (
        lax.all_gather(key_rows, "ctx", axis=0, tiled=True),
        lax.all_gather(value_rows, "ctx", axis=0, tiled=True),
    )
    key_heads = split_heads(portion[0])
    value_heads = split_heads(portion[1])
    scores = jnp.einsum("qhd,khd->hqk", query_heads, key_heads, preferred_element_type=f32) * 0.125
    weights = jnp.exp(scores)
    across = jnp.einsum("qhd,khd->hqk", grad_heads, value_heads, preferred_element_type=f32)
    slopes = (weights * (across - delta_heads[:, :, None])).astype(bf16)
    part_grad = jnp.einsum("hqk,khd->qhd", slopes, key_heads, preferred_element_type=f32)
    query_acc = part_grad.reshape(row_count, model_width)
    delta_all = lax.all_gather(delta_rows, "ctx", axis=0, tiled=True)
    portion = (
        lax.all_gather(query_rows, "ctx", axis=0, tiled=True),
        lax.all_gather(grad_rows, "ctx", axis=0, tiled=True),
    )
    query_part = split_heads(portion[0])
    grad_part = split_heads(portion[1])
    scores = jnp.einsum("qhd,khd->hqk", query_part, key_local, preferred_element_type=f32) * 0.125
    weights = jnp.exp(scores)
    value_part = jnp.einsum(
        "hqk,qhd->khd", weights.astype(bf16), grad_part, preferred_element_type=f32
    )
    across = jnp.einsum("qhd,khd->hqk", grad_part, value_local, preferred_element_type=f32)
    slopes = (weights * (across - jnp.transpose(delta_all)[:, :, None])).astype(bf16)
    key_part = jnp.einsum("hqk,qhd->khd", slopes, query_part, preferred_element_type=f32)
    key_acc = key_part.reshape(row_count, model_width)
    value_acc = value_part.reshape(row_count, model_width)
    query_grad = (0.125 * query_acc).astype(bf16)
    key_grad = (0.125 * key_acc).astype(bf16)
    value_grad = value_acc.astype(bf16)
    wq_grad = jnp.einsum("td,te->de", tokens, query_grad, preferred_element_type=f32)
    wk_grad = jnp.einsum("td,te->de", tokens, key_grad, preferred_element_type=f32)
    wv_grad = jnp.einsum("td,te->de", tokens, value_grad, preferred_element_type=f32)
    bq_grad = jnp.sum(query_grad, axis=0, dtype=f32)
    bv_grad = jnp.sum(value_grad, axis=0, dtype=f32)
    input_grad = (
        dsum_one
        + jnp.einsum("te,de->td", query_grad, wq_full, preferred_element_type=f32)
        + jnp.einsum("te,de->td", key_grad, wk_full, preferred_element_type=f32)
        + jnp.einsum("te,de->td", value_grad, wv_full, preferred_element_type=f32)
    )
    attn_owned = (
        lax.psum_scatter(wq_grad, ("dp", "ctx"), scatter_dimension=0, tiled=True),
        lax.psum_scatter(wk_grad, ("dp", "ctx"), scatter_dimension=0, tiled=True),
        lax.psum_scatter(wv_grad, ("dp", "ctx"), scatter_dimension=0, tiled=True),
        lax.psum_scatter(wo_grad, ("dp", "ctx"), scatter_dimension=0, tiled=True),
        lax.psum_scatter(bq_grad, ("dp", "ctx"), scatter_dimension=0, tiled=True),
        lax.psum_scatter(bv_grad, ("dp", "ctx"), scatter_dimension=0, tiled=True),
        lax.psum_scatter(bo_grad, ("dp", "ctx"), scatter_dimension=0, tiled=True),
        lax.psum_scatter(gain_one_grad, ("dp", "ctx"), scatter_dimension=0, tiled=True),
        lax.psum_scatter(shift_one_grad, ("dp", "ctx"), scatter_dimension=0, tiled=True),
    )
    ffn_owned = (
        lax.psum_scatter(w1_grad, ("dp", "ctx"), scatter_dimension=0, tiled=True),
        lax.psum_scatter(b1_grad, ("dp", "ctx"), scatter_dimension=0, tiled=True),
        lax.psum_scatter(w2_grad, ("dp", "ctx"), scatter_dimension=0, tiled=True),
        lax.psum_scatter(b2_grad, ("dp", "ctx"), scatter_dimension=0, tiled=True),
        lax.psum_scatter(gain_two_grad, ("dp", "ctx"), scatter_dimension=0, tiled=True),
        lax.psum_scatter(shift_two_grad, ("dp", "ctx"), scatter_dimension=0, tiled=True),
    )
    return (
        layer_out,
        input_grad,
        attn_owned[0],
        attn_owned[1],
        attn_owned[2],
        attn_owned[3],
        attn_owned[4],
        attn_owned[5],
        attn_owned[6],
        attn_owned[7],
        attn_owned[8],
        ffn_owned[0],
        ffn_owned[1],
        ffn_owned[2],
        ffn_owned[3],
        ffn_owned[4],
        ffn_owned[5],
        rms_values,
    )


def solution(mesh):
    rows, flat = P(("dp", "ctx"), None), P(("dp", "ctx"))
    in_specs = (rows,) * 5 + (flat,) * 5 + (rows, flat, rows) + (flat,) * 3 + (rows,)
    out_specs = (rows,) * 6 + (flat,) * 5 + (rows, flat, rows) + (flat,) * 3 + (P(),)
    body = fused if (mesh.shape["dp"], mesh.shape["ctx"]) == (4, 8) else general
    return jax.shard_map(body, mesh=mesh, in_specs=in_specs, out_specs=out_specs, check_vma=False)
```
